256 devices in a mesh: chain: 8 (over x, core), sector: 32 (over z, y).
Axes of the slice: x: 4, y: 4, z: 8, core: 2. Of those that a mesh axis runs over, the one named last changes fastest.
Arguments:
- wavefunction: float32 [8, 128, 24, 384], P('chain', 'sector')
- transfer: float32 [8, 128, 576], P('chain', 'sector')
- left_env: bfloat16 [8, 256, 13, 576], P('chain', 'sector')
- right_env: bfloat16 [8, 256, 13, 576], P('chain', 'sector')
- pair_ops: bfloat16 [8, 13, 256], P('chain')
- env_slot: int32 [8, 128], P('chain'), may hold values from 0 to 255, as said below
- kept_ranks: int32 [8, 128], P('chain', 'sector'), may hold values from 6 to 24
Outputs:
- new_state: float32 [8, 128, 24, 384], P('chain', 'sector')
- energy: float32 [8], P('chain')
The draws below stay inside these ranges and needn't reach their ends.
Inputs may be any that keep to these rules, and one draw needn't show every extreme that they name: `env_slot`: within a segment the values are distinct; slot g lies at sector index floor(g / 8). The 4 sectors i * 4 to (i + 1) * 4 - 1 have their slots at 4 different indices; in every segment some index holds the slots of 8 sectors.
All inputs are finite; a program needn't handle non-finite values.
Results may differ from the reference program's by a relative error of at most 0.0062.
Values may be sent and summed in bfloat16 or wider, within the bound.
A program may use at most 64 MiB of HBM per device.

```python
import jax
import jax.numpy as jnp
from jax import lax

B = 24
PAIR = 16
W = 13
ITERS = 4
SEGMENTS = 8
SEC_DEV = 4
SECTORS = 128
CAP = 8
SLOTS = 256


def symmetrize(noise, scale):
    return (noise + jnp.swapaxes(noise, -1, -2)) * scale


def first_term_identity(count, order):
    first = (jnp.arange(count, dtype=jnp.int32) == 0).astype(jnp.float32)
    return first[:, None, None] * jnp.eye(order, dtype=jnp.float32)[None]


def draw_wavefunction(key, part):
    key = jax.random.fold_in(key, 11)
    shape = (SEGMENTS, SECTORS, B, PAIR * B)
    sector_ramp = 1.0 + 2.0 * jnp.arange(SECTORS, dtype=jnp.float32) / max(SECTORS - 1, 1)
    values = jax.random.normal(key, shape, jnp.float32)
    return values * sector_ramp[None, :, None, None]


def draw_transfer(key, part):
    key = jax.random.fold_in(key, 12)
    shape = (SEGMENTS, SECTORS, B, B)
    noise = jax.random.normal(key, shape, jnp.float32)
    blocks = jnp.eye(B, dtype=jnp.float32)[None, None] + noise * (0.25 / B ** 0.5)
    return blocks.reshape(SEGMENTS, SECTORS, B * B)


def draw_left_env(key, part):
    key = jax.random.fold_in(key, 13)
    shape = (SEGMENTS, SLOTS, W, B, B)
    noise = jax.random.normal(key, shape, jnp.float32)
    terms = symmetrize(noise, (2.0 * B * W) ** (-0.5)) + first_term_identity(W, B)[None, None]
    return (terms * 0.01).reshape(SEGMENTS, SLOTS, W, B * B).astype(jnp.bfloat16)


def draw_right_env(key, part):
    key = jax.random.fold_in(key, 14)
    shape = (SEGMENTS, SLOTS, W, B, B)
    noise = jax.random.normal(key, shape, jnp.float32)
    terms = symmetrize(noise, (2.0 * B) ** (-0.5)) + first_term_identity(W, B)[None, None]
    return terms.reshape(SEGMENTS, SLOTS, W, B * B).astype(jnp.bfloat16)


def draw_pair_ops(key, part):
    key = jax.random.fold_in(key, 15)
    shape = (SEGMENTS, W, PAIR, PAIR)
    noise = jax.random.normal(key, shape, jnp.float32)
    terms = symmetrize(noise, (2.0 * PAIR) ** (-0.5)) + first_term_identity(W, PAIR)[None]
    return terms.reshape(SEGMENTS, W, PAIR * PAIR).astype(jnp.bfloat16)


def draw_env_slot(key, part):
    key = jax.random.fold_in(key, 17)
    home_count = SECTORS // SEC_DEV

    def per_segment(seg_key):
        sub_keys = jax.random.split(seg_key, 4)
        column = jnp.arange(home_count, dtype=jnp.int32)
        column_load = jnp.where(column < home_count // 4, 2 * SEC_DEV, jnp.where(column < home_count // 2, 0, SEC_DEV)).astype(jnp.int32)
        run_ends = jnp.cumsum(column_load).astype(jnp.int32)
        begins = run_ends - column_load
        owner_of_column = jax.random.permutation(sub_keys[0], home_count).astype(jnp.int32)
        row_of_home = jax.random.permutation(sub_keys[1], home_count).astype(jnp.int32)
        unit_pos = row_of_home[:, None] + home_count * jnp.arange(SEC_DEV, dtype=jnp.int32)[None, :]
        picked = jnp.searchsorted(run_ends, unit_pos, side='right').astype(jnp.int32)
        run_depth = unit_pos - begins[picked]
        slot_orders = jax.vmap(lambda one_key: jax.random.permutation(one_key, CAP))(jax.random.split(sub_keys[2], home_count)).astype(jnp.int32)
        slot_pick = slot_orders[picked, run_depth]
        target = owner_of_column[picked] * CAP + slot_pick
        orders = jax.vmap(lambda one_key: jax.random.permutation(one_key, SEC_DEV))(jax.random.split(sub_keys[3], home_count)).astype(jnp.int32)
        sector_index = jnp.arange(home_count, dtype=jnp.int32)[:, None] * SEC_DEV + orders
        return jnp.zeros((SECTORS,), jnp.int32).at[sector_index.reshape(-1)].set(target.reshape(-1).astype(jnp.int32))
    seg_keys = jax.vmap(lambda number: jax.random.fold_in(key, number))(jnp.arange(SEGMENTS))
    return jax.vmap(per_segment)(seg_keys)


def touch_ends(drawn, stream_key, low, top_value):
    index_at = [jax.random.randint(jax.random.fold_in(stream_key, axis), (), 0, length) for axis, length in enumerate(drawn.shape)]
    longest = drawn.shape.index(max(drawn.shape))
    beside = index_at[:longest] + [(index_at[longest] + 1) % drawn.shape[longest]] + index_at[longest + 1:]
    return drawn.at[tuple(index_at)].set(low).at[tuple(beside)].set(top_value)


def setup_inputs(seed: int = 0) -> dict:
    splits = jax.random.split(jax.random.key(seed), 8)
    wavefunction = draw_wavefunction(jax.random.fold_in(splits[7], 71), 0)
    transfer = draw_transfer(jax.random.fold_in(splits[7], 71), 0)
    left_env = draw_left_env(jax.random.fold_in(splits[7], 71), 0)
    right_env = draw_right_env(jax.random.fold_in(splits[7], 71), 0)
    pair_ops = draw_pair_ops(jax.random.fold_in(splits[7], 71), 0)
    env_slot = draw_env_slot(jax.random.fold_in(splits[7], 71), 0)
    kept_ranks = touch_ends(jax.random.randint(splits[6], (SEGMENTS, SECTORS), B // 4, B + 1), jax.random.fold_in(splits[6], 1), B // 4, B).astype(jnp.int32)
    return dict(wavefunction=wavefunction, transfer=transfer, left_env=left_env, right_env=right_env, pair_ops=pair_ops, env_slot=env_slot, kept_ranks=kept_ranks)


exact_mode = lax.Precision.HIGHEST

def hamiltonian_block(state_block, left_terms, right_terms, pair_terms):
    state_grid = state_block.reshape(B, PAIR, B).astype(jnp.float32)
    pair_mats = pair_terms.reshape(W, PAIR, PAIR).astype(jnp.float32)
    mixed_pair = jnp.einsum('lpr,wqp->wlqr', state_grid, pair_mats).astype(jnp.bfloat16)
    right_mats = right_terms.reshape(W, B, B).astype(jnp.float32)
    moved_right = jnp.einsum('wlqr,wsr->wlqs', mixed_pair.astype(jnp.float32), right_mats).astype(jnp.bfloat16)
    left_cat = jnp.transpose(left_terms.reshape(W, B, B), (1, 0, 2)).reshape(B, W * B)
    return jnp.dot(left_cat, moved_right.reshape(W * B, PAIR * B), preferred_element_type=jnp.float32)

def lowest_pair(diagonal, offdiag):
    padded = jnp.concatenate([jnp.zeros((1,), jnp.float32), jnp.abs(offdiag), jnp.zeros((1,), jnp.float32)])
    bounds = diagonal - padded[:-1] - padded[1:]
    initial = jnp.min(bounds) - 1.0
    dimension = diagonal.shape[0]

    def newton(unused_index, estimate):
        value_prev = jnp.ones((), jnp.float32)
        value_now = diagonal[0] - estimate
        slope_prev = jnp.zeros((), jnp.float32)
        slope_now = -jnp.ones((), jnp.float32)
        for position in range(1, dimension):
            shifted = diagonal[position] - estimate
            weight = offdiag[position - 1] * offdiag[position - 1]
            value_next = shifted * value_now - weight * value_prev
            slope_next = shifted * slope_now - value_now - weight * slope_prev
            value_prev, value_now = (value_now, value_next)
            slope_prev, slope_now = (slope_now, slope_next)
        return estimate - value_now / slope_now
    energy = lax.fori_loop(0, 40, newton, initial)
    coefficients = [jnp.ones((), jnp.float32), (energy - diagonal[0]) / offdiag[0]]
    for position in range(1, dimension - 1):
        following = ((energy - diagonal[position]) * coefficients[position] - offdiag[position - 1] * coefficients[position - 1]) / offdiag[position]
        coefficients.append(following)
    stacked = jnp.stack(coefficients)
    return (energy, stacked / jnp.sqrt(jnp.sum(stacked * stacked)))

def one_segment(packed):
    initial, prefix, left_all, right_all, pair_terms, slot_row, rank_row = packed
    left_terms = left_all[slot_row]
    right_terms = right_all[slot_row]
    apply_all = jax.vmap(hamiltonian_block, in_axes=(0, 0, 0, None))

    def image_of(vector):
        turned = jnp.einsum('klm,klx->kmx', prefix, vector, precision=exact_mode).astype(jnp.bfloat16)
        inner_terms = apply_all(turned, left_terms, right_terms, pair_terms)
        return jnp.einsum('klm,kmx->klx', prefix, inner_terms, precision=exact_mode)
    current = initial / jnp.sqrt(jnp.sum(initial * initial))
    previous = jnp.zeros_like(current)
    coupling = jnp.zeros((), jnp.float32)
    basis = []
    diagonal = []
    offdiag = []
    for section in range(ITERS):
        basis.append(current)
        result = image_of(current)
        correlation = jnp.sum(current * result)
        diagonal.append(correlation)
        if section + 1 < ITERS:
            result = result - correlation * current - coupling * previous
            coupling = jnp.sqrt(jnp.sum(result * result))
            offdiag.append(coupling)
            previous = current
            current = result / coupling
    energy, coefficients = lowest_pair(jnp.stack(diagonal), jnp.stack(offdiag))
    combined = basis[0] * coefficients[0]
    for section in range(1, ITERS):
        combined = combined + coefficients[section] * basis[section]
    right_index = jnp.arange(PAIR * B, dtype=jnp.int32) % B
    truncated = jnp.where(right_index[None, None, :] < rank_row[:, None, None], combined, 0.0)
    entries = float(SECTORS * B * PAIR * B)
    new_state = truncated * jnp.sqrt(entries / jnp.sum(truncated * truncated))
    return (new_state, energy)

def reference(wavefunction, transfer, left_env, right_env, pair_ops, env_slot, kept_ranks):
    steps_all = transfer.reshape(SEGMENTS, SECTORS, B, B)
    identity_blocks = jnp.broadcast_to(jnp.eye(B, dtype=jnp.float32), (SECTORS, B, B))

    def advance(carried, step_block):
        return (jnp.einsum('kij,kjl->kil', step_block, carried, precision=exact_mode), carried)
    unused_last, prefixes = lax.scan(advance, identity_blocks, steps_all)
    new_state, energy = lax.map(one_segment, (wavefunction, prefixes, left_env, right_env, pair_ops, env_slot, kept_ranks))
    return (new_state, energy)
```

```python
import functools
import jax, jax.numpy as jnp
from jax import lax
from jax.experimental import pallas as pl
from jax.sharding import PartitionSpec as P
from jax.experimental.pallas import tpu as pltpu
F=jnp.float32; H=jnp.bfloat16
NT=4; NB=24; NP=16; NW=13

def split(x):
    h=x.astype(H)
    return h,(x-h.astype(F)).astype(H)

def grab(ref_cols, off, t, lane):
    c0,o=off//128,off%128
    sh=(32*t-o)%128
    a=ref_cols(c0)
    a=pltpu.roll(a,sh,1) if sh else a
    if o+24>128:
        b=ref_cols(c0+1)
        b=pltpu.roll(b,sh,1) if sh else b
        a=jnp.where(lane<32*t+128-o,a,b)
    return jnp.where((lane>=32*t)&(lane<32*t+24),a,0.0)

def full(x):
    return jnp.sum(jnp.sum(x,axis=0,keepdims=True),axis=1,keepdims=True)

def k2(chain_ref,kept_ref,trans_ref,env_ref,x_ref,b_ref,v_ref,st_ref,
       tpad,tbd,ebd,b2,c2,mixed,moved,acat):
    me=chain_ref[0]
    lane=lax.broadcasted_iota(jnp.int32,(1,128),1)
    row128=lax.broadcasted_iota(jnp.int32,(128,128),0)
    col128=lax.broadcasted_iota(jnp.int32,(128,128),1)
    tbd[...]=jnp.zeros_like(tbd)
    for t in range(NT):
        tpad[:,:576]=trans_ref[:,t,:]
        for i in range(NB):
            tbd[pl.ds(32*t+i,8,stride=128),:]=grab(lambda c:tpad[:,c*128:(c+1)*128],24*i,t,lane)
    eye=(row128==col128).astype(F)
    T=[jnp.where(me>c,tbd[c*128:(c+1)*128,:],eye) for c in range(7)]
    mm=lambda a,b: jnp.dot(a,b,precision=lax.Precision.HIGHEST,preferred_element_type=F)
    pre=mm(mm(T[6],mm(T[5],T[4])),mm(mm(T[3],T[2]),mm(T[1],T[0])))
    PT=pre.T
    ph,plo=split(PT)
    bf=b_ref[...].astype(F)
    for q in range(NP):
        off=16*q
        a=bf[:,(off//128)*128:(off//128)*128+128]
        sh=(-(off%128))%128
        a=pltpu.roll(a,sh,1) if sh else a
        tpadb=jnp.where(lane<16,a,0.0)
        tbd[pl.ds(q,13,stride=16),:]=tpadb
    bb=tbd[0:208,:]
    bb=jnp.where(lane<16,bb,0.0)+pltpu.roll(bb,16,1)
    b2[...]=bb[:,:32].astype(H)
    for side in (1,0):
        ebd[...]=jnp.zeros_like(ebd)
        for t in range(NT):
            ev=env_ref[t].astype(F)
            for i in range(NB):
                ebd[pl.ds(32*t+i,13,stride=128),:]=grab(lambda c:ev[:,c*128:(c+1)*128],576*side+24*i,t,lane)
        if side==1:
            for w in range(NW):
                ct=ebd[w*128:(w+1)*128,:].T.astype(H)
                c2[w,0:128,:]=ct
                c2[w,128:256,:]=ct
        else:
            pp=jnp.concatenate([ph,plo],0)
            pq=jnp.concatenate([ph,plo,ph],0)
            for w in range(NW):
                e=ebd[w*128:(w+1)*128,:].astype(H)
                s=jnp.dot(jnp.concatenate([e,e],1),pp,preferred_element_type=F)
                sh,sl=split(s.T)
                at=jnp.dot(jnp.concatenate([sh,sh,sl],1),pq,preferred_element_type=F)
                acat[24*w:24*w+24,:]=at[0:24]+at[32:56]+at[64:88]+at[96:120]
    acat[312:384,:]=jnp.zeros((72,128),F)
    al=acat[...].T
    al=jnp.concatenate([al[32*t:32*t+24] for t in range(NT)],0)[:,:312].astype(H)
    a2=jnp.concatenate([al.astype(F),al.astype(F)],1).astype(H)
    for p in range(NP):
        acc=jnp.zeros((24,128),F)
        for t in range(NT):
            acc=acc+grab(lambda c:x_ref[t,:,c*128:(c+1)*128],24*p,t,lane)
        v_ref[0,pl.ds(p,24,stride=16),:]=acc
    x=v_ref[0]
    n0=jnp.sqrt(full(x*x))
    inv=lambda n: jnp.where(n>0,1.0/n,0.0)
    v_ref[0]=x*inv(n0)
    bm=b2[...]
    tl=lane//32
    alphas=[];betas=[]
    for k in range(4):
        for l in range(0,NB,2):
            xx=jnp.concatenate([v_ref[k,16*l:16*l+16,:],v_ref[k,16*l+16:16*l+32,:]],1)
            h,lo=split(xx)
            o=jnp.dot(bm,jnp.concatenate([h,lo],0),preferred_element_type=F)
            h,lo=split(o)
            mixed[0,l]=h[:,:128]; mixed[0,l+1]=h[:,128:]
            mixed[1,l]=lo[:,:128]; mixed[1,l+1]=lo[:,128:]
        for w in range(NW):
            h=mixed[0,:,16*w:16*w+16,:].reshape(384,128)
            lo=mixed[1,:,16*w:16*w+16,:].reshape(384,128)
            moved[w]=jnp.dot(jnp.concatenate([h,lo],1),c2[w],preferred_element_type=F)
        for q in range(0,NP,2):
            r=jnp.concatenate([jnp.concatenate([moved[w,pl.ds(q+j,24,stride=16),:] for w in range(NW)],0) for j in range(2)],1)
            h=r.astype(H).astype(F)
            o=jnp.dot(a2,jnp.concatenate([h,r-h],0).astype(H),preferred_element_type=F)
            for j in range(2):
                oj=o[:,128*j:128*j+128]
                y=jnp.where(tl==0,oj[0:24],jnp.where(tl==1,oj[24:48],jnp.where(tl==2,oj[48:72],oj[72:96])))
                v_ref[k+1,pl.ds(q+j,24,stride=16),:]=y
        w_=v_ref[k+1]
        if k<3:
            a=full(v_ref[k]*w_)
            r=w_-a*v_ref[k]
            if k>0: r=r-betas[-1]*v_ref[k-1]
            b=jnp.sqrt(full(r*r))
            alphas.append(a); betas.append(b)
            v_ref[k+1]=r*inv(b)
    rows=[]
    for i in range(4):
        for j in range(i,5):
            rows.append(jnp.sum(v_ref[i]*v_ref[j],axis=0,keepdims=True))
    rows+= [jnp.zeros((1,128),F)]*2
    g=jnp.concatenate(rows,0)
    kp=jnp.where(tl==0,kept_ref[0,0],jnp.where(tl==1,kept_ref[0,1],jnp.where(tl==2,kept_ref[0,2],kept_ref[0,3])))
    msk=((lane%32)<kp).astype(F)
    r8=lax.broadcasted_iota(jnp.int32,(8,128),0)
    lhs=jnp.where(r8==0,1.0,jnp.where(r8==1,jnp.broadcast_to(msk,(8,128)),0.0))
    g=jnp.concatenate([g,jnp.zeros((112,128),F)],0)
    s=lax.dot_general(lhs,g,(((1,),(1,)),((),())),precision=lax.Precision.HIGHEST,preferred_element_type=F)
    for i,val in enumerate([n0]+alphas+betas):
        s=s+jnp.where((lane==16+i)&(r8==0),val,0.0)
    st_ref[...]=s

def call_k2(chain,kept,trans,env,x,b):
    return pl.pallas_call(k2,
      out_shape=(jax.ShapeDtypeStruct((5,384,128),F),jax.ShapeDtypeStruct((8,128),F)),
      in_specs=[pl.BlockSpec(memory_space=pltpu.SMEM)]*2+[pl.BlockSpec(memory_space=pltpu.VMEM)]*4,
      out_specs=(pl.BlockSpec(memory_space=pltpu.VMEM),)*2,
      scratch_shapes=[pltpu.VMEM((8,640),F),pltpu.VMEM((1024,128),F),pltpu.VMEM((1664,128),F),
        pltpu.VMEM((208,32),H),pltpu.VMEM((13,256,128),H),pltpu.VMEM((2,24,208,128),H),
        pltpu.VMEM((13,384,128),F),pltpu.VMEM((384,128),F)],
      compiler_params=pltpu.CompilerParams(vmem_limit_bytes=48*2**20),
      name="lanczos_local")(chain,kept,trans,env,x,b)

def global_solve(q0,q1,entries):
    tot=lambda x: jnp.sum(x,axis=1,keepdims=True)
    pos={}
    n=0
    for i in range(4):
        for j in range(i,5):
            pos[i,j]=n; n+=1
    M=[[q0(pos[min(i,j),max(i,j)]) for j in range(4)] for i in range(4)]
    Mk=[[q1(pos[min(i,j),max(i,j)]) for j in range(4)] for i in range(4)]
    Wv=[q0(pos[i,4]) for i in range(4)]
    n0=q0(16); al=[q0(17+i) for i in range(3)]; be=[q0(20+i) for i in range(3)]
    def tmul(c):
        k=len(c)-1
        y=[None]*min(k+2,4)
        def add(i,z):
            y[i]=z if y[i] is None else y[i]+z
        for j in range(min(k+1,3)):
            add(j,al[j]*c[j]); add(j+1,be[j]*c[j])
            if j>0: add(j-1,be[j-1]*c[j])
        return y
    def dot(Mx,a,b):
        acc=None
        for i in range(len(a)):
            s=None
            for j in range(len(b)):
                z=Mx[i][j]*b[j]; s=z if s is None else s+z
            s=s*a[i]; acc=s if acc is None else acc+s
        return acc
    c=[n0/jnp.sqrt(tot(n0*n0))]
    cp=[]; b=None
    cs=[]; A=[]; Bt=[]
    for k in range(4):
        cs.append(c)
        y=tmul(c)
        g=dot(M,c,y)
        if k==3:
            s=None
            for i in range(4):
                z=c[i]*Wv[i]; s=z if s is None else s+z
            g=g+s*c[3]
        a=tot(g); A.append(a)
        if k<3:
            r=[]
            for i in range(len(y)):
                z=y[i]
                if i<len(c): z=z-a*c[i]
                if i<len(cp): z=z-b*cp[i]
                r.append(z)
            b=jnp.sqrt(tot(dot(M,r,r))); Bt.append(b)
            cp=c; c=[z/b for z in r]
    ab=[jnp.abs(z) for z in Bt]
    bounds=[A[0]-ab[0],A[1]-ab[0]-ab[1],A[2]-ab[1]-ab[2],A[3]-ab[2]]
    init=jnp.minimum(jnp.minimum(bounds[0],bounds[1]),jnp.minimum(bounds[2],bounds[3]))-1.0
    B2=[z*z for z in Bt]
    def newton(_,e):
        vp=jnp.ones_like(e); vn=A[0]-e; sp=jnp.zeros_like(e); sn=-jnp.ones_like(e)
        for p in range(1,4):
            sh=A[p]-e; w=B2[p-1]
            v2=sh*vn-w*vp; s2=sh*sn-vn-w*sp
            vp,vn=vn,v2; sp,sn=sn,s2
        return e-vn/sn
    e=lax.fori_loop(0,40,newton,init)
    co=[jnp.ones_like(e),(e-A[0])/Bt[0]]
    for p in range(1,3):
        co.append(((e-A[p])*co[p]-Bt[p-1]*co[p-1])/Bt[p])
    nrm=jnp.sqrt(co[0]*co[0]+co[1]*co[1]+co[2]*co[2]+co[3]*co[3])
    f=[None]*4
    for k in range(4):
        for i in range(len(cs[k])):
            z=(co[k]/nrm)*cs[k][i]; f[i]=z if f[i] is None else f[i]+z
    scale=jnp.sqrt(entries/tot(dot(Mk,f,f)))
    return e,[z*scale for z in f]

def k4(entries,me_ref,kept_ref,st_ref,v_ref,out_ref,en_ref,ybuf):
    me=me_ref[0]
    lane=lax.broadcasted_iota(jnp.int32,(1,128),1)
    z=jnp.zeros((96,128),F)
    Q0=jnp.concatenate([st_ref[:,0,:],z],0).T
    Q1=jnp.concatenate([st_ref[:,1,:],z],0).T
    e,f=global_solve(lambda i:Q0[i:i+1,:],lambda i:Q1[i:i+1,:],entries)
    en_ref[...]=jnp.broadcast_to(e,(8,128))
    tl=lane//32
    kp=jnp.where(tl==0,kept_ref[0,0],jnp.where(tl==1,kept_ref[0,1],jnp.where(tl==2,kept_ref[0,2],kept_ref[0,3])))
    keep=(lane%32)<kp
    mine=[jnp.sum(jnp.where(lane==me,z,0.0),axis=1,keepdims=True) for z in f]
    y=mine[0]*v_ref[0]
    for i in range(1,4): y=y+mine[i]*v_ref[i]
    ybuf[...]=jnp.where(keep,y,0.0)
    for p in range(NP):
        a=ybuf[pl.ds(p,24,stride=16),:]
        for t in range(NT):
            out_ref[t,:,24*p:24*p+24]=a[:,32*t:32*t+24]

def call_k4(entries,me,kept,st,v):
    return pl.pallas_call(functools.partial(k4,entries),
      out_shape=(jax.ShapeDtypeStruct((4,24,384),F),jax.ShapeDtypeStruct((8,128),F)),
      in_specs=[pl.BlockSpec(memory_space=pltpu.SMEM)]*2+[pl.BlockSpec(memory_space=pltpu.VMEM)]*2,
      out_specs=(pl.BlockSpec(memory_space=pltpu.VMEM),)*2,
      scratch_shapes=[pltpu.VMEM((384,128),F)],
      compiler_params=pltpu.CompilerParams(vmem_limit_bytes=16*2**20),
      name="global_solve")(me,kept,st,v)

def body(wavefunction, transfer, left_env, right_env, pair_ops, env_slot, kept_ranks):
    sector_count = lax.axis_size("sector")
    me = lax.axis_index("sector")
    chain = lax.axis_index("chain")
    slots = left_env.shape[1]
    trans = lax.all_gather(transfer[0], "chain")
    slot_all = env_slot[0]
    owner = slot_all // slots
    within = slot_all - owner * slots
    match = owner.reshape(sector_count, NT) == me
    slot_of_home = jnp.sum(jnp.where(match, within.reshape(sector_count, NT), 0), axis=1)
    env = jnp.concatenate([left_env[0], right_env[0]], axis=-1)
    arrived = lax.all_to_all(env[slot_of_home], "sector", split_axis=0, concat_axis=0, tiled=True)
    owner_mine = lax.dynamic_slice_in_dim(owner, me * NT, NT)
    mine = arrived[owner_mine]
    v, st = call_k2(chain.reshape(1), kept_ranks, trans, mine, wavefunction[0], pair_ops[0])
    stats = lax.all_gather(st, "sector")
    entries = float(sector_count * NT * NB * NP * NB)
    out, en = call_k4(entries, me.reshape(1), kept_ranks, stats, v)
    return out[None], en[0, :1]


def solution(mesh):
    return jax.shard_map(
        body,
        mesh=mesh,
        in_specs=(
            P("chain", "sector", None, None),
            P("chain", "sector", None),
            P("chain", "sector", None, None),
            P("chain", "sector", None, None),
            P("chain", None, None),
            P("chain", None),
            P("chain", "sector"),
        ),
        out_specs=(P("chain", "sector", None, None), P("chain")),
        check_vma=False,
    )
```

```python
import functools
import jax, jax.numpy as jnp
from jax import lax
from jax.experimental import pallas as pl
from jax.sharding import PartitionSpec as P
from jax.experimental.pallas import tpu as pltpu
F=jnp.float32; H=jnp.bfloat16
NT=4; NB=24; NP=16; NW=13

def split(x):
    h=x.astype(H)
    return h,(x-h.astype(F)).astype(H)

def grab(ref_cols, off, t, lane):
    c0,o=off//128,off%128
    sh=(32*t-o)%128
    a=ref_cols(c0)
    a=pltpu.roll(a,sh,1) if sh else a
    if o+24>128:
        b=ref_cols(c0+1)
        b=pltpu.roll(b,sh,1) if sh else b
        a=jnp.where(lane<32*t+128-o,a,b)
    return jnp.where((lane>=32*t)&(lane<32*t+24),a,0.0)

def full(x):
    return jnp.sum(jnp.sum(x,axis=0,keepdims=True),axis=1,keepdims=True)

def k2(chain_ref,kept_ref,trans_ref,env_ref,x_ref,b_ref,v_ref,st_ref,
       tpad,tbd,ebd,b2,c2,mixed,moved,acat):
    me=chain_ref[0]
    lane=lax.broadcasted_iota(jnp.int32,(1,128),1)
    row128=lax.broadcasted_iota(jnp.int32,(128,128),0)
    col128=lax.broadcasted_iota(jnp.int32,(128,128),1)
    tbd[...]=jnp.zeros_like(tbd)
    for t in range(NT):
        tpad[:,:576]=trans_ref[:,t,:]
        for i in range(NB):
            tbd[pl.ds(32*t+i,8,stride=128),:]=grab(lambda c:tpad[:,c*128:(c+1)*128],24*i,t,lane)
    eye=(row128==col128).astype(F)
    T=[jnp.where(me>c,tbd[c*128:(c+1)*128,:],eye) for c in range(7)]
    mm=lambda a,b: jnp.dot(a,b,precision=lax.Precision.HIGHEST,preferred_element_type=F)
    pre=mm(mm(T[6],mm(T[5],T[4])),mm(mm(T[3],T[2]),mm(T[1],T[0])))
    PT=pre.T
    ph,plo=split(PT)
    bf=b_ref[...].astype(F)
    for q in range(NP):
        off=16*q
        a=bf[:,(off//128)*128:(off//128)*128+128]
        sh=(-(off%128))%128
        a=pltpu.roll(a,sh,1) if sh else a
        tpadb=jnp.where(lane<16,a,0.0)
        tbd[pl.ds(q,13,stride=16),:]=tpadb
    bb=tbd[0:208,:]
    bb=jnp.where(lane<16,bb,0.0)+pltpu.roll(bb,16,1)
    b2[...]=bb[:,:32].astype(H)
    for side in (1,0):
        ebd[...]=jnp.zeros_like(ebd)
        for t in range(NT):
            ev=env_ref[t].astype(F)
            for i in range(NB):
                ebd[pl.ds(32*t+i,13,stride=128),:]=grab(lambda c:ev[:,c*128:(c+1)*128],576*side+24*i,t,lane)[:13]
        if side==1:
            for w in range(NW):
                ct=ebd[w*128:(w+1)*128,:].T.astype(H)
                c2[w,0:128,:]=ct
                c2[w,128:256,:]=ct
        else:
            pp=jnp.concatenate([ph,plo],0)
            pq=jnp.concatenate([ph,plo,ph],0)
            for w in range(NW):
                e=ebd[w*128:(w+1)*128,:].astype(H)
                s=jnp.dot(jnp.concatenate([e,e],1),pp,preferred_element_type=F)
                sh,sl=split(s.T)
                at=jnp.dot(jnp.concatenate([sh,sh,sl],1),pq,preferred_element_type=F)
                acat[24*w:24*w+24,:]=at[0:24]+at[32:56]+at[64:88]+at[96:120]
    acat[312:384,:]=jnp.zeros((72,128),F)
    al=acat[...].T
    al=jnp.concatenate([al[32*t:32*t+24] for t in range(NT)],0)[:,:312].astype(H)
    a2=jnp.concatenate([al.astype(F),al.astype(F)],1).astype(H)
    for p in range(NP):
        acc=jnp.zeros((24,128),F)
        for t in range(NT):
            acc=acc+grab(lambda c:x_ref[t,:,c*128:(c+1)*128],24*p,t,lane)
        v_ref[0,pl.ds(p,24,stride=16),:]=acc
    x=v_ref[0]
    n0=jnp.sqrt(full(x*x))
    inv=lambda n: jnp.where(n>0,1.0/n,0.0)
    v_ref[0]=x*inv(n0)
    bm=b2[...]
    tl=lane//32
    alphas=[];betas=[]
    for k in range(4):
        for l in range(0,NB,2):
            xx=jnp.concatenate([v_ref[k,16*l:16*l+16,:],v_ref[k,16*l+16:16*l+32,:]],1)
            h,lo=split(xx)
            o=jnp.dot(bm,jnp.concatenate([h,lo],0),preferred_element_type=F)
            h,lo=split(o)
            mixed[0,l]=h[:,:128]; mixed[0,l+1]=h[:,128:]
            mixed[1,l]=lo[:,:128]; mixed[1,l+1]=lo[:,128:]
        for w in range(NW):
            h=mixed[0,:,16*w:16*w+16,:].reshape(384,128)
            lo=mixed[1,:,16*w:16*w+16,:].reshape(384,128)
            moved[w]=jnp.dot(jnp.concatenate([h,lo],1),c2[w],preferred_element_type=F)
        for q in range(0,NP,2):
            r=jnp.concatenate([jnp.concatenate([moved[w,pl.ds(q+j,24,stride=16),:] for w in range(NW)],0) for j in range(2)],1)
            h=r.astype(H).astype(F)
            o=jnp.dot(a2,jnp.concatenate([h,r-h],0).astype(H),preferred_element_type=F)
            for j in range(2):
                oj=o[:,128*j:128*j+128]
                y=jnp.where(tl==0,oj[0:24],jnp.where(tl==1,oj[24:48],jnp.where(tl==2,oj[48:72],oj[72:96])))
                v_ref[k+1,pl.ds(q+j,24,stride=16),:]=y
        w_=v_ref[k+1]
        if k<3:
            a=full(v_ref[k]*w_)
            r=w_-a*v_ref[k]
            if k>0: r=r-betas[-1]*v_ref[k-1]
            b=jnp.sqrt(full(r*r))
            alphas.append(a); betas.append(b)
            v_ref[k+1]=r*inv(b)
    rows=[]
    for i in range(4):
        for j in range(i,5):
            rows.append(jnp.sum(v_ref[i]*v_ref[j],axis=0,keepdims=True))
    rows+= [jnp.zeros((1,128),F)]*2
    g=jnp.concatenate(rows,0)
    kp=jnp.where(tl==0,kept_ref[0,0],jnp.where(tl==1,kept_ref[0,1],jnp.where(tl==2,kept_ref[0,2],kept_ref[0,3])))
    msk=((lane%32)<kp).astype(F)
    r8=lax.broadcasted_iota(jnp.int32,(8,128),0)
    lhs=jnp.where(r8==0,1.0,jnp.where(r8==1,jnp.broadcast_to(msk,(8,128)),0.0))
    g=jnp.concatenate([g,jnp.zeros((112,128),F)],0)
    s=lax.dot_general(lhs,g,(((1,),(1,)),((),())),precision=lax.Precision.HIGHEST,preferred_element_type=F)
    for i,val in enumerate([n0]+alphas+betas):
        s=s+jnp.where((lane==16+i)&(r8==0),val,0.0)
    st_ref[...]=s

def call_k2(chain,kept,trans,env,x,b):
    return pl.pallas_call(k2,
      out_shape=(jax.ShapeDtypeStruct((5,384,128),F),jax.ShapeDtypeStruct((8,128),F)),
      in_specs=[pl.BlockSpec(memory_space=pltpu.SMEM)]*2+[pl.BlockSpec(memory_space=pltpu.VMEM)]*4,
      out_specs=(pl.BlockSpec(memory_space=pltpu.VMEM),)*2,
      scratch_shapes=[pltpu.VMEM((8,640),F),pltpu.VMEM((1024,128),F),pltpu.VMEM((1664,128),F),
        pltpu.VMEM((208,32),H),pltpu.VMEM((13,256,128),H),pltpu.VMEM((2,24,208,128),H),
        pltpu.VMEM((13,384,128),F),pltpu.VMEM((384,128),F)],
      compiler_params=pltpu.CompilerParams(vmem_limit_bytes=48*2**20),
      name="lanczos_local")(chain,kept,trans,env,x,b)

def global_solve(q0,q1,entries):
    tot=lambda x: jnp.sum(x,axis=1,keepdims=True)
    pos={}
    n=0
    for i in range(4):
        for j in range(i,5):
            pos[i,j]=n; n+=1
    M=[[q0(pos[min(i,j),max(i,j)]) for j in range(4)] for i in range(4)]
    Mk=[[q1(pos[min(i,j),max(i,j)]) for j in range(4)] for i in range(4)]
    Wv=[q0(pos[i,4]) for i in range(4)]
    n0=q0(16); al=[q0(17+i) for i in range(3)]; be=[q0(20+i) for i in range(3)]
    def tmul(c):
        k=len(c)-1
        y=[None]*min(k+2,4)
        def add(i,z):
            y[i]=z if y[i] is None else y[i]+z
        for j in range(min(k+1,3)):
            add(j,al[j]*c[j]); add(j+1,be[j]*c[j])
            if j>0: add(j-1,be[j-1]*c[j])
        return y
    def dot(Mx,a,b):
        acc=None
        for i in range(len(a)):
            s=None
            for j in range(len(b)):
                z=Mx[i][j]*b[j]; s=z if s is None else s+z
            s=s*a[i]; acc=s if acc is None else acc+s
        return acc
    c=[n0/jnp.sqrt(tot(n0*n0))]
    cp=[]; b=None
    cs=[]; A=[]; Bt=[]
    for k in range(4):
        cs.append(c)
        y=tmul(c)
        g=dot(M,c,y)
        if k==3:
            s=None
            for i in range(4):
                z=c[i]*Wv[i]; s=z if s is None else s+z
            g=g+s*c[3]
        a=tot(g); A.append(a)
        if k<3:
            r=[]
            for i in range(len(y)):
                z=y[i]
                if i<len(c): z=z-a*c[i]
                if i<len(cp): z=z-b*cp[i]
                r.append(z)
            b=jnp.sqrt(tot(dot(M,r,r))); Bt.append(b)
            cp=c; c=[z/b for z in r]
    ab=[jnp.abs(z) for z in Bt]
    bounds=[A[0]-ab[0],A[1]-ab[0]-ab[1],A[2]-ab[1]-ab[2],A[3]-ab[2]]
    init=jnp.minimum(jnp.minimum(bounds[0],bounds[1]),jnp.minimum(bounds[2],bounds[3]))-1.0
    B2=[z*z for z in Bt]
    def newton(_,e):
        vp=jnp.ones_like(e); vn=A[0]-e; sp=jnp.zeros_like(e); sn=-jnp.ones_like(e)
        for p in range(1,4):
            sh=A[p]-e; w=B2[p-1]
            v2=sh*vn-w*vp; s2=sh*sn-vn-w*sp
            vp,vn=vn,v2; sp,sn=sn,s2
        return e-vn/sn
    e=lax.fori_loop(0,40,newton,init)
    co=[jnp.ones_like(e),(e-A[0])/Bt[0]]
    for p in range(1,3):
        co.append(((e-A[p])*co[p]-Bt[p-1]*co[p-1])/Bt[p])
    nrm=jnp.sqrt(co[0]*co[0]+co[1]*co[1]+co[2]*co[2]+co[3]*co[3])
    f=[None]*4
    for k in range(4):
        for i in range(len(cs[k])):
            z=(co[k]/nrm)*cs[k][i]; f[i]=z if f[i] is None else f[i]+z
    scale=jnp.sqrt(entries/tot(dot(Mk,f,f)))
    return e,[z*scale for z in f]


def device_id(ch, sec):
    return (ch, sec)

def exchange(nsec,nch,left,right,slot_ref,tr,env_out,trans_out,cat,stage,recv,trecv,ssem,rsem,tssem,trsem):
    me=lax.axis_index("sector"); ch=lax.axis_index("chain")
    cap=left.shape[0]
    bar=pltpu.get_barrier_semaphore()
    def sig(j,c):
        pl.semaphore_signal(bar,inc=1,device_id=(ch,lax.rem(me+j,nsec)),device_id_type=pl.DeviceIdType.MESH)
        return c
    lax.fori_loop(1,nsec,sig,0)
    def sigc(j,c):
        pl.semaphore_signal(bar,inc=1,device_id=(lax.rem(ch+j,nch),me),device_id_type=pl.DeviceIdType.MESH)
        return c
    lax.fori_loop(1,nch,sigc,0)
    cat[...]=jnp.zeros_like(cat)
    for s in range(cap):
        cat[s,0:13,:]=jnp.concatenate([left[s].astype(F),right[s].astype(F)],1).astype(H)
    trecv[ch]=tr[...]
    def put(j,c):
        h=lax.rem(me+j,nsec)
        s=jnp.int32(0)
        for k in range(NT):
            g=slot_ref[0,h*NT+k]
            s=s+jnp.where(g//cap==me,lax.rem(g,cap),0)
        stage[j]=cat[s]
        return c
    lax.fori_loop(0,nsec,put,0)
    pl.semaphore_wait(bar,nsec+nch-2)
    def tcopy(j):
        return pltpu.make_async_remote_copy(src_ref=tr,dst_ref=trecv.at[ch],send_sem=tssem.at[j],recv_sem=trsem.at[j],
            device_id=(lax.rem(ch+j,nch),me),device_id_type=pl.DeviceIdType.MESH)
    def ecopy(j):
        return pltpu.make_async_remote_copy(src_ref=stage.at[j],dst_ref=recv.at[j],send_sem=ssem.at[j],recv_sem=rsem.at[j],
            device_id=(ch,lax.rem(me+j,nsec)),device_id_type=pl.DeviceIdType.MESH)
    lax.fori_loop(1,nch,lambda j,c:(tcopy(j).start(),c)[1],0)
    lax.fori_loop(1,nsec,lambda j,c:(ecopy(j).start(),c)[1],0)
    recv[0]=stage[0]
    lax.fori_loop(1,nch,lambda j,c:(tcopy(j).wait(),c)[1],0)
    trans_out[...]=trecv[...]
    lax.fori_loop(1,nsec,lambda j,c:(ecopy(j).wait(),c)[1],0)
    for t in range(NT):
        o=slot_ref[0,me*NT+t]//cap
        env_out[t]=recv[lax.rem(me-o+nsec,nsec)]

def call_exchange(nsec,nch,left,right,slot,tr):
    cap=left.shape[0]
    return pl.pallas_call(functools.partial(exchange,nsec,nch),
      out_shape=(jax.ShapeDtypeStruct((NT,16,1152),H),jax.ShapeDtypeStruct((nch,NT,576),F)),
      in_specs=[pl.BlockSpec(memory_space=pltpu.VMEM)]*2+[pl.BlockSpec(memory_space=pltpu.SMEM),pl.BlockSpec(memory_space=pltpu.VMEM)],
      out_specs=(pl.BlockSpec(memory_space=pltpu.VMEM),)*2,
      scratch_shapes=[pltpu.VMEM((cap,16,1152),H),pltpu.VMEM((nsec,16,1152),H),pltpu.VMEM((nsec,16,1152),H),pltpu.VMEM((nch,NT,576),F),
        pltpu.SemaphoreType.DMA((nsec,)),pltpu.SemaphoreType.DMA((nsec,)),pltpu.SemaphoreType.DMA((nch,)),pltpu.SemaphoreType.DMA((nch,))],
      compiler_params=pltpu.CompilerParams(collective_id=0,has_side_effects=True,vmem_limit_bytes=16*2**20),
      name="exchange")(left,right,slot,tr)

def gather_solve(entries,nsec,kept_ref,st,v_ref,out_ref,en_ref,recv,ybuf,ssem,rsem):
    me=lax.axis_index("sector"); ch=lax.axis_index("chain")
    bar=pltpu.get_barrier_semaphore()
    def sig(j,c):
        pl.semaphore_signal(bar,inc=1,device_id=(ch,lax.rem(me+j,nsec)),device_id_type=pl.DeviceIdType.MESH)
        return c
    lax.fori_loop(1,nsec,sig,0)
    recv[me]=st[...]
    pl.semaphore_wait(bar,nsec-1)
    def cp(j):
        return pltpu.make_async_remote_copy(src_ref=st,dst_ref=recv.at[me],send_sem=ssem.at[j],recv_sem=rsem.at[j],
            device_id=(ch,lax.rem(me+j,nsec)),device_id_type=pl.DeviceIdType.MESH)
    lax.fori_loop(1,nsec,lambda j,c:(cp(j).start(),c)[1],0)
    lax.fori_loop(1,nsec,lambda j,c:(cp(j).wait(),c)[1],0)
    finish(entries,me,kept_ref,recv,v_ref,out_ref,en_ref,ybuf)

def finish(entries,me,kept_ref,st_ref,v_ref,out_ref,en_ref,ybuf):
    lane=lax.broadcasted_iota(jnp.int32,(1,128),1)
    z=jnp.zeros((128-st_ref.shape[0],128),F)
    Q0=jnp.concatenate([st_ref[:,0,:],z],0).T
    Q1=jnp.concatenate([st_ref[:,1,:],z],0).T
    e,f=global_solve(lambda i:Q0[i:i+1,:],lambda i:Q1[i:i+1,:],entries)
    en_ref[...]=jnp.broadcast_to(e,(8,128))
    tl=lane//32
    kp=jnp.where(tl==0,kept_ref[0,0],jnp.where(tl==1,kept_ref[0,1],jnp.where(tl==2,kept_ref[0,2],kept_ref[0,3])))
    keep=(lane%32)<kp
    mine=[jnp.sum(jnp.where(lane==me,z,0.0),axis=1,keepdims=True) for z in f]
    y=mine[0]*v_ref[0]
    for i in range(1,4): y=y+mine[i]*v_ref[i]
    ybuf[...]=jnp.where(keep,y,0.0)
    for p in range(NP):
        a=ybuf[pl.ds(p,24,stride=16),:]
        for t in range(NT):
            out_ref[t,:,24*p:24*p+24]=a[:,32*t:32*t+24]

def call_gather_solve(entries,nsec,kept,st,v):
    return pl.pallas_call(functools.partial(gather_solve,entries,nsec),
      out_shape=(jax.ShapeDtypeStruct((4,24,384),F),jax.ShapeDtypeStruct((8,128),F)),
      in_specs=[pl.BlockSpec(memory_space=pltpu.SMEM)]+[pl.BlockSpec(memory_space=pltpu.VMEM)]*2,
      out_specs=(pl.BlockSpec(memory_space=pltpu.VMEM),)*2,
      scratch_shapes=[pltpu.VMEM((nsec,8,128),F),pltpu.VMEM((384,128),F),pltpu.SemaphoreType.DMA((nsec,)),pltpu.SemaphoreType.DMA((nsec,))],
      compiler_params=pltpu.CompilerParams(collective_id=1,has_side_effects=True,vmem_limit_bytes=16*2**20),
      name="gather_solve")(kept,st,v)

def body(wavefunction, transfer, left_env, right_env, pair_ops, env_slot, kept_ranks):
    nsec = lax.axis_size("sector")
    nch = lax.axis_size("chain")
    chain = lax.axis_index("chain")
    env, trans = call_exchange(nsec, nch, left_env[0], right_env[0], env_slot, transfer[0])
    v, st = call_k2(chain.reshape(1), kept_ranks, trans, env, wavefunction[0], pair_ops[0])
    entries = float(nsec * NT * NB * NP * NB)
    out, en = call_gather_solve(entries, nsec, kept_ranks, st, v)
    return out[None], en[0, :1]


def solution(mesh):
    return jax.shard_map(
        body,
        mesh=mesh,
        in_specs=(
            P("chain", "sector", None, None),
            P("chain", "sector", None),
            P("chain", "sector", None, None),
            P("chain", "sector", None, None),
            P("chain", None, None),
            P("chain", None),
            P("chain", "sector"),
        ),
        out_specs=(P("chain", "sector", None, None), P("chain")),
        check_vma=False,
    )
```

```python
import functools

import jax
import jax.numpy as jnp
from jax import lax
from jax.experimental import pallas as pl
from jax.experimental.pallas import tpu as pltpu
from jax.sharding import PartitionSpec as P

F = jnp.float32
H = jnp.bfloat16
NT = 4
NB = 24
NP = 16
NW = 13
MESH = pl.DeviceIdType.MESH


def split(x):
    h = x.astype(H)
    return h, (x - h.astype(F)).astype(H)


def grab(tile, off, t, lane):
    c0, o = off // 128, off % 128
    sh = (32 * t - o) % 128
    a = tile(c0)
    a = pltpu.roll(a, sh, 1) if sh else a
    if o + NB > 128:
        b = tile(c0 + 1)
        b = pltpu.roll(b, sh, 1) if sh else b
        a = jnp.where(lane < 32 * t + 128 - o, a, b)
    return jnp.where((lane >= 32 * t) & (lane < 32 * t + NB), a, 0.0)


def full(x):
    return jnp.sum(jnp.sum(x, axis=0, keepdims=True), axis=1, keepdims=True)


def inverse(n):
    return jnp.where(n > 0, 1.0 / n, 0.0)


def loop(a, b, f):
    def step(j, c):
        f(j)
        return c

    lax.fori_loop(a, b, step, 0)


def global_solve(q0,q1,entries):
    tot=lambda x: jnp.sum(x,axis=1,keepdims=True)
    pos={}
    n=0
    for i in range(4):
        for j in range(i,5):
            pos[i,j]=n; n+=1
    M=[[q0(pos[min(i,j),max(i,j)]) for j in range(4)] for i in range(4)]
    Mk=[[q1(pos[min(i,j),max(i,j)]) for j in range(4)] for i in range(4)]
    Wv=[q0(pos[i,4]) for i in range(4)]
    n0=q0(16); al=[q0(17+i) for i in range(3)]; be=[q0(20+i) for i in range(3)]
    def tmul(c):
        k=len(c)-1
        y=[None]*min(k+2,4)
        def add(i,z):
            y[i]=z if y[i] is None else y[i]+z
        for j in range(min(k+1,3)):
            add(j,al[j]*c[j]); add(j+1,be[j]*c[j])
            if j>0: add(j-1,be[j-1]*c[j])
        return y
    def dot(Mx,a,b):
        acc=None
        for i in range(len(a)):
            s=None
            for j in range(len(b)):
                z=Mx[i][j]*b[j]; s=z if s is None else s+z
            s=s*a[i]; acc=s if acc is None else acc+s
        return acc
    c=[n0/jnp.sqrt(tot(n0*n0))]
    cp=[]; b=None
    cs=[]; A=[]; Bt=[]
    for k in range(4):
        cs.append(c)
        y=tmul(c)
        g=dot(M,c,y)
        if k==3:
            s=None
            for i in range(4):
                z=c[i]*Wv[i]; s=z if s is None else s+z
            g=g+s*c[3]
        a=tot(g); A.append(a)
        if k<3:
            r=[]
            for i in range(len(y)):
                z=y[i]
                if i<len(c): z=z-a*c[i]
                if i<len(cp): z=z-b*cp[i]
                r.append(z)
            b=jnp.sqrt(tot(dot(M,r,r))); Bt.append(b)
            cp=c; c=[z/b for z in r]
    ab=[jnp.abs(z) for z in Bt]
    bounds=[A[0]-ab[0],A[1]-ab[0]-ab[1],A[2]-ab[1]-ab[2],A[3]-ab[2]]
    init=jnp.minimum(jnp.minimum(bounds[0],bounds[1]),jnp.minimum(bounds[2],bounds[3]))-1.0
    B2=[z*z for z in Bt]
    def newton(_,e):
        vp=jnp.ones_like(e); vn=A[0]-e; sp=jnp.zeros_like(e); sn=-jnp.ones_like(e)
        for p in range(1,4):
            sh=A[p]-e; w=B2[p-1]
            v2=sh*vn-w*vp; s2=sh*sn-vn-w*sp
            vp,vn=vn,v2; sp,sn=sn,s2
        return e-vn/sn
    e=lax.fori_loop(0,40,newton,init)
    co=[jnp.ones_like(e),(e-A[0])/Bt[0]]
    for p in range(1,3):
        co.append(((e-A[p])*co[p]-Bt[p-1]*co[p-1])/Bt[p])
    nrm=jnp.sqrt(co[0]*co[0]+co[1]*co[1]+co[2]*co[2]+co[3]*co[3])
    f=[None]*4
    for k in range(4):
        for i in range(len(cs[k])):
            z=(co[k]/nrm)*cs[k][i]; f[i]=z if f[i] is None else f[i]+z
    scale=jnp.sqrt(entries/tot(dot(Mk,f,f)))
    return e,[z*scale for z in f]


def whole(
    entries, nsec, nch,
    left, right, slot_ref, tr, x_ref, b_ref, kept_ref,
    out_ref, en_ref,
    wide, wire, cat, stage, recv0, recv1, trecv, v_ref, st, strecv,
    tpad, tbd, ebd, b2, c2, mixed, moved, acat, ybuf,
    ssem, rsem, tssem, trsem, qssem, qrsem,
):
    me = lax.axis_index("sector")
    ch = lax.axis_index("chain")
    cap = left.shape[1]
    lane = lax.broadcasted_iota(jnp.int32, (1, 128), 1)
    tl = lane // 32
    bar = pltpu.get_barrier_semaphore()
    loop(1, nsec, lambda j: pl.semaphore_signal(bar, inc=1, device_id=(ch, lax.rem(me + j, nsec)), device_id_type=MESH))
    loop(1, nch, lambda j: pl.semaphore_signal(bar, inc=1, device_id=(lax.rem(ch + j, nch), me), device_id_type=MESH))
    wire[...] = jnp.zeros_like(wire)
    for side, src in ((0, right), (1, left)):
        for w in range(NW):
            row8 = src[w].astype(F)
            for c in range(4):
                wide[c, cap * w:cap * w + cap, :] = row8[:, 128 * c:128 * c + 128]
            wide[4, cap * w:cap * w + cap, 0:64] = row8[:, 512:576]
        for s in range(cap):
            for c in range(4):
                wire[s, 13 * c:13 * c + 13, :] = wide[c, pl.ds(s, 13, stride=cap), :]
            lo = wide[4, pl.ds(s, 7, stride=cap), :]
            hi = pltpu.roll(wide[4, pl.ds(s + 7 * cap, 6, stride=cap), :], 64, 1)
            wire[s, 52:59, :] = jnp.where(lane < 64, lo, 0.0)
            wire[s, 52:58, :] = jnp.where(lane < 64, lo[0:6], hi)
        cat[side] = wire[...].astype(H)
    trecv[ch] = tr[...]

    def put(j):
        h = lax.rem(me + j, nsec)
        s = jnp.int32(0)
        for k in range(NT):
            g = slot_ref[0, h * NT + k]
            s = s + jnp.where(g // cap == me, lax.rem(g, cap), 0)
        stage[0, j] = cat[0, s]
        stage[1, j] = cat[1, s]

    loop(0, nsec, put)
    pl.semaphore_wait(bar, nsec + nch - 2)

    def tcopy(j):
        return pltpu.make_async_remote_copy(
            src_ref=tr, dst_ref=trecv.at[ch], send_sem=tssem.at[j], recv_sem=trsem.at[j],
            device_id=(lax.rem(ch + j, nch), me), device_id_type=MESH)

    def ecopy(side, j):
        return pltpu.make_async_remote_copy(
            src_ref=stage.at[side, j], dst_ref=(recv0, recv1)[side].at[j], send_sem=ssem.at[side, j], recv_sem=rsem.at[side, j],
            device_id=(ch, lax.rem(me + j, nsec)), device_id_type=MESH)

    loop(1, nch, lambda j: tcopy(j).start())
    loop(1, nsec, lambda j: ecopy(0, j).start())
    loop(1, nsec, lambda j: ecopy(1, j).start())
    recv0[0] = stage[0, 0]
    recv1[0] = stage[1, 0]

    bf = b_ref[...].astype(F)
    for q in range(NP):
        off = 16 * q
        a = bf[:, (off // 128) * 128:(off // 128) * 128 + 128]
        sh = (-(off % 128)) % 128
        a = pltpu.roll(a, sh, 1) if sh else a
        tbd[pl.ds(q, NW, stride=NP), :] = jnp.where(lane < 16, a, 0.0)
    bb = tbd[0:208, :]
    b2[...] = (bb + pltpu.roll(bb, 16, 1))[:, :32].astype(H)
    for p in range(NP):
        acc = jnp.zeros((NB, 128), F)
        for t in range(NT):
            acc = acc + grab(lambda c: x_ref[t, :, c * 128:(c + 1) * 128], NB * p, t, lane)
        v_ref[0, pl.ds(p, NB, stride=NP), :] = acc
    x = v_ref[0]
    n0 = jnp.sqrt(full(x * x))
    v_ref[0] = x * inverse(n0)
    loop(1, nch, lambda j: tcopy(j).wait())
    tbd[...] = jnp.zeros_like(tbd)
    for t in range(NT):
        tpad[0:8, 0:576] = trecv[:, t, :]
        for i in range(NB):
            tbd[pl.ds(32 * t + i, 8, stride=128), :] = grab(lambda c: tpad[0:8, c * 128:(c + 1) * 128], NB * i, t, lane)
    row = lax.broadcasted_iota(jnp.int32, (128, 128), 0)
    col = lax.broadcasted_iota(jnp.int32, (128, 128), 1)
    eye = (row == col).astype(F)
    T = [jnp.where(ch > c, tbd[c * 128:(c + 1) * 128, :], eye) for c in range(7)]

    def mm(a, b):
        return jnp.dot(a, b, precision=lax.Precision.HIGHEST, preferred_element_type=F)

    pre = mm(mm(T[6], mm(T[5], T[4])), mm(mm(T[3], T[2]), mm(T[1], T[0])))
    ph, plo = split(pre.T)

    ebd[...] = jnp.zeros_like(ebd)

    def spread(side):
        for t in range(NT):
            o = slot_ref[0, me * NT + t] // cap
            wire[t] = (recv0, recv1)[side][lax.rem(me - o + nsec, nsec)].astype(F)
            tpad[0:7, 0:128] = wire[t, 52:59, :]
            tpad[7:13, 0:128] = pltpu.roll(wire[t, 52:58, :], 64, 1)
            tile = lambda c: wire[t, 13 * c:13 * c + 13, :] if c < 4 else tpad[0:13, 0:128]
            for i in range(NB):
                ebd[pl.ds(32 * t + i, NW, stride=128), :] = grab(tile, NB * i, t, lane)

    def pair_step(k):
        bm = b2[...]
        for l in range(0, NB, 2):
            xx = jnp.concatenate([v_ref[k, 16 * l:16 * l + 16, :], v_ref[k, 16 * l + 16:16 * l + 32, :]], 1)
            h, lo = split(xx)
            o = jnp.dot(bm, jnp.concatenate([h, lo], 0), preferred_element_type=F)
            h, lo = split(o)
            mixed[0, l] = h[:, :128]
            mixed[0, l + 1] = h[:, 128:]
            mixed[1, l] = lo[:, :128]
            mixed[1, l + 1] = lo[:, 128:]

    def right_step():
        for w in range(NW):
            h = mixed[0, :, 16 * w:16 * w + 16, :].reshape(384, 128)
            lo = mixed[1, :, 16 * w:16 * w + 16, :].reshape(384, 128)
            moved[w] = jnp.dot(jnp.concatenate([h, lo], 1), c2[w], preferred_element_type=F)

    def left_step(k, a2):
        for q in range(0, NP, 2):
            r = jnp.concatenate([jnp.concatenate([moved[w, pl.ds(q + j, NB, stride=NP), :] for w in range(NW)], 0) for j in range(2)], 1)
            h = r.astype(H).astype(F)
            o = jnp.dot(a2, jnp.concatenate([h, r - h], 0).astype(H), preferred_element_type=F)
            for j in range(2):
                oj = o[:, 128 * j:128 * j + 128]
                y = jnp.where(tl == 0, oj[0:24], jnp.where(tl == 1, oj[24:48], jnp.where(tl == 2, oj[48:72], oj[72:96])))
                v_ref[k + 1, pl.ds(q + j, NB, stride=NP), :] = y

    pair_step(0)
    loop(1, nsec, lambda j: ecopy(0, j).wait())
    spread(0)
    for w in range(NW):
        ct = ebd[w * 128:(w + 1) * 128, :].T.astype(H)
        c2[w, 0:128, :] = ct
        c2[w, 128:256, :] = ct
    right_step()
    loop(1, nsec, lambda j: ecopy(1, j).wait())
    spread(1)
    pp = jnp.concatenate([ph, plo], 0)
    pq = jnp.concatenate([ph, plo, ph], 0)
    for w in range(NW):
        e = ebd[w * 128:(w + 1) * 128, :].astype(H)
        s = jnp.dot(jnp.concatenate([e, e], 1), pp, preferred_element_type=F)
        sh, sl = split(s.T)
        at = jnp.dot(jnp.concatenate([sh, sh, sl], 1), pq, preferred_element_type=F)
        acat[24 * w:24 * w + 24, :] = at[0:24] + at[32:56] + at[64:88] + at[96:120]
    acat[312:384, :] = jnp.zeros((72, 128), F)
    al = acat[...].T
    al = jnp.concatenate([al[32 * t:32 * t + 24] for t in range(NT)], 0)[:, :312].astype(H).astype(F)
    a2 = jnp.concatenate([al, al], 1).astype(H)

    alphas = []
    betas = []
    for k in range(4):
        if k > 0:
            pair_step(k)
            right_step()
        left_step(k, a2)
        if k < 3:
            y = v_ref[k + 1]
            a = full(v_ref[k] * y)
            r = y - a * v_ref[k]
            if k > 0:
                r = r - betas[-1] * v_ref[k - 1]
            b = jnp.sqrt(full(r * r))
            alphas.append(a)
            betas.append(b)
            v_ref[k + 1] = r * inverse(b)
    rows = []
    for i in range(4):
        for j in range(i, 5):
            rows.append(jnp.sum(v_ref[i] * v_ref[j], axis=0, keepdims=True))
    g = jnp.concatenate(rows + [jnp.zeros((114, 128), F)], 0)
    kp = jnp.where(tl == 0, kept_ref[0, 0], jnp.where(tl == 1, kept_ref[0, 1], jnp.where(tl == 2, kept_ref[0, 2], kept_ref[0, 3])))
    keep = lax.rem(lane, 32) < kp
    r8 = lax.broadcasted_iota(jnp.int32, (8, 128), 0)
    lhs = jnp.where(r8 == 0, 1.0, jnp.where((r8 == 1) & keep, 1.0, 0.0))
    s = lax.dot_general(lhs, g, (((1,), (1,)), ((), ())), precision=lax.Precision.HIGHEST, preferred_element_type=F)
    for i, val in enumerate([n0] + alphas + betas):
        s = s + jnp.where((lane == 16 + i) & (r8 == 0), val, 0.0)
    st[...] = s

    def qcopy(j):
        return pltpu.make_async_remote_copy(
            src_ref=st, dst_ref=strecv.at[me], send_sem=qssem.at[j], recv_sem=qrsem.at[j],
            device_id=(ch, lax.rem(me + j, nsec)), device_id_type=MESH)

    loop(1, nsec, lambda j: qcopy(j).start())
    strecv[me] = s
    loop(1, nsec, lambda j: qcopy(j).wait())
    z = jnp.zeros((128 - nsec, 128), F)
    q0 = jnp.concatenate([strecv[:, 0, :], z], 0).T
    q1 = jnp.concatenate([strecv[:, 1, :], z], 0).T
    e, f = global_solve(lambda i: q0[i:i + 1, :], lambda i: q1[i:i + 1, :], entries)
    en_ref[...] = jnp.broadcast_to(e, (8, 128))
    mine = [jnp.sum(jnp.where(lane == me, c, 0.0), axis=1, keepdims=True) for c in f]
    y = mine[0] * v_ref[0]
    for i in range(1, 4):
        y = y + mine[i] * v_ref[i]
    ybuf[...] = jnp.where(keep, y, 0.0)
    for p in range(NP):
        a = ybuf[pl.ds(p, NB, stride=NP), :]
        for t in range(NT):
            out_ref[t, :, NB * p:NB * p + NB] = a[:, 32 * t:32 * t + NB]


def body(wavefunction, transfer, left_env, right_env, pair_ops, env_slot, kept_ranks):
    nsec = lax.axis_size("sector")
    nch = lax.axis_size("chain")
    cap = left_env.shape[1]
    entries = float(nsec * NT * NB * NP * NB)
    vmem = pl.BlockSpec(memory_space=pltpu.VMEM)
    smem = pl.BlockSpec(memory_space=pltpu.SMEM)
    dma = pltpu.SemaphoreType.DMA
    out, en = pl.pallas_call(
        functools.partial(whole, entries, nsec, nch),
        out_shape=(jax.ShapeDtypeStruct((NT, NB, NP * NB), F), jax.ShapeDtypeStruct((8, 128), F)),
        in_specs=[vmem, vmem, smem, vmem, vmem, vmem, smem],
        out_specs=(vmem, vmem),
        scratch_shapes=[
            pltpu.VMEM((5, cap * NW, 128), F),
            pltpu.VMEM((cap, 64, 128), F),
            pltpu.VMEM((2, cap, 64, 128), H),
            pltpu.VMEM((2, nsec, 64, 128), H),
            pltpu.VMEM((nsec, 64, 128), H),
            pltpu.VMEM((nsec, 64, 128), H),
            pltpu.VMEM((nch, NT, 576), F),
            pltpu.VMEM((5, 384, 128), F),
            pltpu.VMEM((8, 128), F),
            pltpu.VMEM((nsec, 8, 128), F),
            pltpu.VMEM((16, 640), F),
            pltpu.VMEM((1024, 128), F),
            pltpu.VMEM((1664, 128), F),
            pltpu.VMEM((208, 32), H),
            pltpu.VMEM((NW, 256, 128), H),
            pltpu.VMEM((2, NB, 208, 128), H),
            pltpu.VMEM((NW, 384, 128), F),
            pltpu.VMEM((384, 128), F),
            pltpu.VMEM((384, 128), F),
            dma((2, nsec)), dma((2, nsec)), dma((nch,)), dma((nch,)), dma((nsec,)), dma((nsec,)),
        ],
        compiler_params=pltpu.CompilerParams(collective_id=0, has_side_effects=True, vmem_limit_bytes=40 * 2**20),
        name="lanczos",
    )(
        jnp.swapaxes(left_env[0], 0, 1), jnp.swapaxes(right_env[0], 0, 1), env_slot, transfer[0], wavefunction[0],
        pair_ops[0], kept_ranks,
    )
    return out[None], en[0, :1]


def solution(mesh):
    return jax.shard_map(
        body,
        mesh=mesh,
        in_specs=(
            P("chain", "sector", None, None),
            P("chain", "sector", None),
            P("chain", "sector", None, None),
            P("chain", "sector", None, None),
            P("chain", None, None),
            P("chain", None),
            P("chain", "sector"),
        ),
        out_specs=(P("chain", "sector", None, None), P("chain")),
        check_vma=False,
    )
```

```python
import functools

import jax
import jax.numpy as jnp
from jax import lax
from jax.experimental import pallas as pl
from jax.experimental.pallas import tpu as pltpu
from jax.sharding import PartitionSpec as P

F = jnp.float32
H = jnp.bfloat16
NT = 4
NB = 24
NP = 16
NW = 13
MESH = pl.DeviceIdType.MESH


def split(x):
    h = x.astype(H)
    return h, (x - h.astype(F)).astype(H)


def grab(tile, off, t, lane):
    c0, o = off // 128, off % 128
    sh = (32 * t - o) % 128
    a = tile(c0)
    a = pltpu.roll(a, sh, 1) if sh else a
    if o + NB > 128:
        b = tile(c0 + 1)
        b = pltpu.roll(b, sh, 1) if sh else b
        a = jnp.where(lane < 32 * t + 128 - o, a, b)
    return jnp.where((lane >= 32 * t) & (lane < 32 * t + NB), a, 0.0)


def full(x):
    return jnp.sum(jnp.sum(x, axis=0, keepdims=True), axis=1, keepdims=True)


def inverse(n):
    return jnp.where(n > 0, 1.0 / n, 0.0)


def loop(a, b, f):
    def step(j, c):
        f(j)
        return c

    lax.fori_loop(a, b, step, 0)


def global_solve(q0,q1,entries):
    tot=lambda x: jnp.sum(x,axis=1,keepdims=True)
    pos={}
    n=0
    for i in range(4):
        for j in range(i,5):
            pos[i,j]=n; n+=1
    M=[[q0(pos[min(i,j),max(i,j)]) for j in range(4)] for i in range(4)]
    Mk=[[q1(pos[min(i,j),max(i,j)]) for j in range(4)] for i in range(4)]
    Wv=[q0(pos[i,4]) for i in range(4)]
    n0=q0(16); al=[q0(17+i) for i in range(3)]; be=[q0(20+i) for i in range(3)]
    def tmul(c):
        k=len(c)-1
        y=[None]*min(k+2,4)
        def add(i,z):
            y[i]=z if y[i] is None else y[i]+z
        for j in range(min(k+1,3)):
            add(j,al[j]*c[j]); add(j+1,be[j]*c[j])
            if j>0: add(j-1,be[j-1]*c[j])
        return y
    def dot(Mx,a,b):
        acc=None
        for i in range(len(a)):
            s=None
            for j in range(len(b)):
                z=Mx[i][j]*b[j]; s=z if s is None else s+z
            s=s*a[i]; acc=s if acc is None else acc+s
        return acc
    c=[n0/jnp.sqrt(tot(n0*n0))]
    cp=[]; b=None
    cs=[]; A=[]; Bt=[]
    for k in range(4):
        cs.append(c)
        y=tmul(c)
        g=dot(M,c,y)
        if k==3:
            s=None
            for i in range(4):
                z=c[i]*Wv[i]; s=z if s is None else s+z
            g=g+s*c[3]
        a=tot(g); A.append(a)
        if k<3:
            r=[]
            for i in range(len(y)):
                z=y[i]
                if i<len(c): z=z-a*c[i]
                if i<len(cp): z=z-b*cp[i]
                r.append(z)
            b=jnp.sqrt(tot(dot(M,r,r))); Bt.append(b)
            cp=c; c=[z/b for z in r]
    ab=[jnp.abs(z) for z in Bt]
    bounds=[A[0]-ab[0],A[1]-ab[0]-ab[1],A[2]-ab[1]-ab[2],A[3]-ab[2]]
    init=jnp.minimum(jnp.minimum(bounds[0],bounds[1]),jnp.minimum(bounds[2],bounds[3]))-1.0
    B2=[z*z for z in Bt]
    def newton(_,e):
        vp=jnp.ones_like(e); vn=A[0]-e; sp=jnp.zeros_like(e); sn=-jnp.ones_like(e)
        for p in range(1,4):
            sh=A[p]-e; w=B2[p-1]
            v2=sh*vn-w*vp; s2=sh*sn-vn-w*sp
            vp,vn=vn,v2; sp,sn=sn,s2
        return e-vn/sn
    e=lax.fori_loop(0,40,newton,init)
    co=[jnp.ones_like(e),(e-A[0])/Bt[0]]
    for p in range(1,3):
        co.append(((e-A[p])*co[p]-Bt[p-1]*co[p-1])/Bt[p])
    nrm=jnp.sqrt(co[0]*co[0]+co[1]*co[1]+co[2]*co[2]+co[3]*co[3])
    f=[None]*4
    for k in range(4):
        for i in range(len(cs[k])):
            z=(co[k]/nrm)*cs[k][i]; f[i]=z if f[i] is None else f[i]+z
    scale=jnp.sqrt(entries/tot(dot(Mk,f,f)))
    return e,[z*scale for z in f]


def whole(
    entries, nsec, nch,
    left_in, right_in, slot_in, tr_in, x_in, b_in, kept_in,
    out_ref, en_ref,
    left, right, slot_ref, tr, x_ref, b_ref, kept_ref, lsem,
    wide, wire, cat, stage, recv0, recv1, trecv, v_ref, st, strecv,
    tpad, tbd, ebd, b2, c2, mixed, moved, acat, ybuf,
    ssem, rsem, tssem, trsem, qssem, qrsem,
):
    me = lax.axis_index("sector")
    ch = lax.axis_index("chain")
    cap = left_in.shape[1]
    lane = lax.broadcasted_iota(jnp.int32, (1, 128), 1)
    tl = lane // 32
    loads = [
        pltpu.make_async_copy(a, b, lsem.at[i])
        for i, (a, b) in enumerate((
            (slot_in, slot_ref), (left_in, left), (tr_in, tr), (right_in, right), (b_in, b_ref), (x_in, x_ref), (kept_in, kept_ref)))
    ]
    for c in loads:
        c.start()
    bar = pltpu.get_barrier_semaphore()
    loop(1, nsec, lambda j: pl.semaphore_signal(bar, inc=1, device_id=(ch, lax.rem(me + j, nsec)), device_id_type=MESH))
    loop(1, nch, lambda j: pl.semaphore_signal(bar, inc=1, device_id=(lax.rem(ch + j, nch), me), device_id_type=MESH))
    def pack(side, src, chosen):
        wire[...] = jnp.zeros_like(wire)
        for w in range(NW):
            row8 = src[w].astype(F)
            for c in range(4):
                wide[c, cap * w:cap * w + cap, :] = row8[:, 128 * c:128 * c + 128]
            wide[4, cap * w:cap * w + cap, 0:64] = row8[:, 512:576]
        for s in range(cap):
            for c in range(4):
                wire[s, 13 * c:13 * c + 13, :] = wide[c, pl.ds(s, 13, stride=cap), :]
            lo = wide[4, pl.ds(s, 7, stride=cap), :]
            hi = pltpu.roll(wide[4, pl.ds(s + 7 * cap, 6, stride=cap), :], 64, 1)
            wire[s, 52:59, :] = jnp.where(lane < 64, lo, 0.0)
            wire[s, 52:58, :] = jnp.where(lane < 64, lo[0:6], hi)
        cat[side] = wire[...].astype(H)
        for j in range(nsec):
            stage[side, j] = cat[side, chosen[j]]

    def tcopy(j):
        return pltpu.make_async_remote_copy(
            src_ref=tr, dst_ref=trecv.at[ch], send_sem=tssem.at[j], recv_sem=trsem.at[j],
            device_id=(lax.rem(ch + j, nch), me), device_id_type=MESH)

    def ecopy(side, j):
        return pltpu.make_async_remote_copy(
            src_ref=stage.at[side, j], dst_ref=(recv0, recv1)[side].at[j], send_sem=ssem.at[side, j], recv_sem=rsem.at[side, j],
            device_id=(ch, lax.rem(me + j, nsec)), device_id_type=MESH)

    loads[0].wait()
    chosen = []
    for j in range(nsec):
        h = lax.rem(me + j, nsec)
        s = jnp.int32(0)
        for k in range(NT):
            g = slot_ref[0, h * NT + k]
            s = s + jnp.where(g // cap == me, lax.rem(g, cap), 0)
        chosen.append(s)
    loads[1].wait()
    pack(1, left, chosen)
    loads[2].wait()
    trecv[ch] = tr[...]
    pl.semaphore_wait(bar, nsec + nch - 2)
    loop(1, nch, lambda j: tcopy(j).start())
    loop(1, nsec, lambda j: ecopy(1, j).start())
    loads[3].wait()
    pack(0, right, chosen)
    loop(1, nsec, lambda j: ecopy(0, j).start())
    recv0[0] = stage[0, 0]
    recv1[0] = stage[1, 0]
    loads[4].wait()
    loads[5].wait()
    loads[6].wait()

    bf = b_ref[...].astype(F)
    for q in range(NP):
        off = 16 * q
        a = bf[:, (off // 128) * 128:(off // 128) * 128 + 128]
        sh = (-(off % 128)) % 128
        a = pltpu.roll(a, sh, 1) if sh else a
        tbd[pl.ds(q, NW, stride=NP), :] = jnp.where(lane < 16, a, 0.0)
    bb = tbd[0:208, :]
    b2[...] = (bb + pltpu.roll(bb, 16, 1))[:, :32].astype(H)
    for p in range(NP):
        acc = jnp.zeros((NB, 128), F)
        for t in range(NT):
            acc = acc + grab(lambda c: x_ref[t, :, c * 128:(c + 1) * 128], NB * p, t, lane)
        v_ref[0, pl.ds(p, NB, stride=NP), :] = acc
    x = v_ref[0]
    n0 = jnp.sqrt(full(x * x))
    v_ref[0] = x * inverse(n0)
    loop(1, nch, lambda j: tcopy(j).wait())
    tbd[...] = jnp.zeros_like(tbd)
    for t in range(NT):
        tpad[0:8, 0:576] = trecv[:, t, :]
        for i in range(NB):
            tbd[pl.ds(32 * t + i, 8, stride=128), :] = grab(lambda c: tpad[0:8, c * 128:(c + 1) * 128], NB * i, t, lane)
    row = lax.broadcasted_iota(jnp.int32, (128, 128), 0)
    col = lax.broadcasted_iota(jnp.int32, (128, 128), 1)
    eye = (row == col).astype(F)
    T = [jnp.where(ch > c, tbd[c * 128:(c + 1) * 128, :], eye) for c in range(7)]

    def mm(a, b):
        return jnp.dot(a, b, precision=lax.Precision.HIGHEST, preferred_element_type=F)

    pre = mm(mm(T[6], mm(T[5], T[4])), mm(mm(T[3], T[2]), mm(T[1], T[0])))
    ph, plo = split(pre.T)

    ebd[...] = jnp.zeros_like(ebd)

    def spread(side):
        for t in range(NT):
            o = slot_ref[0, me * NT + t] // cap
            wire[t] = (recv0, recv1)[side][lax.rem(me - o + nsec, nsec)].astype(F)
            tpad[0:7, 0:128] = wire[t, 52:59, :]
            tpad[7:13, 0:128] = pltpu.roll(wire[t, 52:58, :], 64, 1)
            tile = lambda c: wire[t, 13 * c:13 * c + 13, :] if c < 4 else tpad[0:13, 0:128]
            for i in range(NB):
                ebd[pl.ds(32 * t + i, NW, stride=128), :] = grab(tile, NB * i, t, lane)

    def pair_step(k):
        bm = b2[...]
        for l in range(0, NB, 2):
            xx = jnp.concatenate([v_ref[k, 16 * l:16 * l + 16, :], v_ref[k, 16 * l + 16:16 * l + 32, :]], 1)
            h, lo = split(xx)
            o = jnp.dot(bm, jnp.concatenate([h, lo], 0), preferred_element_type=F)
            h, lo = split(o)
            mixed[0, l] = h[:, :128]
            mixed[0, l + 1] = h[:, 128:]
            mixed[1, l] = lo[:, :128]
            mixed[1, l + 1] = lo[:, 128:]

    def right_step():
        for w in range(NW):
            h = mixed[0, :, 16 * w:16 * w + 16, :].reshape(384, 128)
            lo = mixed[1, :, 16 * w:16 * w + 16, :].reshape(384, 128)
            moved[w] = jnp.dot(jnp.concatenate([h, lo], 1), c2[w], preferred_element_type=F)

    def left_step(k, a2):
        for q in range(0, NP, 2):
            r = jnp.concatenate([jnp.concatenate([moved[w, pl.ds(q + j, NB, stride=NP), :] for w in range(NW)], 0) for j in range(2)], 1)
            h = r.astype(H).astype(F)
            o = jnp.dot(a2, jnp.concatenate([h, r - h], 0).astype(H), preferred_element_type=F)
            for j in range(2):
                oj = o[:, 128 * j:128 * j + 128]
                y = jnp.where(tl == 0, oj[0:24], jnp.where(tl == 1, oj[24:48], jnp.where(tl == 2, oj[48:72], oj[72:96])))
                v_ref[k + 1, pl.ds(q + j, NB, stride=NP), :] = y

    pair_step(0)
    loop(1, nsec, lambda j: ecopy(1, j).wait())
    spread(1)
    pp = jnp.concatenate([ph, plo], 0)
    pq = jnp.concatenate([ph, plo, ph], 0)
    for w in range(NW):
        e = ebd[w * 128:(w + 1) * 128, :].astype(H)
        s = jnp.dot(jnp.concatenate([e, e], 1), pp, preferred_element_type=F)
        sh, sl = split(s.T)
        at = jnp.dot(jnp.concatenate([sh, sh, sl], 1), pq, preferred_element_type=F)
        acat[24 * w:24 * w + 24, :] = at[0:24] + at[32:56] + at[64:88] + at[96:120]
    acat[312:384, :] = jnp.zeros((72, 128), F)
    al = acat[...].T
    al = jnp.concatenate([al[32 * t:32 * t + 24] for t in range(NT)], 0)[:, :312].astype(H).astype(F)
    a2 = jnp.concatenate([al, al], 1).astype(H)
    loop(1, nsec, lambda j: ecopy(0, j).wait())
    spread(0)
    for w in range(NW):
        ct = ebd[w * 128:(w + 1) * 128, :].T.astype(H)
        c2[w, 0:128, :] = ct
        c2[w, 128:256, :] = ct
    right_step()

    alphas = []
    betas = []
    for k in range(4):
        if k > 0:
            pair_step(k)
            right_step()
        left_step(k, a2)
        if k < 3:
            y = v_ref[k + 1]
            a = full(v_ref[k] * y)
            r = y - a * v_ref[k]
            if k > 0:
                r = r - betas[-1] * v_ref[k - 1]
            b = jnp.sqrt(full(r * r))
            alphas.append(a)
            betas.append(b)
            v_ref[k + 1] = r * inverse(b)
    rows = []
    for i in range(4):
        for j in range(i, 5):
            rows.append(jnp.sum(v_ref[i] * v_ref[j], axis=0, keepdims=True))
    g = jnp.concatenate(rows + [jnp.zeros((114, 128), F)], 0)
    kp = jnp.where(tl == 0, kept_ref[0, 0], jnp.where(tl == 1, kept_ref[0, 1], jnp.where(tl == 2, kept_ref[0, 2], kept_ref[0, 3])))
    keep = lax.rem(lane, 32) < kp
    r8 = lax.broadcasted_iota(jnp.int32, (8, 128), 0)
    lhs = jnp.where(r8 == 0, 1.0, jnp.where((r8 == 1) & keep, 1.0, 0.0))
    s = lax.dot_general(lhs, g, (((1,), (1,)), ((), ())), precision=lax.Precision.HIGHEST, preferred_element_type=F)
    for i, val in enumerate([n0] + alphas + betas):
        s = s + jnp.where((lane == 16 + i) & (r8 == 0), val, 0.0)
    st[...] = s

    def qcopy(j):
        return pltpu.make_async_remote_copy(
            src_ref=st, dst_ref=strecv.at[me], send_sem=qssem.at[j], recv_sem=qrsem.at[j],
            device_id=(ch, lax.rem(me + j, nsec)), device_id_type=MESH)

    loop(1, nsec, lambda j: qcopy(j).start())
    strecv[me] = s
    loop(1, nsec, lambda j: qcopy(j).wait())
    z = jnp.zeros((128 - nsec, 128), F)
    q0 = jnp.concatenate([strecv[:, 0, :], z], 0).T
    q1 = jnp.concatenate([strecv[:, 1, :], z], 0).T
    e, f = global_solve(lambda i: q0[i:i + 1, :], lambda i: q1[i:i + 1, :], entries)
    en_ref[...] = e
    mine = [jnp.sum(jnp.where(lane == me, c, 0.0), axis=1, keepdims=True) for c in f]
    y = mine[0] * v_ref[0]
    for i in range(1, 4):
        y = y + mine[i] * v_ref[i]
    ybuf[...] = jnp.where(keep, y, 0.0)
    for p in range(NP):
        a = ybuf[pl.ds(p, NB, stride=NP), :]
        for t in range(NT):
            out_ref[t, :, NB * p:NB * p + NB] = a[:, 32 * t:32 * t + NB]


def body(wavefunction, transfer, left_env, right_env, pair_ops, env_slot, kept_ranks):
    nsec = lax.axis_size("sector")
    nch = lax.axis_size("chain")
    cap = left_env.shape[1]
    entries = float(nsec * NT * NB * NP * NB)
    vmem = pl.BlockSpec(memory_space=pltpu.VMEM)
    hbm = pl.BlockSpec(memory_space=pltpu.HBM)
    dma = pltpu.SemaphoreType.DMA
    out, en = pl.pallas_call(
        functools.partial(whole, entries, nsec, nch),
        out_shape=(jax.ShapeDtypeStruct((NT, NB, NP * NB), F), jax.ShapeDtypeStruct((1, 1), F)),
        in_specs=[hbm] * 7,
        out_specs=(vmem, vmem),
        scratch_shapes=[
            pltpu.VMEM((NW, cap, 576), H),
            pltpu.VMEM((NW, cap, 576), H),
            pltpu.SMEM(env_slot.shape, jnp.int32),
            pltpu.VMEM(transfer.shape[1:], F),
            pltpu.VMEM(wavefunction.shape[1:], F),
            pltpu.VMEM(pair_ops.shape[1:], H),
            pltpu.SMEM(kept_ranks.shape, jnp.int32),
            dma((7,)),
            pltpu.VMEM((5, cap * NW, 128), F),
            pltpu.VMEM((cap, 64, 128), F),
            pltpu.VMEM((2, cap, 64, 128), H),
            pltpu.VMEM((2, nsec, 64, 128), H),
            pltpu.VMEM((nsec, 64, 128), H),
            pltpu.VMEM((nsec, 64, 128), H),
            pltpu.VMEM((nch, NT, 576), F),
            pltpu.VMEM((5, 384, 128), F),
            pltpu.VMEM((8, 128), F),
            pltpu.VMEM((nsec, 8, 128), F),
            pltpu.VMEM((16, 640), F),
            pltpu.VMEM((1024, 128), F),
            pltpu.VMEM((1664, 128), F),
            pltpu.VMEM((208, 32), H),
            pltpu.VMEM((NW, 256, 128), H),
            pltpu.VMEM((2, NB, 208, 128), H),
            pltpu.VMEM((NW, 384, 128), F),
            pltpu.VMEM((384, 128), F),
            pltpu.VMEM((384, 128), F),
            dma((2, nsec)), dma((2, nsec)), dma((nch,)), dma((nch,)), dma((nsec,)), dma((nsec,)),
        ],
        compiler_params=pltpu.CompilerParams(collective_id=0, has_side_effects=True, vmem_limit_bytes=64 * 2**20),
        name="lanczos",
    )(
        jnp.swapaxes(left_env[0], 0, 1), jnp.swapaxes(right_env[0], 0, 1), env_slot, transfer[0], wavefunction[0],
        pair_ops[0], kept_ranks,
    )
    return out[None], en.reshape(1)


def solution(mesh):
    return jax.shard_map(
        body,
        mesh=mesh,
        in_specs=(
            P("chain", "sector", None, None),
            P("chain", "sector", None),
            P("chain", "sector", None, None),
            P("chain", "sector", None, None),
            P("chain", None, None),
            P("chain", None),
            P("chain", "sector"),
        ),
        out_specs=(P("chain", "sector", None, None), P("chain")),
        check_vma=False,
    )
```

```python
import functools

import jax
import jax.numpy as jnp
from jax import lax
from jax.experimental import pallas as pl
from jax.experimental.pallas import tpu as pltpu
from jax.sharding import PartitionSpec as P

F = jnp.float32
H = jnp.bfloat16
NT = 4
NB = 24
NP = 16
NW = 13
MESH = pl.DeviceIdType.MESH


def split(x):
    h = x.astype(H)
    return h, (x - h.astype(F)).astype(H)


def grab(tile, off, t, lane):
    c0, o = off // 128, off % 128
    sh = (32 * t - o) % 128
    a = tile(c0)
    a = pltpu.roll(a, sh, 1) if sh else a
    if o + NB > 128:
        b = tile(c0 + 1)
        b = pltpu.roll(b, sh, 1) if sh else b
        a = jnp.where(lane < 32 * t + 128 - o, a, b)
    return jnp.where((lane >= 32 * t) & (lane < 32 * t + NB), a, 0.0)


def full(x):
    return jnp.sum(jnp.sum(x, axis=0, keepdims=True), axis=1, keepdims=True)


def inverse(n):
    return jnp.where(n > 0, 1.0 / n, 0.0)


def loop(a, b, f):
    def step(j, c):
        f(j)
        return c

    lax.fori_loop(a, b, step, 0)


def global_solve(q0,q1,entries):
    tot=lambda x: jnp.sum(x,axis=1,keepdims=True)
    pos={}
    n=0
    for i in range(4):
        for j in range(i,5):
            pos[i,j]=n; n+=1
    M=[[q0(pos[min(i,j),max(i,j)]) for j in range(4)] for i in range(4)]
    Mk=[[q1(pos[min(i,j),max(i,j)]) for j in range(4)] for i in range(4)]
    Wv=[q0(pos[i,4]) for i in range(4)]
    n0=q0(16); al=[q0(17+i) for i in range(3)]; be=[q0(20+i) for i in range(3)]
    def tmul(c):
        k=len(c)-1
        y=[None]*min(k+2,4)
        def add(i,z):
            y[i]=z if y[i] is None else y[i]+z
        for j in range(min(k+1,3)):
            add(j,al[j]*c[j]); add(j+1,be[j]*c[j])
            if j>0: add(j-1,be[j-1]*c[j])
        return y
    def dot(Mx,a,b):
        acc=None
        for i in range(len(a)):
            s=None
            for j in range(len(b)):
                z=Mx[i][j]*b[j]; s=z if s is None else s+z
            s=s*a[i]; acc=s if acc is None else acc+s
        return acc
    c=[n0/jnp.sqrt(tot(n0*n0))]
    cp=[]; b=None
    cs=[]; A=[]; Bt=[]
    for k in range(4):
        cs.append(c)
        y=tmul(c)
        g=dot(M,c,y)
        if k==3:
            s=None
            for i in range(4):
                z=c[i]*Wv[i]; s=z if s is None else s+z
            g=g+s*c[3]
        a=tot(g); A.append(a)
        if k<3:
            r=[]
            for i in range(len(y)):
                z=y[i]
                if i<len(c): z=z-a*c[i]
                if i<len(cp): z=z-b*cp[i]
                r.append(z)
            b=jnp.sqrt(tot(dot(M,r,r))); Bt.append(b)
            cp=c; c=[z/b for z in r]
    ab=[jnp.abs(z) for z in Bt]
    bounds=[A[0]-ab[0],A[1]-ab[0]-ab[1],A[2]-ab[1]-ab[2],A[3]-ab[2]]
    init=jnp.minimum(jnp.minimum(bounds[0],bounds[1]),jnp.minimum(bounds[2],bounds[3]))-1.0
    B2=[z*z for z in Bt]
    def newton(_,e):
        vp=jnp.ones_like(e); vn=A[0]-e; sp=jnp.zeros_like(e); sn=-jnp.ones_like(e)
        for p in range(1,4):
            sh=A[p]-e; w=B2[p-1]
            v2=sh*vn-w*vp; s2=sh*sn-vn-w*sp
            vp,vn=vn,v2; sp,sn=sn,s2
        return e-vn/sn
    e=lax.fori_loop(0,40,newton,init)
    co=[jnp.ones_like(e),(e-A[0])/Bt[0]]
    for p in range(1,3):
        co.append(((e-A[p])*co[p]-Bt[p-1]*co[p-1])/Bt[p])
    nrm=jnp.sqrt(co[0]*co[0]+co[1]*co[1]+co[2]*co[2]+co[3]*co[3])
    f=[None]*4
    for k in range(4):
        for i in range(len(cs[k])):
            z=(co[k]/nrm)*cs[k][i]; f[i]=z if f[i] is None else f[i]+z
    scale=jnp.sqrt(entries/tot(dot(Mk,f,f)))
    return e,[z*scale for z in f]


def whole(
    entries, nsec, nch,
    left_in, right_in, slot_in, tr_in, x_in, b_in, kept_in,
    out_ref, en_ref,
    left, right, slot_ref, tr, x_ref, b_ref, kept_ref, lsem,
    wide, wire, cat, stage, recv0, recv1, trecv, v_ref, st, strecv,
    tpad, tbd, ebd, b2, c2, mixed, moved, acat, ybuf,
    ssem, rsem, tssem, trsem, qssem, qrsem,
):
    me = lax.axis_index("sector")
    ch = lax.axis_index("chain")
    cap = left_in.shape[1]
    lane = lax.broadcasted_iota(jnp.int32, (1, 128), 1)
    tl = lane // 32
    loads = [
        pltpu.make_async_copy(a, b, lsem.at[i])
        for i, (a, b) in enumerate((
            (slot_in, slot_ref), (left_in, left), (tr_in, tr), (right_in, right), (b_in, b_ref), (x_in, x_ref), (kept_in, kept_ref)))
    ]
    for c in loads:
        c.start()
    bar = pltpu.get_barrier_semaphore()
    loop(1, nsec, lambda j: pl.semaphore_signal(bar, inc=1, device_id=(ch, lax.rem(me + j, nsec)), device_id_type=MESH))
    loop(1, nch, lambda j: pl.semaphore_signal(bar, inc=1, device_id=(lax.rem(ch + j, nch), me), device_id_type=MESH))
    def pack(side, src, chosen):
        wire[...] = jnp.zeros_like(wire)
        for w in range(NW):
            row8 = src[w].astype(F)
            for c in range(4):
                wide[c, cap * w:cap * w + cap, :] = row8[:, 128 * c:128 * c + 128]
            wide[4, cap * w:cap * w + cap, 0:64] = row8[:, 512:576]
        for s in range(cap):
            for c in range(4):
                wire[s, 13 * c:13 * c + 13, :] = wide[c, pl.ds(s, 13, stride=cap), :]
            lo = wide[4, pl.ds(s, 7, stride=cap), :]
            hi = pltpu.roll(wide[4, pl.ds(s + 7 * cap, 6, stride=cap), :], 64, 1)
            wire[s, 52:59, :] = jnp.where(lane < 64, lo, 0.0)
            wire[s, 52:58, :] = jnp.where(lane < 64, lo[0:6], hi)
        cat[side] = wire[...].astype(H)
        for j in range(nsec):
            stage[side, j] = cat[side, chosen[j]]

    def tcopy(j):
        return pltpu.make_async_remote_copy(
            src_ref=tr, dst_ref=trecv.at[ch], send_sem=tssem.at[j], recv_sem=trsem.at[j],
            device_id=(lax.rem(ch + j, nch), me), device_id_type=MESH)

    def ecopy(side, j):
        return pltpu.make_async_remote_copy(
            src_ref=stage.at[side, j], dst_ref=(recv0, recv1)[side].at[j], send_sem=ssem.at[side, j], recv_sem=rsem.at[side, j],
            device_id=(ch, lax.rem(me + j, nsec)), device_id_type=MESH)

    loads[0].wait()
    chosen = []
    for j in range(nsec):
        h = lax.rem(me + j, nsec)
        s = jnp.int32(0)
        for k in range(NT):
            g = slot_ref[0, h * NT + k]
            s = s + jnp.where(g // cap == me, lax.rem(g, cap), 0)
        chosen.append(s)
    loads[1].wait()
    pack(1, left, chosen)
    loads[2].wait()
    trecv[ch] = tr[...]
    pl.semaphore_wait(bar, nsec + nch - 2)
    loop(1, nch, lambda j: tcopy(j).start())
    loop(1, nsec, lambda j: ecopy(1, j).start())
    loads[3].wait()
    pack(0, right, chosen)
    loop(1, nsec, lambda j: ecopy(0, j).start())
    recv0[0] = stage[0, 0]
    recv1[0] = stage[1, 0]
    loads[4].wait()
    loads[5].wait()
    loads[6].wait()

    bf = b_ref[...].astype(F)
    for q in range(NP):
        off = 16 * q
        a = bf[:, (off // 128) * 128:(off // 128) * 128 + 128]
        sh = (-(off % 128)) % 128
        a = pltpu.roll(a, sh, 1) if sh else a
        tbd[pl.ds(q, NW, stride=NP), :] = jnp.where(lane < 16, a, 0.0)
    bb = tbd[0:208, :]
    b2[...] = (bb + pltpu.roll(bb, 16, 1))[:, :32].astype(H)
    for p in range(NP):
        acc = jnp.zeros((NB, 128), F)
        for t in range(NT):
            acc = acc + grab(lambda c: x_ref[t, :, c * 128:(c + 1) * 128], NB * p, t, lane)
        v_ref[0, pl.ds(p, NB, stride=NP), :] = acc
    x = v_ref[0]
    n0 = jnp.sqrt(full(x * x))
    v_ref[0] = x * inverse(n0)
    loop(1, nch, lambda j: tcopy(j).wait())
    tbd[...] = jnp.zeros_like(tbd)
    for t in range(NT):
        tpad[0:8, 0:576] = trecv[:, t, :]
        for i in range(NB):
            tbd[pl.ds(32 * t + i, 8, stride=128), :] = grab(lambda c: tpad[0:8, c * 128:(c + 1) * 128], NB * i, t, lane)
    row = lax.broadcasted_iota(jnp.int32, (128, 128), 0)
    col = lax.broadcasted_iota(jnp.int32, (128, 128), 1)
    eye = (row == col).astype(F)
    T = [jnp.where(ch > c, tbd[c * 128:(c + 1) * 128, :], eye) for c in range(7)]

    def mm(a, b):
        return jnp.dot(a, b, precision=lax.Precision.HIGHEST, preferred_element_type=F)

    pre = mm(mm(T[6], mm(T[5], T[4])), mm(mm(T[3], T[2]), mm(T[1], T[0])))
    ph, plo = split(pre.T)

    ebd[...] = jnp.zeros_like(ebd)

    def spread(side):
        for t in range(NT):
            o = slot_ref[0, me * NT + t] // cap
            wire[t] = (recv0, recv1)[side][lax.rem(me - o + nsec, nsec)].astype(F)
            tpad[0:7, 0:128] = wire[t, 52:59, :]
            tpad[7:13, 0:128] = pltpu.roll(wire[t, 52:58, :], 64, 1)
            tile = lambda c: wire[t, 13 * c:13 * c + 13, :] if c < 4 else tpad[0:13, 0:128]
            for i in range(NB):
                ebd[pl.ds(32 * t + i, NW, stride=128), :] = grab(tile, NB * i, t, lane)

    def pair_step(k):
        bm = b2[...]
        for l in range(0, NB, 2):
            xx = jnp.concatenate([v_ref[k, 16 * l:16 * l + 16, :], v_ref[k, 16 * l + 16:16 * l + 32, :]], 1)
            h, lo = split(xx)
            o = jnp.dot(bm, jnp.concatenate([h, lo], 0), preferred_element_type=F)
            h, lo = split(o)
            mixed[0, l] = h[:, :128]
            mixed[0, l + 1] = h[:, 128:]
            mixed[1, l] = lo[:, :128]
            mixed[1, l + 1] = lo[:, 128:]

    def right_step():
        for w in range(NW):
            h = mixed[0, :, 16 * w:16 * w + 16, :].reshape(384, 128)
            lo = mixed[1, :, 16 * w:16 * w + 16, :].reshape(384, 128)
            o = jnp.dot(jnp.concatenate([h, lo], 1), c2[w], preferred_element_type=F)
            moved[w] = jnp.swapaxes(o.reshape(NB, NP, 128), 0, 1)

    def left_step(k, a2):
        for q in range(0, NP, 2):
            r = jnp.concatenate([jnp.concatenate([moved[w, q + j] for w in range(NW)], 0) for j in range(2)], 1)
            h = r.astype(H).astype(F)
            o = jnp.dot(a2, jnp.concatenate([h, r - h], 0).astype(H), preferred_element_type=F)
            for j in range(2):
                oj = o[:, 128 * j:128 * j + 128]
                y = jnp.where(tl == 0, oj[0:24], jnp.where(tl == 1, oj[24:48], jnp.where(tl == 2, oj[48:72], oj[72:96])))
                v_ref[k + 1, pl.ds(q + j, NB, stride=NP), :] = y

    pair_step(0)
    loop(1, nsec, lambda j: ecopy(1, j).wait())
    spread(1)
    pp = jnp.concatenate([ph, plo], 0)
    pq = jnp.concatenate([ph, plo, ph], 0)
    for w in range(NW):
        e = ebd[w * 128:(w + 1) * 128, :].astype(H)
        s = jnp.dot(jnp.concatenate([e, e], 1), pp, preferred_element_type=F)
        sh, sl = split(s.T)
        at = jnp.dot(jnp.concatenate([sh, sh, sl], 1), pq, preferred_element_type=F)
        acat[24 * w:24 * w + 24, :] = at[0:24] + at[32:56] + at[64:88] + at[96:120]
    acat[312:384, :] = jnp.zeros((72, 128), F)
    al = acat[...].T
    al = jnp.concatenate([al[32 * t:32 * t + 24] for t in range(NT)], 0)[:, :312].astype(H).astype(F)
    a2 = jnp.concatenate([al, al], 1).astype(H)
    loop(1, nsec, lambda j: ecopy(0, j).wait())
    spread(0)
    for w in range(NW):
        ct = ebd[w * 128:(w + 1) * 128, :].T.astype(H)
        c2[w, 0:128, :] = ct
        c2[w, 128:256, :] = ct
    right_step()

    alphas = []
    betas = []
    for k in range(4):
        if k > 0:
            pair_step(k)
            right_step()
        left_step(k, a2)
        if k < 3:
            y = v_ref[k + 1]
            a = full(v_ref[k] * y)
            r = y - a * v_ref[k]
            if k > 0:
                r = r - betas[-1] * v_ref[k - 1]
            b = jnp.sqrt(full(r * r))
            alphas.append(a)
            betas.append(b)
            v_ref[k + 1] = r * inverse(b)
    rows = []
    for i in range(4):
        for j in range(i, 5):
            rows.append(jnp.sum(v_ref[i] * v_ref[j], axis=0, keepdims=True))
    g = jnp.concatenate(rows + [jnp.zeros((114, 128), F)], 0)
    kp = jnp.where(tl == 0, kept_ref[0, 0], jnp.where(tl == 1, kept_ref[0, 1], jnp.where(tl == 2, kept_ref[0, 2], kept_ref[0, 3])))
    keep = lax.rem(lane, 32) < kp
    r8 = lax.broadcasted_iota(jnp.int32, (8, 128), 0)
    lhs = jnp.where(r8 == 0, 1.0, jnp.where((r8 == 1) & keep, 1.0, 0.0))
    s = lax.dot_general(lhs, g, (((1,), (1,)), ((), ())), precision=lax.Precision.HIGHEST, preferred_element_type=F)
    s = s[0:1] + pltpu.roll(s[1:2], 64, 1)
    for i, val in enumerate([n0] + alphas + betas):
        s = s + jnp.where(lane == 16 + i, val, 0.0)
    st[...] = s

    def qcopy(j):
        return pltpu.make_async_remote_copy(
            src_ref=st, dst_ref=strecv.at[me], send_sem=qssem.at[j], recv_sem=qrsem.at[j],
            device_id=(ch, lax.rem(me + j, nsec)), device_id_type=MESH)

    loop(1, nsec, lambda j: qcopy(j).start())
    strecv[me] = s
    loop(1, nsec, lambda j: qcopy(j).wait())
    z = jnp.zeros((128 - nsec, 128), F)
    q0 = jnp.concatenate([strecv[:, 0, :], z], 0).T
    e, f = global_solve(lambda i: q0[i:i + 1, :], lambda i: q0[64 + i:65 + i, :], entries)
    en_ref[...] = e
    mine = [jnp.sum(jnp.where(lane == me, c, 0.0), axis=1, keepdims=True) for c in f]
    y = mine[0] * v_ref[0]
    for i in range(1, 4):
        y = y + mine[i] * v_ref[i]
    ybuf[...] = jnp.where(keep, y, 0.0)
    for p in range(NP):
        a = ybuf[pl.ds(p, NB, stride=NP), :]
        for t in range(NT):
            out_ref[t, :, NB * p:NB * p + NB] = a[:, 32 * t:32 * t + NB]


def body(wavefunction, transfer, left_env, right_env, pair_ops, env_slot, kept_ranks):
    nsec = lax.axis_size("sector")
    nch = lax.axis_size("chain")
    cap = left_env.shape[1]
    entries = float(nsec * NT * NB * NP * NB)
    vmem = pl.BlockSpec(memory_space=pltpu.VMEM)
    hbm = pl.BlockSpec(memory_space=pltpu.HBM)
    dma = pltpu.SemaphoreType.DMA
    out, en = pl.pallas_call(
        functools.partial(whole, entries, nsec, nch),
        out_shape=(jax.ShapeDtypeStruct((NT, NB, NP * NB), F), jax.ShapeDtypeStruct((1, 1), F)),
        in_specs=[hbm] * 7,
        out_specs=(vmem, vmem),
        scratch_shapes=[
            pltpu.VMEM((NW, cap, 576), H),
            pltpu.VMEM((NW, cap, 576), H),
            pltpu.SMEM(env_slot.shape, jnp.int32),
            pltpu.VMEM(transfer.shape[1:], F),
            pltpu.VMEM(wavefunction.shape[1:], F),
            pltpu.VMEM(pair_ops.shape[1:], H),
            pltpu.SMEM(kept_ranks.shape, jnp.int32),
            dma((7,)),
            pltpu.VMEM((5, cap * NW, 128), F),
            pltpu.VMEM((cap, 64, 128), F),
            pltpu.VMEM((2, cap, 64, 128), H),
            pltpu.VMEM((2, nsec, 64, 128), H),
            pltpu.VMEM((nsec, 64, 128), H),
            pltpu.VMEM((nsec, 64, 128), H),
            pltpu.VMEM((nch, NT, 576), F),
            pltpu.VMEM((5, 384, 128), F),
            pltpu.VMEM((1, 128), F),
            pltpu.VMEM((nsec, 1, 128), F),
            pltpu.VMEM((16, 640), F),
            pltpu.VMEM((1024, 128), F),
            pltpu.VMEM((1664, 128), F),
            pltpu.VMEM((208, 32), H),
            pltpu.VMEM((NW, 256, 128), H),
            pltpu.VMEM((2, NB, 208, 128), H),
            pltpu.VMEM((NW, NP, NB, 128), F),
            pltpu.VMEM((384, 128), F),
            pltpu.VMEM((384, 128), F),
            dma((2, nsec)), dma((2, nsec)), dma((nch,)), dma((nch,)), dma((nsec,)), dma((nsec,)),
        ],
        compiler_params=pltpu.CompilerParams(collective_id=0, has_side_effects=True, vmem_limit_bytes=48 * 2**20),
        name="lanczos",
    )(*(
        pltpu.with_memory_space_constraint(a, pltpu.HBM)
        for a in (
            jnp.swapaxes(left_env[0], 0, 1), jnp.swapaxes(right_env[0], 0, 1), env_slot, transfer[0], wavefunction[0],
            pair_ops[0], kept_ranks)
    ))
    return out[None], en.reshape(1)


def solution(mesh):
    return jax.shard_map(
        body,
        mesh=mesh,
        in_specs=(
            P("chain", "sector", None, None),
            P("chain", "sector", None),
            P("chain", "sector", None, None),
            P("chain", "sector", None, None),
            P("chain", None, None),
            P("chain", None),
            P("chain", "sector"),
        ),
        out_specs=(P("chain", "sector", None, None), P("chain")),
        check_vma=False,
    )
```

```python
import functools

import jax
import jax.numpy as jnp
from jax import lax
from jax.experimental import pallas as pl
from jax.experimental.pallas import tpu as pltpu
from jax.sharding import PartitionSpec as P

F = jnp.float32
H = jnp.bfloat16
NT = 4
NB = 24
NP = 16
NW = 13
MESH = pl.DeviceIdType.MESH


def split(x):
    h = x.astype(H)
    return h, (x - h.astype(F)).astype(H)


def grab(tile, off, t, lane):
    c0, o = off // 128, off % 128
    sh = (32 * t - o) % 128
    a = tile(c0)
    a = pltpu.roll(a, sh, 1) if sh else a
    if o + NB > 128:
        b = tile(c0 + 1)
        b = pltpu.roll(b, sh, 1) if sh else b
        a = jnp.where(lane < 32 * t + 128 - o, a, b)
    return jnp.where((lane >= 32 * t) & (lane < 32 * t + NB), a, 0.0)


def full(x):
    return jnp.sum(jnp.sum(x, axis=0, keepdims=True), axis=1, keepdims=True)


def inverse(n):
    return jnp.where(n > 0, 1.0 / n, 0.0)


def loop(a, b, f):
    def step(j, c):
        f(j)
        return c

    lax.fori_loop(a, b, step, 0)


def total(x):
    return jnp.sum(x, axis=1, keepdims=True)


def weighted(m, a, b):
    acc = None
    for i in range(len(a)):
        s = None
        for j in range(len(b)):
            z = m[i][j] * b[j]
            s = z if s is None else s + z
        s = s * a[i]
        acc = s if acc is None else acc + s
    return acc


def recursion(q, sel):
    pos = {}
    for i in range(4):
        for j in range(i, 4):
            pos[i, j] = pos[j, i] = len(set(pos.values()))
    gram = [[q(pos[i, j]) for j in range(4)] for i in range(4)]
    kept = [[q(64 + pos[i, j]) for j in range(4)] for i in range(4)]
    n0 = q(16)
    al = [q(17 + i) for i in range(3)]
    be = [q(20 + i) for i in range(3)]

    def image(c):
        k = len(c) - 1
        y = [None] * min(k + 2, 4)

        def add(i, z):
            y[i] = z if y[i] is None else y[i] + z

        for j in range(min(k + 1, 3)):
            add(j, al[j] * c[j])
            add(j + 1, be[j] * c[j])
            if j > 0:
                add(j - 1, be[j - 1] * c[j])
        return y

    c = [n0 / jnp.sqrt(total(n0 * n0))]
    cp = []
    b = None
    cs = []
    diag = []
    off = []
    for k in range(4):
        cs.append(c)
        y = image(c)
        g = weighted(gram, c, y)
        if k == 3:
            break
        a = total(g)
        diag.append(a)
        r = []
        for i in range(len(y)):
            z = y[i]
            if i < len(c):
                z = z - a * c[i]
            if i < len(cp):
                z = z - b * cp[i]
            r.append(z)
        b = jnp.sqrt(total(weighted(gram, r, r)))
        off.append(b)
        cp = c
        c = [z / b for z in r]
    norms = [[total(weighted(kept, cs[k], cs[m])) for m in range(4)] for k in range(4)]
    mine = [[total(jnp.where(sel, z, 0.0)) for z in cs[k]] for k in range(4)]
    return cs, g, diag, off, norms, mine


def smallest(d, off):
    ab = [jnp.abs(z) for z in off]
    w2 = [z * z for z in off]
    least = lambda v: jnp.minimum(jnp.minimum(v[0], v[1]), jnp.minimum(v[2], v[3]))
    lo = least([d[0] - ab[0], d[1] - ab[0] - ab[1], d[2] - ab[1] - ab[2], d[3] - ab[2]])
    hi = least(d)
    idx = (lax.broadcasted_iota(jnp.int32, (8, 128), 0) * 128 + lax.broadcasted_iota(jnp.int32, (8, 128), 1) + 1).astype(F)
    for _ in range(2):
        h = (hi - lo) * (1.0 / 1024.0)
        x = lo + h * idx
        p1 = d[0] - x
        p2 = (d[1] - x) * p1 - w2[0]
        p3 = (d[2] - x) * p2 - w2[1] * p1
        p4 = (d[3] - x) * p3 - w2[2] * p2
        below = (p1 > 0) & (p2 > 0) & (p3 > 0) & (p4 > 0)
        x = jnp.where(below, x, lo)
        lo = jnp.max(jnp.max(x, axis=0, keepdims=True), axis=1, keepdims=True)
        hi = lo + h
    e = lo
    for _ in range(3):
        vp, vn, sp, sn = jnp.ones_like(e), d[0] - e, jnp.zeros_like(e), -jnp.ones_like(e)
        for p in range(1, 4):
            z = d[p] - e
            v2 = z * vn - w2[p - 1] * vp
            s2 = z * sn - vn - w2[p - 1] * sp
            vp, vn, sp, sn = vn, v2, sn, s2
        e = e - jnp.where(sn != 0, vn / sn, 0.0)
    return e


def ritz(d, off):
    e = smallest(d, off)
    co = [jnp.ones_like(e), (e - d[0]) / off[0]]
    for p in range(1, 3):
        co.append(((e - d[p]) * co[p] - off[p - 1] * co[p - 1]) / off[p])
    n = jnp.sqrt(co[0] * co[0] + co[1] * co[1] + co[2] * co[2] + co[3] * co[3])
    return e, [z / n for z in co]


def whole(
    entries, nsec, nch,
    left_in, right_in, slot_in, tr_in, x_in, b_in, kept_in,
    out_ref, en_ref,
    left, right, slot_ref, tr, x_ref, b_ref, kept_ref, lsem,
    wide, wire, cat, stage, recv0, recv1, trecv, v_ref, st, strecv0, strecv1, vout,
    tpad, tbd, ebd, b2, c2, mixed, moved, acat,
    ssem, rsem, tssem, trsem, qssem, qrsem,
):
    me = lax.axis_index("sector")
    ch = lax.axis_index("chain")
    cap = left_in.shape[1]
    lane = lax.broadcasted_iota(jnp.int32, (1, 128), 1)
    tl = lane // 32
    loads = [
        pltpu.make_async_copy(a, b, lsem.at[i])
        for i, (a, b) in enumerate((
            (slot_in, slot_ref), (left_in, left), (tr_in, tr), (right_in, right), (b_in, b_ref), (x_in, x_ref), (kept_in, kept_ref)))
    ]
    for c in loads:
        c.start()
    bar = pltpu.get_barrier_semaphore()
    loop(1, nsec, lambda j: pl.semaphore_signal(bar, inc=1, device_id=(ch, lax.rem(me + j, nsec)), device_id_type=MESH))
    loop(1, nch, lambda j: pl.semaphore_signal(bar, inc=1, device_id=(lax.rem(ch + j, nch), me), device_id_type=MESH))
    def pack(side, src, chosen):
        wire[...] = jnp.zeros_like(wire)
        for w in range(NW):
            row8 = src[w].astype(F)
            for c in range(4):
                wide[c, cap * w:cap * w + cap, :] = row8[:, 128 * c:128 * c + 128]
            wide[4, cap * w:cap * w + cap, 0:64] = row8[:, 512:576]
        for s in range(cap):
            for c in range(4):
                wire[s, 13 * c:13 * c + 13, :] = wide[c, pl.ds(s, 13, stride=cap), :]
            lo = wide[4, pl.ds(s, 7, stride=cap), :]
            hi = pltpu.roll(wide[4, pl.ds(s + 7 * cap, 6, stride=cap), :], 64, 1)
            wire[s, 52:59, :] = jnp.where(lane < 64, lo, 0.0)
            wire[s, 52:58, :] = jnp.where(lane < 64, lo[0:6], hi)
        cat[side] = wire[...].astype(H)
        for j in range(nsec):
            stage[side, j] = cat[side, chosen[j]]

    def tcopy(j):
        return pltpu.make_async_remote_copy(
            src_ref=tr, dst_ref=trecv.at[ch], send_sem=tssem.at[j], recv_sem=trsem.at[j],
            device_id=(lax.rem(ch + j, nch), me), device_id_type=MESH)

    def ecopy(side, j):
        return pltpu.make_async_remote_copy(
            src_ref=stage.at[side, j], dst_ref=(recv0, recv1)[side].at[j], send_sem=ssem.at[side, j], recv_sem=rsem.at[side, j],
            device_id=(ch, lax.rem(me + j, nsec)), device_id_type=MESH)

    loads[0].wait()
    chosen = []
    for j in range(nsec):
        h = lax.rem(me + j, nsec)
        s = jnp.int32(0)
        for k in range(NT):
            g = slot_ref[0, h * NT + k]
            s = s + jnp.where(g // cap == me, lax.rem(g, cap), 0)
        chosen.append(s)
    loads[1].wait()
    pack(1, left, chosen)
    loads[2].wait()
    trecv[ch] = tr[...]
    pl.semaphore_wait(bar, nsec + nch - 2)
    loop(1, nch, lambda j: tcopy(j).start())
    loop(1, nsec, lambda j: ecopy(1, j).start())
    loads[3].wait()
    pack(0, right, chosen)
    loop(1, nsec, lambda j: ecopy(0, j).start())
    recv0[0] = stage[0, 0]
    recv1[0] = stage[1, 0]
    loads[4].wait()
    loads[5].wait()
    loads[6].wait()

    bf = b_ref[...].astype(F)
    for q in range(NP):
        off = 16 * q
        a = bf[:, (off // 128) * 128:(off // 128) * 128 + 128]
        sh = (-(off % 128)) % 128
        a = pltpu.roll(a, sh, 1) if sh else a
        tbd[pl.ds(q, NW, stride=NP), :] = jnp.where(lane < 16, a, 0.0)
    bb = tbd[0:208, :]
    b2[...] = (bb + pltpu.roll(bb, 16, 1))[:, :32].astype(H)
    for p in range(NP):
        acc = jnp.zeros((NB, 128), F)
        for t in range(NT):
            acc = acc + grab(lambda c: x_ref[t, :, c * 128:(c + 1) * 128], NB * p, t, lane)
        v_ref[0, pl.ds(p, NB, stride=NP), :] = acc
    x = v_ref[0]
    n0 = jnp.sqrt(full(x * x))
    v_ref[0] = x * inverse(n0)
    loop(1, nch, lambda j: tcopy(j).wait())
    tbd[...] = jnp.zeros_like(tbd)
    for t in range(NT):
        tpad[0:8, 0:576] = trecv[:, t, :]
        for i in range(NB):
            tbd[pl.ds(32 * t + i, 8, stride=128), :] = grab(lambda c: tpad[0:8, c * 128:(c + 1) * 128], NB * i, t, lane)
    row = lax.broadcasted_iota(jnp.int32, (128, 128), 0)
    col = lax.broadcasted_iota(jnp.int32, (128, 128), 1)
    eye = (row == col).astype(F)
    T = [jnp.where(ch > c, tbd[c * 128:(c + 1) * 128, :], eye) for c in range(7)]

    def mm(a, b):
        return jnp.dot(a, b, precision=lax.Precision.HIGHEST, preferred_element_type=F)

    pre = mm(mm(T[6], mm(T[5], T[4])), mm(mm(T[3], T[2]), mm(T[1], T[0])))
    ph, plo = split(pre.T)

    ebd[...] = jnp.zeros_like(ebd)

    def spread(side):
        for t in range(NT):
            o = slot_ref[0, me * NT + t] // cap
            wire[t] = (recv0, recv1)[side][lax.rem(me - o + nsec, nsec)].astype(F)
            tpad[0:7, 0:128] = wire[t, 52:59, :]
            tpad[7:13, 0:128] = pltpu.roll(wire[t, 52:58, :], 64, 1)
            tile = lambda c: wire[t, 13 * c:13 * c + 13, :] if c < 4 else tpad[0:13, 0:128]
            for i in range(NB):
                ebd[pl.ds(32 * t + i, NW, stride=128), :] = grab(tile, NB * i, t, lane)

    def pair_step(k):
        bm = b2[...]
        for l in range(0, NB, 2):
            xx = jnp.concatenate([v_ref[k, 16 * l:16 * l + 16, :], v_ref[k, 16 * l + 16:16 * l + 32, :]], 1)
            h, lo = split(xx)
            o = jnp.dot(bm, jnp.concatenate([h, lo], 0), preferred_element_type=F)
            h, lo = split(o)
            mixed[0, l] = h[:, :128]
            mixed[0, l + 1] = h[:, 128:]
            mixed[1, l] = lo[:, :128]
            mixed[1, l + 1] = lo[:, 128:]

    def right_step():
        for w in range(NW):
            h = mixed[0, :, 16 * w:16 * w + 16, :].reshape(384, 128)
            lo = mixed[1, :, 16 * w:16 * w + 16, :].reshape(384, 128)
            o = jnp.dot(jnp.concatenate([h, lo], 1), c2[w], preferred_element_type=F)
            moved[w] = jnp.swapaxes(o.reshape(NB, NP, 128), 0, 1)

    def left_step(k, a2):
        for q in range(0, NP, 2):
            r = jnp.concatenate([jnp.concatenate([moved[w, q + j] for w in range(NW)], 0) for j in range(2)], 1)
            h = r.astype(H).astype(F)
            o = jnp.dot(a2, jnp.concatenate([h, r - h], 0).astype(H), preferred_element_type=F)
            for j in range(2):
                oj = o[:, 128 * j:128 * j + 128]
                y = jnp.where(tl == 0, oj[0:24], jnp.where(tl == 1, oj[24:48], jnp.where(tl == 2, oj[48:72], oj[72:96])))
                v_ref[k + 1, pl.ds(q + j, NB, stride=NP), :] = y

    pair_step(0)
    loop(1, nsec, lambda j: ecopy(1, j).wait())
    spread(1)
    pp = jnp.concatenate([ph, plo], 0)
    pq = jnp.concatenate([ph, plo, ph], 0)
    for w in range(NW):
        e = ebd[w * 128:(w + 1) * 128, :].astype(H)
        s = jnp.dot(jnp.concatenate([e, e], 1), pp, preferred_element_type=F)
        sh, sl = split(s.T)
        at = jnp.dot(jnp.concatenate([sh, sh, sl], 1), pq, preferred_element_type=F)
        acat[24 * w:24 * w + 24, :] = at[0:24] + at[32:56] + at[64:88] + at[96:120]
    acat[312:384, :] = jnp.zeros((72, 128), F)
    al = acat[...].T
    al = jnp.concatenate([al[32 * t:32 * t + 24] for t in range(NT)], 0)[:, :312].astype(H).astype(F)
    a2 = jnp.concatenate([al, al], 1).astype(H)
    loop(1, nsec, lambda j: ecopy(0, j).wait())
    spread(0)
    for w in range(NW):
        ct = ebd[w * 128:(w + 1) * 128, :].T.astype(H)
        c2[w, 0:128, :] = ct
        c2[w, 128:256, :] = ct
    right_step()

    alphas = []
    betas = []
    for k in range(3):
        if k > 0:
            pair_step(k)
            right_step()
        left_step(k, a2)
        y = v_ref[k + 1]
        a = full(v_ref[k] * y)
        r = y - a * v_ref[k]
        if k > 0:
            r = r - betas[-1] * v_ref[k - 1]
        b = jnp.sqrt(full(r * r))
        alphas.append(a)
        betas.append(b)
        v_ref[k + 1] = r * inverse(b)

    def qcopy(i, j):
        return pltpu.make_async_remote_copy(
            src_ref=st.at[i], dst_ref=(strecv0, strecv1)[i].at[me], send_sem=qssem.at[i, j], recv_sem=qrsem.at[i, j],
            device_id=(ch, lax.rem(me + j, nsec)), device_id_type=MESH)

    def lanes(rows):
        g = jnp.concatenate(rows + [jnp.zeros((128 - len(rows), 128), F)], 0)
        return lax.dot_general(lhs, g, (((1,), (1,)), ((), ())), precision=lax.Precision.HIGHEST, preferred_element_type=F)

    def gathered(ref):
        return jnp.concatenate([ref[:, 0, :], jnp.zeros((128 - nsec, 128), F)], 0).T

    kp = jnp.where(tl == 0, kept_ref[0, 0], jnp.where(tl == 1, kept_ref[0, 1], jnp.where(tl == 2, kept_ref[0, 2], kept_ref[0, 3])))
    keep = lax.rem(lane, 32) < kp
    r8 = lax.broadcasted_iota(jnp.int32, (8, 128), 0)
    lhs = jnp.where(r8 == 0, 1.0, jnp.where((r8 == 1) & keep, 1.0, 0.0))
    s = lanes([jnp.sum(v_ref[i] * v_ref[j], axis=0, keepdims=True) for i in range(4) for j in range(i, 4)])
    s = s[0:1] + pltpu.roll(s[1:2], 64, 1)
    for i, val in enumerate([n0] + alphas + betas):
        s = s + jnp.where(lane == 16 + i, val, 0.0)
    st[0] = s
    loop(1, nsec, lambda j: qcopy(0, j).start())
    strecv0[me] = s
    pair_step(3)
    right_step()
    left_step(3, a2)
    s = lanes([jnp.sum(v_ref[i] * v_ref[4], axis=0, keepdims=True) for i in range(4)])[0:1]
    st[1] = s
    loop(1, nsec, lambda j: qcopy(1, j).start())
    strecv1[me] = s
    for k in range(1, 4):
        for p in range(NP):
            a = v_ref[k, pl.ds(p, NB, stride=NP), :]
            for t in range(NT):
                vout[k - 1, t, :, NB * p:NB * p + NB] = a[:, 32 * t:32 * t + NB]
    loop(1, nsec, lambda j: qcopy(0, j).wait())
    q0 = gathered(strecv0)
    cs, g, diag, off, norms, mine = recursion(lambda i: q0[i:i + 1, :], lane == me)
    loop(1, nsec, lambda j: qcopy(1, j).wait())
    q1 = gathered(strecv1)
    z = cs[3][0] * q1[0:1, :]
    for i in range(1, 4):
        z = z + cs[3][i] * q1[i:i + 1, :]
    diag.append(total(g + z * cs[3][3]))
    e, co = ritz(diag, off)
    en_ref[...] = e
    n2 = None
    for k in range(4):
        for m in range(4):
            z = co[k] * co[m] * norms[k][m]
            n2 = z if n2 is None else n2 + z
    scale = jnp.sqrt(entries / n2)
    f = []
    for i in range(4):
        z = None
        for k in range(i, 4):
            c = co[k] * mine[k][i]
            z = c if z is None else z + c
        f.append(z * scale)
    f[0] = f[0] * inverse(n0)
    column = lax.rem(lax.broadcasted_iota(jnp.int32, (1, NP * NB), 1), NB)
    for t in range(NT):
        y = f[0] * x_ref[t]
        for k in range(1, 4):
            y = y + f[k] * vout[k - 1, t]
        out_ref[t] = jnp.where(column < kept_ref[0, t], y, 0.0)


def body(wavefunction, transfer, left_env, right_env, pair_ops, env_slot, kept_ranks):
    nsec = lax.axis_size("sector")
    nch = lax.axis_size("chain")
    cap = left_env.shape[1]
    entries = float(nsec * NT * NB * NP * NB)
    vmem = pl.BlockSpec(memory_space=pltpu.VMEM)
    hbm = pl.BlockSpec(memory_space=pltpu.HBM)
    dma = pltpu.SemaphoreType.DMA
    out, en = pl.pallas_call(
        functools.partial(whole, entries, nsec, nch),
        out_shape=(jax.ShapeDtypeStruct((NT, NB, NP * NB), F), jax.ShapeDtypeStruct((1, 1), F)),
        in_specs=[hbm] * 7,
        out_specs=(vmem, vmem),
        scratch_shapes=[
            pltpu.VMEM((NW, cap, 576), H),
            pltpu.VMEM((NW, cap, 576), H),
            pltpu.SMEM(env_slot.shape, jnp.int32),
            pltpu.VMEM(transfer.shape[1:], F),
            pltpu.VMEM(wavefunction.shape[1:], F),
            pltpu.VMEM(pair_ops.shape[1:], H),
            pltpu.SMEM(kept_ranks.shape, jnp.int32),
            dma((7,)),
            pltpu.VMEM((5, cap * NW, 128), F),
            pltpu.VMEM((cap, 64, 128), F),
            pltpu.VMEM((2, cap, 64, 128), H),
            pltpu.VMEM((2, nsec, 64, 128), H),
            pltpu.VMEM((nsec, 64, 128), H),
            pltpu.VMEM((nsec, 64, 128), H),
            pltpu.VMEM((nch, NT, 576), F),
            pltpu.VMEM((5, 384, 128), F),
            pltpu.VMEM((2, 1, 128), F),
            pltpu.VMEM((nsec, 1, 128), F),
            pltpu.VMEM((nsec, 1, 128), F),
            pltpu.VMEM((3, NT, NB, NP * NB), F),
            pltpu.VMEM((16, 640), F),
            pltpu.VMEM((1024, 128), F),
            pltpu.VMEM((1664, 128), F),
            pltpu.VMEM((208, 32), H),
            pltpu.VMEM((NW, 256, 128), H),
            pltpu.VMEM((2, NB, 208, 128), H),
            pltpu.VMEM((NW, NP, NB, 128), F),
            pltpu.VMEM((384, 128), F),
            dma((2, nsec)), dma((2, nsec)), dma((nch,)), dma((nch,)), dma((2, nsec)), dma((2, nsec)),
        ],
        compiler_params=pltpu.CompilerParams(collective_id=0, has_side_effects=True, vmem_limit_bytes=48 * 2**20),
        name="lanczos",
    )(*(
        pltpu.with_memory_space_constraint(a, pltpu.HBM)
        for a in (
            jnp.swapaxes(left_env[0], 0, 1), jnp.swapaxes(right_env[0], 0, 1), env_slot, transfer[0], wavefunction[0],
            pair_ops[0], kept_ranks)
    ))
    return out[None], en.reshape(1)


def solution(mesh):
    return jax.shard_map(
        body,
        mesh=mesh,
        in_specs=(
            P("chain", "sector", None, None),
            P("chain", "sector", None),
            P("chain", "sector", None, None),
            P("chain", "sector", None, None),
            P("chain", None, None),
            P("chain", None),
            P("chain", "sector"),
        ),
        out_specs=(P("chain", "sector", None, None), P("chain")),
        check_vma=False,
    )
```

```python
import functools

import jax
import jax.numpy as jnp
from jax import lax
from jax.experimental import pallas as pl
from jax.experimental.pallas import tpu as pltpu
from jax.sharding import PartitionSpec as P

F = jnp.float32
H = jnp.bfloat16
NT = 4
NB = 24
NP = 16
NW = 13
MESH = pl.DeviceIdType.MESH


def split(x):
    h = x.astype(H)
    return h, (x - h.astype(F)).astype(H)


def grab(tile, off, t, lane):
    c0, o = off // 128, off % 128
    sh = (32 * t - o) % 128
    a = tile(c0)
    a = pltpu.roll(a, sh, 1) if sh else a
    if o + NB > 128:
        b = tile(c0 + 1)
        b = pltpu.roll(b, sh, 1) if sh else b
        a = jnp.where(lane < 32 * t + 128 - o, a, b)
    return jnp.where((lane >= 32 * t) & (lane < 32 * t + NB), a, 0.0)


def full(x):
    return jnp.sum(jnp.sum(x, axis=0, keepdims=True), axis=1, keepdims=True)


def inverse(n):
    return jnp.where(n > 0, 1.0 / n, 0.0)


def loop(a, b, f):
    def step(j, c):
        f(j)
        return c

    lax.fori_loop(a, b, step, 0)


def total(x):
    return jnp.sum(x, axis=1, keepdims=True)


def weighted(m, a, b):
    acc = None
    for i in range(len(a)):
        s = None
        for j in range(len(b)):
            z = m[i][j] * b[j]
            s = z if s is None else s + z
        s = s * a[i]
        acc = s if acc is None else acc + s
    return acc


def recursion(q, sel):
    pos = {}
    for i in range(4):
        for j in range(i, 4):
            pos[i, j] = pos[j, i] = len(set(pos.values()))
    gram = [[q(pos[i, j]) for j in range(4)] for i in range(4)]
    kept = [[q(64 + pos[i, j]) for j in range(4)] for i in range(4)]
    n0 = q(16)
    al = [q(17 + i) for i in range(3)]
    be = [q(20 + i) for i in range(3)]

    def image(c):
        k = len(c) - 1
        y = [None] * min(k + 2, 4)

        def add(i, z):
            y[i] = z if y[i] is None else y[i] + z

        for j in range(min(k + 1, 3)):
            add(j, al[j] * c[j])
            add(j + 1, be[j] * c[j])
            if j > 0:
                add(j - 1, be[j - 1] * c[j])
        return y

    c = [n0 / jnp.sqrt(total(n0 * n0))]
    cp = []
    b = None
    cs = []
    diag = []
    off = []
    for k in range(4):
        cs.append(c)
        y = image(c)
        g = weighted(gram, c, y)
        if k == 3:
            break
        a = total(g)
        diag.append(a)
        r = []
        for i in range(len(y)):
            z = y[i]
            if i < len(c):
                z = z - a * c[i]
            if i < len(cp):
                z = z - b * cp[i]
            r.append(z)
        b = jnp.sqrt(total(weighted(gram, r, r)))
        off.append(b)
        cp = c
        c = [z / b for z in r]
    norms = [[total(weighted(kept, cs[k], cs[m])) for m in range(4)] for k in range(4)]
    mine = [[total(jnp.where(sel, z, 0.0)) for z in cs[k]] for k in range(4)]
    return cs, g, diag, off, norms, mine


def smallest(d, off):
    ab = [jnp.abs(z) for z in off]
    w2 = [z * z for z in off]
    least = lambda v: jnp.minimum(jnp.minimum(v[0], v[1]), jnp.minimum(v[2], v[3]))
    lo = least([d[0] - ab[0], d[1] - ab[0] - ab[1], d[2] - ab[1] - ab[2], d[3] - ab[2]])
    hi = least(d)
    idx = (lax.broadcasted_iota(jnp.int32, (8, 128), 0) * 128 + lax.broadcasted_iota(jnp.int32, (8, 128), 1) + 1).astype(F)
    for _ in range(2):
        h = (hi - lo) * (1.0 / 1024.0)
        x = lo + h * idx
        p1 = d[0] - x
        p2 = (d[1] - x) * p1 - w2[0]
        p3 = (d[2] - x) * p2 - w2[1] * p1
        p4 = (d[3] - x) * p3 - w2[2] * p2
        below = (p1 > 0) & (p2 > 0) & (p3 > 0) & (p4 > 0)
        x = jnp.where(below, x, lo)
        lo = jnp.max(jnp.max(x, axis=0, keepdims=True), axis=1, keepdims=True)
        hi = lo + h
    e = lo
    for _ in range(3):
        vp, vn, sp, sn = jnp.ones_like(e), d[0] - e, jnp.zeros_like(e), -jnp.ones_like(e)
        for p in range(1, 4):
            z = d[p] - e
            v2 = z * vn - w2[p - 1] * vp
            s2 = z * sn - vn - w2[p - 1] * sp
            vp, vn, sp, sn = vn, v2, sn, s2
        e = e - jnp.where(sn != 0, vn / sn, 0.0)
    return e


def ritz(d, off):
    e = smallest(d, off)
    co = [jnp.ones_like(e), (e - d[0]) / off[0]]
    for p in range(1, 3):
        co.append(((e - d[p]) * co[p] - off[p - 1] * co[p - 1]) / off[p])
    n = jnp.sqrt(co[0] * co[0] + co[1] * co[1] + co[2] * co[2] + co[3] * co[3])
    return e, [z / n for z in co]


def whole(
    entries, nsec, nch,
    left_in, right_in, slot_in, tr_in, x_in, b_in, kept_in,
    out_ref, en_ref,
    left, right, slot_ref, tr, x_ref, b_ref, kept_ref, lsem,
    wide, wire, cat, stage, recv0, recv1, trecv, v_ref, st, strecv0, strecv1, vout,
    tpad, tbd, ebd, b2, c2, c1, mixed, moved, acat,
    ssem, rsem, tssem, trsem, qssem, qrsem,
):
    me = lax.axis_index("sector")
    ch = lax.axis_index("chain")
    cap = left_in.shape[1]
    lane = lax.broadcasted_iota(jnp.int32, (1, 128), 1)
    tl = lane // 32
    loads = [
        pltpu.make_async_copy(a, b, lsem.at[i])
        for i, (a, b) in enumerate((
            (slot_in, slot_ref), (left_in, left), (tr_in, tr), (right_in, right), (b_in, b_ref), (x_in, x_ref), (kept_in, kept_ref)))
    ]
    for c in loads:
        c.start()
    bar = pltpu.get_barrier_semaphore()
    loop(1, nsec, lambda j: pl.semaphore_signal(bar, inc=1, device_id=(ch, lax.rem(me + j, nsec)), device_id_type=MESH))
    loop(1, nch, lambda j: pl.semaphore_signal(bar, inc=1, device_id=(lax.rem(ch + j, nch), me), device_id_type=MESH))
    def pack(side, src, chosen):
        wire[...] = jnp.zeros_like(wire)
        for w in range(NW):
            row8 = src[w].astype(F)
            for c in range(4):
                wide[c, cap * w:cap * w + cap, :] = row8[:, 128 * c:128 * c + 128]
            wide[4, cap * w:cap * w + cap, 0:64] = row8[:, 512:576]
        for s in range(cap):
            for c in range(4):
                wire[s, 13 * c:13 * c + 13, :] = wide[c, pl.ds(s, 13, stride=cap), :]
            lo = wide[4, pl.ds(s, 7, stride=cap), :]
            hi = pltpu.roll(wide[4, pl.ds(s + 7 * cap, 6, stride=cap), :], 64, 1)
            wire[s, 52:59, :] = jnp.where(lane < 64, lo, 0.0)
            wire[s, 52:58, :] = jnp.where(lane < 64, lo[0:6], hi)
        cat[side] = wire[...].astype(H)
        for j in range(nsec):
            stage[side, j] = cat[side, chosen[j]]

    def tcopy(j):
        return pltpu.make_async_remote_copy(
            src_ref=tr, dst_ref=trecv.at[ch], send_sem=tssem.at[j], recv_sem=trsem.at[j],
            device_id=(lax.rem(ch + j, nch), me), device_id_type=MESH)

    def ecopy(side, j):
        return pltpu.make_async_remote_copy(
            src_ref=stage.at[side, j], dst_ref=(recv0, recv1)[side].at[j], send_sem=ssem.at[side], recv_sem=rsem.at[side],
            device_id=(ch, lax.rem(me + j, nsec)), device_id_type=MESH)

    def everyone(ref, send_sem, recv_sem):
        rows = ref.at[pl.ds(1, nsec - 1)]
        return pltpu.make_async_remote_copy(
            src_ref=rows, dst_ref=rows, send_sem=send_sem, recv_sem=recv_sem,
            device_id=(ch, lax.rem(me + 1, nsec)), device_id_type=MESH)

    loads[0].wait()
    chosen = []
    for j in range(nsec):
        h = lax.rem(me + j, nsec)
        s = jnp.int32(0)
        for k in range(NT):
            g = slot_ref[0, h * NT + k]
            s = s + jnp.where(g // cap == me, lax.rem(g, cap), 0)
        chosen.append(s)
    loads[1].wait()
    pack(1, left, chosen)
    loads[2].wait()
    trecv[ch] = tr[...]
    pl.semaphore_wait(bar, nsec + nch - 2)
    loop(1, nch, lambda j: tcopy(j).start())
    loop(1, nsec, lambda j: ecopy(1, j).start())
    loads[3].wait()
    pack(0, right, chosen)
    loop(1, nsec, lambda j: ecopy(0, j).start())
    recv0[0] = stage[0, 0]
    recv1[0] = stage[1, 0]
    loads[4].wait()
    loads[5].wait()
    loads[6].wait()

    bf = b_ref[...].astype(F)
    for q in range(NP):
        off = 16 * q
        a = bf[:, (off // 128) * 128:(off // 128) * 128 + 128]
        sh = (-(off % 128)) % 128
        a = pltpu.roll(a, sh, 1) if sh else a
        tbd[pl.ds(q, NW, stride=NP), :] = jnp.where(lane < 16, a, 0.0)
    bb = tbd[0:208, :]
    b2[...] = (bb + pltpu.roll(bb, 16, 1))[:, :32].astype(H)
    for p in range(NP):
        acc = jnp.zeros((NB, 128), F)
        for t in range(NT):
            acc = acc + grab(lambda c: x_ref[t, :, c * 128:(c + 1) * 128], NB * p, t, lane)
        v_ref[0, pl.ds(p, NB, stride=NP), :] = acc
    x = v_ref[0]
    n0 = jnp.sqrt(full(x * x))
    v_ref[0] = x * inverse(n0)
    loop(1, nch, lambda j: tcopy(j).wait())
    tbd[...] = jnp.zeros_like(tbd)
    for t in range(NT):
        tpad[0:8, 0:576] = trecv[:, t, :]
        for i in range(NB):
            tbd[pl.ds(32 * t + i, 8, stride=128), :] = grab(lambda c: tpad[0:8, c * 128:(c + 1) * 128], NB * i, t, lane)
    row = lax.broadcasted_iota(jnp.int32, (128, 128), 0)
    col = lax.broadcasted_iota(jnp.int32, (128, 128), 1)
    eye = (row == col).astype(F)
    T = [jnp.where(ch > c, tbd[c * 128:(c + 1) * 128, :], eye) for c in range(7)]

    def mm(a, b):
        return jnp.dot(a, b, precision=lax.Precision.HIGHEST, preferred_element_type=F)

    pre = mm(mm(T[6], mm(T[5], T[4])), mm(mm(T[3], T[2]), mm(T[1], T[0])))
    ph, plo = split(pre.T)

    ebd[...] = jnp.zeros_like(ebd)
    c1[...] = jnp.zeros_like(c1)

    def spread(side):
        for t in range(NT):
            o = slot_ref[0, me * NT + t] // cap
            wire[t] = (recv0, recv1)[side][lax.rem(me - o + nsec, nsec)].astype(F)
            tpad[0:7, 0:128] = wire[t, 52:59, :]
            tpad[7:13, 0:128] = pltpu.roll(wire[t, 52:58, :], 64, 1)
            tile = lambda c: wire[t, 13 * c:13 * c + 13, :] if c < 4 else tpad[0:13, 0:128]
            for i in range(NB):
                ebd[pl.ds(32 * t + i, NW, stride=128), :] = grab(tile, NB * i, t, lane)

    def pair_step(k, parts=2):
        bm = b2[...]
        for l in range(0, NB, 2):
            xx = jnp.concatenate([v_ref[k, 16 * l:16 * l + 16, :], v_ref[k, 16 * l + 16:16 * l + 32, :]], 1)
            h, lo = split(xx)
            o = jnp.dot(bm, jnp.concatenate([h, lo], 0), preferred_element_type=F)
            h, lo = split(o)
            mixed[0, l] = h[:, :128]
            mixed[0, l + 1] = h[:, 128:]
            if parts == 2:
                mixed[1, l] = lo[:, :128]
                mixed[1, l + 1] = lo[:, 128:]

    def right_step():
        for w in range(NW):
            h = mixed[0, :, 16 * w:16 * w + 16, :].reshape(384, 128)
            lo = mixed[1, :, 16 * w:16 * w + 16, :].reshape(384, 128)
            o = jnp.dot(jnp.concatenate([h, lo], 1), c2[w], preferred_element_type=F)
            moved[w] = jnp.swapaxes(o.reshape(NB, NP, 128), 0, 1)

    def right_step_rounded():
        for w in range(0, NW, 2):
            n = min(2, NW - w)
            h = jnp.concatenate([mixed[0, :, 16 * (w + i):16 * (w + i) + 16, :].reshape(384, 128) for i in range(n)], 1)
            o = jnp.dot(h, c1[w // 2, 0:128 * n, 0:128 * n], preferred_element_type=F)
            for i in range(n):
                moved[w + i] = jnp.swapaxes(o[:, 128 * i:128 * i + 128].reshape(NB, NP, 128), 0, 1)

    def left_step(k, a2, parts=2):
        for q in range(0, NP, 2):
            r = jnp.concatenate([jnp.concatenate([moved[w, q + j] for w in range(NW)], 0) for j in range(2)], 1)
            if parts == 2:
                h = r.astype(H).astype(F)
                r = jnp.concatenate([h, r - h], 0)
            o = jnp.dot(a2[:, :312 * parts], r.astype(H), preferred_element_type=F)
            for j in range(2):
                oj = o[:, 128 * j:128 * j + 128]
                y = jnp.where(tl == 0, oj[0:24], jnp.where(tl == 1, oj[24:48], jnp.where(tl == 2, oj[48:72], oj[72:96])))
                v_ref[k + 1, pl.ds(q + j, NB, stride=NP), :] = y

    pair_step(0)
    everyone(recv1, ssem.at[1], rsem.at[1]).wait()
    spread(1)
    pp = jnp.concatenate([ph, plo], 0)
    pq = jnp.concatenate([ph, plo, ph], 0)
    for w in range(NW):
        e = ebd[w * 128:(w + 1) * 128, :].astype(H)
        s = jnp.dot(jnp.concatenate([e, e], 1), pp, preferred_element_type=F)
        sh, sl = split(s.T)
        at = jnp.dot(jnp.concatenate([sh, sh, sl], 1), pq, preferred_element_type=F)
        acat[24 * w:24 * w + 24, :] = at[0:24] + at[32:56] + at[64:88] + at[96:120]
    acat[312:384, :] = jnp.zeros((72, 128), F)
    al = acat[...].T
    al = jnp.concatenate([al[32 * t:32 * t + 24] for t in range(NT)], 0)[:, :312].astype(H).astype(F)
    a2 = jnp.concatenate([al, al], 1).astype(H)
    everyone(recv0, ssem.at[0], rsem.at[0]).wait()
    spread(0)
    for w in range(NW):
        ct = ebd[w * 128:(w + 1) * 128, :].T.astype(H)
        c2[w, 0:128, :] = ct
        c2[w, 128:256, :] = ct
        i = 128 * (w % 2)
        c1[w // 2, i:i + 128, i:i + 128] = ct
    right_step()

    alphas = []
    betas = []
    for k in range(3):
        if k > 0:
            pair_step(k)
            right_step()
        left_step(k, a2)
        y = v_ref[k + 1]
        a = full(v_ref[k] * y)
        r = y - a * v_ref[k]
        if k > 0:
            r = r - betas[-1] * v_ref[k - 1]
        b = jnp.sqrt(full(r * r))
        alphas.append(a)
        betas.append(b)
        v_ref[k + 1] = r * inverse(b)

    def qcopy(i, j):
        return pltpu.make_async_remote_copy(
            src_ref=st.at[i], dst_ref=(strecv0, strecv1)[i].at[j], send_sem=qssem.at[i], recv_sem=qrsem.at[i],
            device_id=(ch, lax.rem(me + j, nsec)), device_id_type=MESH)

    def lanes(rows):
        g = jnp.concatenate(rows + [jnp.zeros((128 - len(rows), 128), F)], 0)
        return lax.dot_general(lhs, g, (((1,), (1,)), ((), ())), precision=lax.Precision.HIGHEST, preferred_element_type=F)

    def gathered(ref):
        return jnp.concatenate([ref[:, 0, :], jnp.zeros((128 - nsec, 128), F)], 0).T

    kp = jnp.where(tl == 0, kept_ref[0, 0], jnp.where(tl == 1, kept_ref[0, 1], jnp.where(tl == 2, kept_ref[0, 2], kept_ref[0, 3])))
    keep = lax.rem(lane, 32) < kp
    r8 = lax.broadcasted_iota(jnp.int32, (8, 128), 0)
    lhs = jnp.where(r8 == 0, 1.0, jnp.where((r8 == 1) & keep, 1.0, 0.0))
    s = lanes([jnp.sum(v_ref[i] * v_ref[j], axis=0, keepdims=True) for i in range(4) for j in range(i, 4)])
    s = s[0:1] + pltpu.roll(s[1:2], 64, 1)
    for i, val in enumerate([n0] + alphas + betas):
        s = s + jnp.where(lane == 16 + i, val, 0.0)
    st[0] = s
    for j in range(1, nsec):
        qcopy(0, j).start()
    strecv0[0] = s
    pair_step(3, 1)
    right_step_rounded()
    left_step(3, a2, 1)
    s = lanes([jnp.sum(v_ref[i] * v_ref[4], axis=0, keepdims=True) for i in range(4)])[0:1]
    st[1] = s
    for j in range(1, nsec):
        qcopy(1, j).start()
    strecv1[0] = s
    for k in range(1, 4):
        for p in range(NP):
            a = v_ref[k, pl.ds(p, NB, stride=NP), :]
            for t in range(NT):
                vout[k - 1, t, :, NB * p:NB * p + NB] = a[:, 32 * t:32 * t + NB]
    everyone(strecv0, qssem.at[0], qrsem.at[0]).wait()
    q0 = gathered(strecv0)
    cs, g, diag, off, norms, mine = recursion(lambda i: q0[i:i + 1, :], lane == 0)
    everyone(strecv1, qssem.at[1], qrsem.at[1]).wait()
    q1 = gathered(strecv1)
    z = cs[3][0] * q1[0:1, :]
    for i in range(1, 4):
        z = z + cs[3][i] * q1[i:i + 1, :]
    diag.append(total(g + z * cs[3][3]))
    e, co = ritz(diag, off)
    en_ref[...] = e
    n2 = None
    for k in range(4):
        for m in range(4):
            z = co[k] * co[m] * norms[k][m]
            n2 = z if n2 is None else n2 + z
    scale = jnp.sqrt(entries / n2)
    f = []
    for i in range(4):
        z = None
        for k in range(i, 4):
            c = co[k] * mine[k][i]
            z = c if z is None else z + c
        f.append(z * scale)
    f[0] = f[0] * inverse(n0)
    column = lax.rem(lax.broadcasted_iota(jnp.int32, (1, NP * NB), 1), NB)
    for t in range(NT):
        y = f[0] * x_ref[t]
        for k in range(1, 4):
            y = y + f[k] * vout[k - 1, t]
        out_ref[t] = jnp.where(column < kept_ref[0, t], y, 0.0)


def body(wavefunction, transfer, left_env, right_env, pair_ops, env_slot, kept_ranks):
    nsec = lax.axis_size("sector")
    nch = lax.axis_size("chain")
    cap = left_env.shape[1]
    entries = float(nsec * NT * NB * NP * NB)
    vmem = pl.BlockSpec(memory_space=pltpu.VMEM)
    hbm = pl.BlockSpec(memory_space=pltpu.HBM)
    dma = pltpu.SemaphoreType.DMA
    out, en = pl.pallas_call(
        functools.partial(whole, entries, nsec, nch),
        out_shape=(jax.ShapeDtypeStruct((NT, NB, NP * NB), F), jax.ShapeDtypeStruct((1, 1), F)),
        in_specs=[hbm] * 7,
        out_specs=(vmem, vmem),
        scratch_shapes=[
            pltpu.VMEM((NW, cap, 576), H),
            pltpu.VMEM((NW, cap, 576), H),
            pltpu.SMEM(env_slot.shape, jnp.int32),
            pltpu.VMEM(transfer.shape[1:], F),
            pltpu.VMEM(wavefunction.shape[1:], F),
            pltpu.VMEM(pair_ops.shape[1:], H),
            pltpu.SMEM(kept_ranks.shape, jnp.int32),
            dma((7,)),
            pltpu.VMEM((5, cap * NW, 128), F),
            pltpu.VMEM((cap, 64, 128), F),
            pltpu.VMEM((2, cap, 64, 128), H),
            pltpu.VMEM((2, nsec, 64, 128), H),
            pltpu.VMEM((nsec, 64, 128), H),
            pltpu.VMEM((nsec, 64, 128), H),
            pltpu.VMEM((nch, NT, 576), F),
            pltpu.VMEM((5, 384, 128), F),
            pltpu.VMEM((2, 1, 128), F),
            pltpu.VMEM((nsec, 1, 128), F),
            pltpu.VMEM((nsec, 1, 128), F),
            pltpu.VMEM((3, NT, NB, NP * NB), F),
            pltpu.VMEM((16, 640), F),
            pltpu.VMEM((1024, 128), F),
            pltpu.VMEM((1664, 128), F),
            pltpu.VMEM((208, 32), H),
            pltpu.VMEM((NW, 256, 128), H),
            pltpu.VMEM(((NW + 1) // 2, 256, 256), H),
            pltpu.VMEM((2, NB, 208, 128), H),
            pltpu.VMEM((NW, NP, NB, 128), F),
            pltpu.VMEM((384, 128), F),
            dma((2,)), dma((2,)), dma((nch,)), dma((nch,)), dma((2,)), dma((2,)),
        ],
        compiler_params=pltpu.CompilerParams(collective_id=0, has_side_effects=True, vmem_limit_bytes=48 * 2**20),
        name="lanczos",
    )(*(
        pltpu.with_memory_space_constraint(a, pltpu.HBM)
        for a in (
            jnp.swapaxes(left_env[0], 0, 1), jnp.swapaxes(right_env[0], 0, 1), env_slot, transfer[0], wavefunction[0],
            pair_ops[0], kept_ranks)
    ))
    return out[None], en.reshape(1)


def solution(mesh):
    return jax.shard_map(
        body,
        mesh=mesh,
        in_specs=(
            P("chain", "sector", None, None),
            P("chain", "sector", None),
            P("chain", "sector", None, None),
            P("chain", "sector", None, None),
            P("chain", None, None),
            P("chain", None),
            P("chain", "sector"),
        ),
        out_specs=(P("chain", "sector", None, None), P("chain")),
        check_vma=False,
    )
```

```python
import functools

import jax
import jax.numpy as jnp
from jax import lax
from jax.experimental import pallas as pl
from jax.experimental.pallas import tpu as pltpu
from jax.sharding import PartitionSpec as P

F = jnp.float32
H = jnp.bfloat16
NT = 4
NB = 24
NP = 16
NW = 13
MESH = pl.DeviceIdType.MESH


def split(x):
    h = x.astype(H)
    return h, (x - h.astype(F)).astype(H)


def grab(tile, off, t, lane):
    c0, o = off // 128, off % 128
    sh = (32 * t - o) % 128
    a = tile(c0)
    a = pltpu.roll(a, sh, 1) if sh else a
    if o + NB > 128:
        b = tile(c0 + 1)
        b = pltpu.roll(b, sh, 1) if sh else b
        a = jnp.where(lane < 32 * t + 128 - o, a, b)
    return jnp.where((lane >= 32 * t) & (lane < 32 * t + NB), a, 0.0)


def full(x):
    return jnp.sum(jnp.sum(x, axis=0, keepdims=True), axis=1, keepdims=True)


def inverse(n):
    return jnp.where(n > 0, 1.0 / n, 0.0)


def loop(a, b, f):
    def step(j, c):
        f(j)
        return c

    lax.fori_loop(a, b, step, 0)


def total(x):
    return jnp.sum(x, axis=1, keepdims=True)


def weighted(m, a, b):
    acc = None
    for i in range(len(a)):
        s = None
        for j in range(len(b)):
            z = m[i][j] * b[j]
            s = z if s is None else s + z
        s = s * a[i]
        acc = s if acc is None else acc + s
    return acc


def recursion(q, sel):
    pos = {}
    for i in range(4):
        for j in range(i, 4):
            pos[i, j] = pos[j, i] = len(set(pos.values()))
    gram = [[q(pos[i, j]) for j in range(4)] for i in range(4)]
    kept = [[q(64 + pos[i, j]) for j in range(4)] for i in range(4)]
    n0 = q(16)
    al = [q(17 + i) for i in range(3)]
    be = [q(20 + i) for i in range(3)]

    def image(c):
        k = len(c) - 1
        y = [None] * min(k + 2, 4)

        def add(i, z):
            y[i] = z if y[i] is None else y[i] + z

        for j in range(min(k + 1, 3)):
            add(j, al[j] * c[j])
            add(j + 1, be[j] * c[j])
            if j > 0:
                add(j - 1, be[j - 1] * c[j])
        return y

    c = [n0 / jnp.sqrt(total(n0 * n0))]
    cp = []
    b = None
    cs = []
    diag = []
    off = []
    for k in range(4):
        cs.append(c)
        y = image(c)
        g = weighted(gram, c, y)
        if k == 3:
            break
        a = total(g)
        diag.append(a)
        r = []
        for i in range(len(y)):
            z = y[i]
            if i < len(c):
                z = z - a * c[i]
            if i < len(cp):
                z = z - b * cp[i]
            r.append(z)
        b = jnp.sqrt(total(weighted(gram, r, r)))
        off.append(b)
        cp = c
        c = [z / b for z in r]
    norms = [[total(weighted(kept, cs[k], cs[m])) for m in range(4)] for k in range(4)]
    mine = [[total(jnp.where(sel, z, 0.0)) for z in cs[k]] for k in range(4)]
    return cs, g, diag, off, norms, mine


def smallest(d, off):
    ab = [jnp.abs(z) for z in off]
    w2 = [z * z for z in off]
    least = lambda v: jnp.minimum(jnp.minimum(v[0], v[1]), jnp.minimum(v[2], v[3]))
    lo = least([d[0] - ab[0], d[1] - ab[0] - ab[1], d[2] - ab[1] - ab[2], d[3] - ab[2]])
    hi = least(d)
    idx = (lax.broadcasted_iota(jnp.int32, (8, 128), 0) * 128 + lax.broadcasted_iota(jnp.int32, (8, 128), 1) + 1).astype(F)
    for _ in range(2):
        h = (hi - lo) * (1.0 / 1024.0)
        x = lo + h * idx
        p1 = d[0] - x
        p2 = (d[1] - x) * p1 - w2[0]
        p3 = (d[2] - x) * p2 - w2[1] * p1
        p4 = (d[3] - x) * p3 - w2[2] * p2
        below = (p1 > 0) & (p2 > 0) & (p3 > 0) & (p4 > 0)
        x = jnp.where(below, x, lo)
        lo = jnp.max(jnp.max(x, axis=0, keepdims=True), axis=1, keepdims=True)
        hi = lo + h
    e = lo
    for _ in range(3):
        vp, vn, sp, sn = jnp.ones_like(e), d[0] - e, jnp.zeros_like(e), -jnp.ones_like(e)
        for p in range(1, 4):
            z = d[p] - e
            v2 = z * vn - w2[p - 1] * vp
            s2 = z * sn - vn - w2[p - 1] * sp
            vp, vn, sp, sn = vn, v2, sn, s2
        e = e - jnp.where(sn != 0, vn / sn, 0.0)
    return e


def ritz(d, off):
    e = smallest(d, off)
    co = [jnp.ones_like(e), (e - d[0]) / off[0]]
    for p in range(1, 3):
        co.append(((e - d[p]) * co[p] - off[p - 1] * co[p - 1]) / off[p])
    n = jnp.sqrt(co[0] * co[0] + co[1] * co[1] + co[2] * co[2] + co[3] * co[3])
    return e, [z / n for z in co]


def whole(
    entries, nsec, nch,
    left_in, right_in, slot_in, tr_in, x_in, b_in, kept_in,
    out_ref, en_ref,
    left, right, slot_ref, tr, x_ref, b_ref, kept_ref, lsem,
    wide, wire, cat, stage, recva, recvb, recvl, trecv, v_ref, st, strecv0, strecv1, vout,
    tpad, tbd, ebd, b2, c2, c1, mixed, moved, acat,
    ssem, rsem, tssem, trsem, qssem, qrsem,
):
    me = lax.axis_index("sector")
    ch = lax.axis_index("chain")
    cap = left_in.shape[1]
    recvs = (recva, recvb, recvl)
    lane = lax.broadcasted_iota(jnp.int32, (1, 128), 1)
    tl = lane // 32
    loads = [
        pltpu.make_async_copy(a, b, lsem.at[i])
        for i, (a, b) in enumerate((
            (slot_in, slot_ref), (left_in, left), (tr_in, tr), (right_in, right), (b_in, b_ref), (x_in, x_ref), (kept_in, kept_ref)))
    ]
    for c in loads:
        c.start()
    bar = pltpu.get_barrier_semaphore()
    loop(1, nsec, lambda j: pl.semaphore_signal(bar, inc=1, device_id=(ch, lax.rem(me + j, nsec)), device_id_type=MESH))
    loop(1, nch, lambda j: pl.semaphore_signal(bar, inc=1, device_id=(lax.rem(ch + j, nch), me), device_id_type=MESH))
    def widen(src):
        for w in range(NW):
            row8 = src[w].astype(F)
            for c in range(4):
                wide[c, cap * w:cap * w + cap, :] = row8[:, 128 * c:128 * c + 128]
            wide[4, cap * w:cap * w + cap, 0:64] = row8[:, 512:576]

    def pack(side, row, first, n):
        half = (n + 1) // 2
        for s in range(cap):
            for c in range(4):
                wire[s, row + n * c:row + n * c + n, :] = wide[c, pl.ds(s + cap * first, n, stride=cap), :]
            lo = wide[4, pl.ds(s + cap * first, half, stride=cap), :]
            hi = pltpu.roll(wide[4, pl.ds(s + cap * (first + half), n - half, stride=cap), :], 64, 1)
            wire[s, row + 4 * n:row + 4 * n + half, :] = jnp.where(lane < 64, lo, 0.0)
            wire[s, row + 4 * n:row + 5 * n - half, :] = jnp.where(lane < 64, lo[0:n - half], hi)

    def place(side, chosen):
        cat[side] = wire[...].astype(H)
        for j in range(nsec):
            stage[side, j] = cat[side, chosen[j]]

    def tcopy(j):
        return pltpu.make_async_remote_copy(
            src_ref=tr, dst_ref=trecv.at[ch], send_sem=tssem.at[j], recv_sem=trsem.at[j],
            device_id=(lax.rem(ch + j, nch), me), device_id_type=MESH)

    def ecopy(part, j):
        src = stage.at[1, j] if part == 2 else stage.at[0, j, pl.ds(32 * part, 32)]
        return pltpu.make_async_remote_copy(
            src_ref=src, dst_ref=recvs[part].at[j], send_sem=ssem.at[part], recv_sem=rsem.at[part],
            device_id=(ch, lax.rem(me + j, nsec)), device_id_type=MESH)

    def everyone(ref, send_sem, recv_sem):
        rows = ref.at[pl.ds(1, nsec - 1)]
        return pltpu.make_async_remote_copy(
            src_ref=rows, dst_ref=rows, send_sem=send_sem, recv_sem=recv_sem,
            device_id=(ch, lax.rem(me + 1, nsec)), device_id_type=MESH)

    loads[0].wait()
    chosen = []
    for j in range(nsec):
        h = lax.rem(me + j, nsec)
        s = jnp.int32(0)
        for k in range(NT):
            g = slot_ref[0, h * NT + k]
            s = s + jnp.where(g // cap == me, lax.rem(g, cap), 0)
        chosen.append(s)
    loads[1].wait()
    wire[...] = jnp.zeros_like(wire)
    widen(left)
    pack(1, 0, 0, NW)
    place(1, chosen)
    loads[2].wait()
    trecv[ch] = tr[...]
    pl.semaphore_wait(bar, nsec + nch - 2)
    loop(1, nch, lambda j: tcopy(j).start())
    loop(1, nsec, lambda j: ecopy(2, j).start())
    loads[3].wait()
    widen(right)
    pack(0, 0, 0, 7)
    pack(0, 32, 7, 6)
    place(0, chosen)
    loop(1, nsec, lambda j: ecopy(0, j).start())
    loop(1, nsec, lambda j: ecopy(1, j).start())
    recvs[0][0] = stage[0, 0, 0:32]
    recvs[1][0] = stage[0, 0, 32:64]
    recvs[2][0] = stage[1, 0]
    loads[4].wait()
    loads[5].wait()
    loads[6].wait()

    bf = b_ref[...].astype(F)
    for q in range(NP):
        off = 16 * q
        a = bf[:, (off // 128) * 128:(off // 128) * 128 + 128]
        sh = (-(off % 128)) % 128
        a = pltpu.roll(a, sh, 1) if sh else a
        tbd[pl.ds(q, NW, stride=NP), :] = jnp.where(lane < 16, a, 0.0)
    bb = tbd[0:208, :]
    b2[...] = (bb + pltpu.roll(bb, 16, 1))[:, :32].astype(H)
    for p in range(NP):
        acc = jnp.zeros((NB, 128), F)
        for t in range(NT):
            acc = acc + grab(lambda c: x_ref[t, :, c * 128:(c + 1) * 128], NB * p, t, lane)
        v_ref[0, pl.ds(p, NB, stride=NP), :] = acc
    x = v_ref[0]
    n0 = jnp.sqrt(full(x * x))
    v_ref[0] = x * inverse(n0)
    loop(1, nch, lambda j: tcopy(j).wait())
    tbd[...] = jnp.zeros_like(tbd)
    for t in range(NT):
        tpad[0:8, 0:576] = trecv[:, t, :]
        for i in range(NB):
            tbd[pl.ds(32 * t + i, 8, stride=128), :] = grab(lambda c: tpad[0:8, c * 128:(c + 1) * 128], NB * i, t, lane)
    row = lax.broadcasted_iota(jnp.int32, (128, 128), 0)
    col = lax.broadcasted_iota(jnp.int32, (128, 128), 1)
    eye = (row == col).astype(F)
    T = [jnp.where(ch > c, tbd[c * 128:(c + 1) * 128, :], eye) for c in range(7)]

    def mm(a, b):
        return jnp.dot(a, b, precision=lax.Precision.HIGHEST, preferred_element_type=F)

    pre = mm(mm(T[6], mm(T[5], T[4])), mm(mm(T[3], T[2]), mm(T[1], T[0])))
    ph, plo = split(pre.T)

    ebd[...] = jnp.zeros_like(ebd)
    c1[...] = jnp.zeros_like(c1)

    def spread(part, first, n):
        half = (n + 1) // 2
        m = recvs[part].shape[1]
        for t in range(NT):
            o = slot_ref[0, me * NT + t] // cap
            wire[t, 0:m] = recvs[part][lax.rem(me - o + nsec, nsec)].astype(F)
            tpad[0:half, 0:128] = wire[t, 4 * n:4 * n + half, :]
            tpad[half:n, 0:128] = pltpu.roll(wire[t, 4 * n:5 * n - half, :], 64, 1)
            tile = lambda c: wire[t, n * c:n * c + n, :] if c < 4 else tpad[0:n, 0:128]
            for i in range(NB):
                ebd[pl.ds(128 * first + 32 * t + i, n, stride=128), :] = grab(tile, NB * i, t, lane)

    def pair_step(k, parts=2):
        bm = b2[...]
        for l in range(0, NB, 2):
            xx = jnp.concatenate([v_ref[k, 16 * l:16 * l + 16, :], v_ref[k, 16 * l + 16:16 * l + 32, :]], 1)
            h, lo = split(xx)
            o = jnp.dot(bm, jnp.concatenate([h, lo], 0), preferred_element_type=F)
            h, lo = split(o)
            mixed[0, l] = h[:, :128]
            mixed[0, l + 1] = h[:, 128:]
            if parts == 2:
                mixed[1, l] = lo[:, :128]
                mixed[1, l + 1] = lo[:, 128:]

    def right_step(first=0, last=NW):
        for w in range(first, last):
            h = mixed[0, :, 16 * w:16 * w + 16, :].reshape(384, 128)
            lo = mixed[1, :, 16 * w:16 * w + 16, :].reshape(384, 128)
            o = jnp.dot(jnp.concatenate([h, lo], 1), c2[w], preferred_element_type=F)
            moved[w] = jnp.swapaxes(o.reshape(NB, NP, 128), 0, 1)

    def right_step_rounded():
        for w in range(0, NW, 2):
            n = min(2, NW - w)
            h = jnp.concatenate([mixed[0, :, 16 * (w + i):16 * (w + i) + 16, :].reshape(384, 128) for i in range(n)], 1)
            o = jnp.dot(h, c1[w // 2, 0:128 * n, 0:128 * n], preferred_element_type=F)
            for i in range(n):
                moved[w + i] = jnp.swapaxes(o[:, 128 * i:128 * i + 128].reshape(NB, NP, 128), 0, 1)

    def left_step(k, a2, parts=2):
        for q in range(0, NP, 2):
            r = jnp.concatenate([jnp.concatenate([moved[w, q + j] for w in range(NW)], 0) for j in range(2)], 1)
            if parts == 2:
                h = r.astype(H).astype(F)
                r = jnp.concatenate([h, r - h], 0)
            o = jnp.dot(a2[:, :312 * parts], r.astype(H), preferred_element_type=F)
            for j in range(2):
                oj = o[:, 128 * j:128 * j + 128]
                y = jnp.where(tl == 0, oj[0:24], jnp.where(tl == 1, oj[24:48], jnp.where(tl == 2, oj[48:72], oj[72:96])))
                v_ref[k + 1, pl.ds(q + j, NB, stride=NP), :] = y

    pair_step(0)
    everyone(recvs[2], ssem.at[2], rsem.at[2]).wait()
    spread(2, 0, NW)
    pp = jnp.concatenate([ph, plo], 0)
    pq = jnp.concatenate([ph, plo, ph], 0)
    for w in range(NW):
        e = ebd[w * 128:(w + 1) * 128, :].astype(H)
        s = jnp.dot(jnp.concatenate([e, e], 1), pp, preferred_element_type=F)
        sh, sl = split(s.T)
        at = jnp.dot(jnp.concatenate([sh, sh, sl], 1), pq, preferred_element_type=F)
        acat[24 * w:24 * w + 24, :] = at[0:24] + at[32:56] + at[64:88] + at[96:120]
    acat[312:384, :] = jnp.zeros((72, 128), F)
    al = acat[...].T
    al = jnp.concatenate([al[32 * t:32 * t + 24] for t in range(NT)], 0)[:, :312].astype(H).astype(F)
    a2 = jnp.concatenate([al, al], 1).astype(H)
    for part, first, last in ((0, 0, 7), (1, 7, NW)):
        everyone(recvs[part], ssem.at[part], rsem.at[part]).wait()
        spread(part, first, last - first)
        for w in range(first, last):
            ct = ebd[w * 128:(w + 1) * 128, :].T.astype(H)
            c2[w, 0:128, :] = ct
            c2[w, 128:256, :] = ct
            i = 128 * (w % 2)
            c1[w // 2, i:i + 128, i:i + 128] = ct
        right_step(first, last)

    alphas = []
    betas = []
    for k in range(3):
        if k == 1:
            pair_step(k)
            right_step()
        if k == 2:
            pair_step(k, 1)
            right_step_rounded()
        left_step(k, a2, 2 if k < 2 else 1)
        y = v_ref[k + 1]
        a = full(v_ref[k] * y)
        r = y - a * v_ref[k]
        if k > 0:
            r = r - betas[-1] * v_ref[k - 1]
        b = jnp.sqrt(full(r * r))
        alphas.append(a)
        betas.append(b)
        v_ref[k + 1] = r * inverse(b)

    def qcopy(i, j):
        return pltpu.make_async_remote_copy(
            src_ref=st.at[i], dst_ref=(strecv0, strecv1)[i].at[j], send_sem=qssem.at[i], recv_sem=qrsem.at[i],
            device_id=(ch, lax.rem(me + j, nsec)), device_id_type=MESH)

    def lanes(rows):
        g = jnp.concatenate(rows + [jnp.zeros((128 - len(rows), 128), F)], 0)
        return lax.dot_general(lhs, g, (((1,), (1,)), ((), ())), precision=lax.Precision.HIGHEST, preferred_element_type=F)

    def gathered(ref):
        return jnp.concatenate([ref[:, 0, :], jnp.zeros((128 - nsec, 128), F)], 0).T

    kp = jnp.where(tl == 0, kept_ref[0, 0], jnp.where(tl == 1, kept_ref[0, 1], jnp.where(tl == 2, kept_ref[0, 2], kept_ref[0, 3])))
    keep = lax.rem(lane, 32) < kp
    r8 = lax.broadcasted_iota(jnp.int32, (8, 128), 0)
    lhs = jnp.where(r8 == 0, 1.0, jnp.where((r8 == 1) & keep, 1.0, 0.0))
    s = lanes([jnp.sum(v_ref[i] * v_ref[j], axis=0, keepdims=True) for i in range(4) for j in range(i, 4)])
    s = s[0:1] + pltpu.roll(s[1:2], 64, 1)
    for i, val in enumerate([n0] + alphas + betas):
        s = s + jnp.where(lane == 16 + i, val, 0.0)
    st[0] = s
    for j in range(1, nsec):
        qcopy(0, j).start()
    strecv0[0] = s
    pair_step(3, 1)
    right_step_rounded()
    left_step(3, a2, 1)
    s = lanes([jnp.sum(v_ref[i] * v_ref[4], axis=0, keepdims=True) for i in range(4)])[0:1]
    st[1] = s
    for j in range(1, nsec):
        qcopy(1, j).start()
    strecv1[0] = s
    for k in range(1, 4):
        for p in range(NP):
            a = v_ref[k, pl.ds(p, NB, stride=NP), :]
            for t in range(NT):
                vout[k - 1, t, :, NB * p:NB * p + NB] = a[:, 32 * t:32 * t + NB]
    everyone(strecv0, qssem.at[0], qrsem.at[0]).wait()
    q0 = gathered(strecv0)
    cs, g, diag, off, norms, mine = recursion(lambda i: q0[i:i + 1, :], lane == 0)
    everyone(strecv1, qssem.at[1], qrsem.at[1]).wait()
    q1 = gathered(strecv1)
    z = cs[3][0] * q1[0:1, :]
    for i in range(1, 4):
        z = z + cs[3][i] * q1[i:i + 1, :]
    diag.append(total(g + z * cs[3][3]))
    e, co = ritz(diag, off)
    en_ref[...] = e
    n2 = None
    for k in range(4):
        for m in range(4):
            z = co[k] * co[m] * norms[k][m]
            n2 = z if n2 is None else n2 + z
    scale = jnp.sqrt(entries / n2)
    f = []
    for i in range(4):
        z = None
        for k in range(i, 4):
            c = co[k] * mine[k][i]
            z = c if z is None else z + c
        f.append(z * scale)
    f[0] = f[0] * inverse(n0)
    column = lax.rem(lax.broadcasted_iota(jnp.int32, (1, NP * NB), 1), NB)
    for t in range(NT):
        y = f[0] * x_ref[t]
        for k in range(1, 4):
            y = y + f[k] * vout[k - 1, t]
        out_ref[t] = jnp.where(column < kept_ref[0, t], y, 0.0)


def body(wavefunction, transfer, left_env, right_env, pair_ops, env_slot, kept_ranks):
    nsec = lax.axis_size("sector")
    nch = lax.axis_size("chain")
    cap = left_env.shape[1]
    entries = float(nsec * NT * NB * NP * NB)
    vmem = pl.BlockSpec(memory_space=pltpu.VMEM)
    hbm = pl.BlockSpec(memory_space=pltpu.HBM)
    dma = pltpu.SemaphoreType.DMA
    out, en = pl.pallas_call(
        functools.partial(whole, entries, nsec, nch),
        out_shape=(jax.ShapeDtypeStruct((NT, NB, NP * NB), F), jax.ShapeDtypeStruct((1, 1), F)),
        in_specs=[hbm] * 7,
        out_specs=(vmem, vmem),
        scratch_shapes=[
            pltpu.VMEM((NW, cap, 576), H),
            pltpu.VMEM((NW, cap, 576), H),
            pltpu.SMEM(env_slot.shape, jnp.int32),
            pltpu.VMEM(transfer.shape[1:], F),
            pltpu.VMEM(wavefunction.shape[1:], F),
            pltpu.VMEM(pair_ops.shape[1:], H),
            pltpu.SMEM(kept_ranks.shape, jnp.int32),
            dma((7,)),
            pltpu.VMEM((5, cap * NW, 128), F),
            pltpu.VMEM((cap, 64, 128), F),
            pltpu.VMEM((2, cap, 64, 128), H),
            pltpu.VMEM((2, nsec, 64, 128), H),
            pltpu.VMEM((nsec, 32, 128), H),
            pltpu.VMEM((nsec, 32, 128), H),
            pltpu.VMEM((nsec, 64, 128), H),
            pltpu.VMEM((nch, NT, 576), F),
            pltpu.VMEM((5, 384, 128), F),
            pltpu.VMEM((2, 1, 128), F),
            pltpu.VMEM((nsec, 1, 128), F),
            pltpu.VMEM((nsec, 1, 128), F),
            pltpu.VMEM((3, NT, NB, NP * NB), F),
            pltpu.VMEM((16, 640), F),
            pltpu.VMEM((1024, 128), F),
            pltpu.VMEM((1664, 128), F),
            pltpu.VMEM((208, 32), H),
            pltpu.VMEM((NW, 256, 128), H),
            pltpu.VMEM(((NW + 1) // 2, 256, 256), H),
            pltpu.VMEM((2, NB, 208, 128), H),
            pltpu.VMEM((NW, NP, NB, 128), F),
            pltpu.VMEM((384, 128), F),
            dma((3,)), dma((3,)), dma((nch,)), dma((nch,)), dma((2,)), dma((2,)),
        ],
        compiler_params=pltpu.CompilerParams(collective_id=0, has_side_effects=True, vmem_limit_bytes=48 * 2**20),
        name="lanczos",
    )(*(
        pltpu.with_memory_space_constraint(a, pltpu.HBM)
        for a in (
            jnp.swapaxes(left_env[0], 0, 1), jnp.swapaxes(right_env[0], 0, 1), env_slot, transfer[0], wavefunction[0],
            pair_ops[0], kept_ranks)
    ))
    return out[None], en.reshape(1)


def solution(mesh):
    return jax.shard_map(
        body,
        mesh=mesh,
        in_specs=(
            P("chain", "sector", None, None),
            P("chain", "sector", None),
            P("chain", "sector", None, None),
            P("chain", "sector", None, None),
            P("chain", None, None),
            P("chain", None),
            P("chain", "sector"),
        ),
        out_specs=(P("chain", "sector", None, None), P("chain")),
        check_vma=False,
    )
```

```python
import functools

import jax
import jax.numpy as jnp
from jax import lax
from jax.experimental import pallas as pl
from jax.experimental.pallas import tpu as pltpu
from jax.sharding import PartitionSpec as P

F = jnp.float32
H = jnp.bfloat16
NT = 4
NB = 24
NP = 16
NW = 13
NY = 4
MESH = pl.DeviceIdType.MESH


def split(x):
    h = x.astype(H)
    return h, (x - h.astype(F)).astype(H)


def grab(tile, off, t, lane):
    c0, o = off // 128, off % 128
    sh = (32 * t - o) % 128
    a = tile(c0)
    a = pltpu.roll(a, sh, 1) if sh else a
    if o + NB > 128:
        b = tile(c0 + 1)
        b = pltpu.roll(b, sh, 1) if sh else b
        a = jnp.where(lane < 32 * t + 128 - o, a, b)
    return jnp.where((lane >= 32 * t) & (lane < 32 * t + NB), a, 0.0)


def full(x):
    return jnp.sum(jnp.sum(x, axis=0, keepdims=True), axis=1, keepdims=True)


def inverse(n):
    return jnp.where(n > 0, 1.0 / n, 0.0)


def loop(a, b, f):
    def step(j, c):
        f(j)
        return c

    lax.fori_loop(a, b, step, 0)


def total(x):
    return jnp.sum(x, axis=1, keepdims=True)


def weighted(m, a, b):
    acc = None
    for i in range(len(a)):
        s = None
        for j in range(len(b)):
            z = m[i][j] * b[j]
            s = z if s is None else s + z
        s = s * a[i]
        acc = s if acc is None else acc + s
    return acc


def recursion(q, sel):
    pos = {}
    for i in range(4):
        for j in range(i, 4):
            pos[i, j] = pos[j, i] = len(set(pos.values()))
    gram = [[q(pos[i, j]) for j in range(4)] for i in range(4)]
    kept = [[q(64 + pos[i, j]) for j in range(4)] for i in range(4)]
    n0 = q(16)
    al = [q(17 + i) for i in range(3)]
    be = [q(20 + i) for i in range(3)]

    def image(c):
        k = len(c) - 1
        y = [None] * min(k + 2, 4)

        def add(i, z):
            y[i] = z if y[i] is None else y[i] + z

        for j in range(min(k + 1, 3)):
            add(j, al[j] * c[j])
            add(j + 1, be[j] * c[j])
            if j > 0:
                add(j - 1, be[j - 1] * c[j])
        return y

    c = [n0 / jnp.sqrt(total(n0 * n0))]
    cp = []
    b = None
    cs = []
    diag = []
    off = []
    for k in range(4):
        cs.append(c)
        y = image(c)
        g = weighted(gram, c, y)
        if k == 3:
            break
        a = total(g)
        diag.append(a)
        r = []
        for i in range(len(y)):
            z = y[i]
            if i < len(c):
                z = z - a * c[i]
            if i < len(cp):
                z = z - b * cp[i]
            r.append(z)
        b = jnp.sqrt(total(weighted(gram, r, r)))
        off.append(b)
        cp = c
        c = [z / b for z in r]
    norms = [[total(weighted(kept, cs[k], cs[m])) for m in range(4)] for k in range(4)]
    mine = [[total(jnp.where(sel, z, 0.0)) for z in cs[k]] for k in range(4)]
    return cs, g, diag, off, norms, mine


def smallest(d, off):
    ab = [jnp.abs(z) for z in off]
    w2 = [z * z for z in off]
    least = lambda v: jnp.minimum(jnp.minimum(v[0], v[1]), jnp.minimum(v[2], v[3]))
    lo = least([d[0] - ab[0], d[1] - ab[0] - ab[1], d[2] - ab[1] - ab[2], d[3] - ab[2]])
    hi = least(d)
    idx = (lax.broadcasted_iota(jnp.int32, (8, 128), 0) * 128 + lax.broadcasted_iota(jnp.int32, (8, 128), 1) + 1).astype(F)
    for _ in range(2):
        h = (hi - lo) * (1.0 / 1024.0)
        x = lo + h * idx
        p1 = d[0] - x
        p2 = (d[1] - x) * p1 - w2[0]
        p3 = (d[2] - x) * p2 - w2[1] * p1
        p4 = (d[3] - x) * p3 - w2[2] * p2
        below = (p1 > 0) & (p2 > 0) & (p3 > 0) & (p4 > 0)
        x = jnp.where(below, x, lo)
        lo = jnp.max(jnp.max(x, axis=0, keepdims=True), axis=1, keepdims=True)
        hi = lo + h
    e = lo
    for _ in range(3):
        vp, vn, sp, sn = jnp.ones_like(e), d[0] - e, jnp.zeros_like(e), -jnp.ones_like(e)
        for p in range(1, 4):
            z = d[p] - e
            v2 = z * vn - w2[p - 1] * vp
            s2 = z * sn - vn - w2[p - 1] * sp
            vp, vn, sp, sn = vn, v2, sn, s2
        e = e - jnp.where(sn != 0, vn / sn, 0.0)
    return e


def ritz(d, off):
    e = smallest(d, off)
    co = [jnp.ones_like(e), (e - d[0]) / off[0]]
    for p in range(1, 3):
        co.append(((e - d[p]) * co[p] - off[p - 1] * co[p - 1]) / off[p])
    n = jnp.sqrt(co[0] * co[0] + co[1] * co[1] + co[2] * co[2] + co[3] * co[3])
    return e, [z / n for z in co]


def whole(
    entries, nsec, nch,
    left_in, right_in, slot_in, tr_in, x_in, b_in, kept_in,
    out_ref, en_ref,
    left, right, slot_ref, tr, x_ref, b_ref, kept_ref, lsem,
    wide, wire, cat, stage, recva, recvb, recvl, trecv, v_ref, st, strecv0, strecv1, vout,
    tpad, tbd, ebd, b2, c2, c1, mixed, moved, acat,
    ssem, rsem, tssem, trsem, qssem, qrsem,
):
    me = lax.axis_index("sector")
    ch = lax.axis_index("chain")
    cap = left_in.shape[1]
    recvs = (recva, recvb, recvl)
    my_z, my_y = me // NY, lax.rem(me, NY)
    nz = nsec // NY

    def peer(j):
        return lax.rem(my_z + j // NY, nz) * NY + lax.rem(my_y + j % NY, NY)

    def row_of(o):
        return lax.rem(my_z - o // NY + nz, nz) * NY + lax.rem(my_y - lax.rem(o, NY) + NY, NY)

    far = sorted(range(1, nsec), key=lambda j: -min(j // NY, nz - j // NY) - min(j % NY, NY - j % NY))
    order = sorted(range(1, nsec), key=lambda j: ((0, 2, 1, 3)[j % NY], -min(j // NY, nz - j // NY)))
    lane = lax.broadcasted_iota(jnp.int32, (1, 128), 1)
    tl = lane // 32
    loads = [
        pltpu.make_async_copy(a, b, lsem.at[i])
        for i, (a, b) in enumerate((
            (slot_in, slot_ref), (left_in, left), (tr_in, tr), (right_in, right), (b_in, b_ref), (x_in, x_ref), (kept_in, kept_ref)))
    ]
    for c in loads:
        c.start()
    bar = pltpu.get_barrier_semaphore()
    loop(1, nsec, lambda j: pl.semaphore_signal(bar, inc=1, device_id=(ch, lax.rem(me + j, nsec)), device_id_type=MESH))
    loop(1, nch, lambda j: pl.semaphore_signal(bar, inc=1, device_id=(lax.rem(ch + j, nch), me), device_id_type=MESH))
    def widen(src):
        for w in range(NW):
            row8 = src[w].astype(F)
            for c in range(4):
                wide[c, cap * w:cap * w + cap, :] = row8[:, 128 * c:128 * c + 128]
            wide[4, cap * w:cap * w + cap, 0:64] = row8[:, 512:576]

    def pack(side, row, first, n):
        half = (n + 1) // 2
        for s in range(cap):
            for c in range(4):
                wire[s, row + n * c:row + n * c + n, :] = wide[c, pl.ds(s + cap * first, n, stride=cap), :]
            lo = wide[4, pl.ds(s + cap * first, half, stride=cap), :]
            hi = pltpu.roll(wide[4, pl.ds(s + cap * (first + half), n - half, stride=cap), :], 64, 1)
            wire[s, row + 4 * n:row + 4 * n + half, :] = jnp.where(lane < 64, lo, 0.0)
            wire[s, row + 4 * n:row + 5 * n - half, :] = jnp.where(lane < 64, lo[0:n - half], hi)

    def place(side, chosen):
        cat[side] = wire[...].astype(H)
        for j in range(nsec):
            stage[side, j] = cat[side, chosen[j]]

    def tcopy(j):
        return pltpu.make_async_remote_copy(
            src_ref=tr, dst_ref=trecv.at[ch], send_sem=tssem.at[j], recv_sem=trsem.at[j],
            device_id=(lax.rem(ch + j, nch), me), device_id_type=MESH)

    def ecopy(part, j):
        src = stage.at[1, j] if part == 2 else stage.at[0, j, pl.ds(48 * part, 48 - 32 * part)]
        return pltpu.make_async_remote_copy(
            src_ref=src, dst_ref=recvs[part].at[j], send_sem=ssem.at[part], recv_sem=rsem.at[part],
            device_id=(ch, peer(j)), device_id_type=MESH)

    def everyone(ref, send_sem, recv_sem):
        rows = ref.at[pl.ds(1, nsec - 1)]
        return pltpu.make_async_remote_copy(
            src_ref=rows, dst_ref=rows, send_sem=send_sem, recv_sem=recv_sem,
            device_id=(ch, lax.rem(me + 1, nsec)), device_id_type=MESH)

    loads[0].wait()
    chosen = []
    for j in range(nsec):
        h = peer(j)
        s = jnp.int32(0)
        for k in range(NT):
            g = slot_ref[0, h * NT + k]
            s = s + jnp.where(g // cap == me, lax.rem(g, cap), 0)
        chosen.append(s)
    loads[1].wait()
    wire[...] = jnp.zeros_like(wire)
    widen(left)
    pack(1, 0, 0, NW)
    place(1, chosen)
    loads[2].wait()
    trecv[ch] = tr[...]
    pl.semaphore_wait(bar, nsec + nch - 2)
    loop(1, nch, lambda j: tcopy(j).start())
    for j in order:
        ecopy(2, j).start()
    loads[3].wait()
    widen(right)
    pack(0, 0, 0, 10)
    pack(0, 48, 10, 3)
    place(0, chosen)
    for j in order:
        ecopy(0, j).start()
    for j in order:
        ecopy(1, j).start()
    recvs[0][0] = stage[0, 0, 0:48]
    recvs[1][0] = stage[0, 0, 48:64]
    recvs[2][0] = stage[1, 0]
    loads[4].wait()
    loads[5].wait()
    loads[6].wait()

    bf = b_ref[...].astype(F)
    for q in range(NP):
        off = 16 * q
        a = bf[:, (off // 128) * 128:(off // 128) * 128 + 128]
        sh = (-(off % 128)) % 128
        a = pltpu.roll(a, sh, 1) if sh else a
        tbd[pl.ds(q, NW, stride=NP), :] = jnp.where(lane < 16, a, 0.0)
    bb = tbd[0:208, :]
    b2[...] = (bb + pltpu.roll(bb, 16, 1))[:, :32].astype(H)
    for p in range(NP):
        acc = jnp.zeros((NB, 128), F)
        for t in range(NT):
            acc = acc + grab(lambda c: x_ref[t, :, c * 128:(c + 1) * 128], NB * p, t, lane)
        v_ref[0, pl.ds(p, NB, stride=NP), :] = acc
    x = v_ref[0]
    n0 = jnp.sqrt(full(x * x))
    v_ref[0] = x * inverse(n0)
    loop(1, nch, lambda j: tcopy(j).wait())
    tbd[...] = jnp.zeros_like(tbd)
    for t in range(NT):
        tpad[0:8, 0:576] = trecv[:, t, :]
        for i in range(NB):
            tbd[pl.ds(32 * t + i, 8, stride=128), :] = grab(lambda c: tpad[0:8, c * 128:(c + 1) * 128], NB * i, t, lane)
    row = lax.broadcasted_iota(jnp.int32, (128, 128), 0)
    col = lax.broadcasted_iota(jnp.int32, (128, 128), 1)
    eye = (row == col).astype(F)
    T = [jnp.where(ch > c, tbd[c * 128:(c + 1) * 128, :], eye) for c in range(7)]

    def mm(a, b):
        return jnp.dot(a, b, precision=lax.Precision.HIGHEST, preferred_element_type=F)

    pre = mm(mm(T[6], mm(T[5], T[4])), mm(mm(T[3], T[2]), mm(T[1], T[0])))
    ph, plo = split(pre.T)

    ebd[...] = jnp.zeros_like(ebd)
    c1[...] = jnp.zeros_like(c1)

    def spread(part, first, n):
        half = (n + 1) // 2
        m = recvs[part].shape[1]
        for t in range(NT):
            o = slot_ref[0, me * NT + t] // cap
            wire[t, 0:m] = recvs[part][row_of(o)].astype(F)
            tpad[0:half, 0:128] = wire[t, 4 * n:4 * n + half, :]
            tpad[half:n, 0:128] = pltpu.roll(wire[t, 4 * n:5 * n - half, :], 64, 1)
            tile = lambda c: wire[t, n * c:n * c + n, :] if c < 4 else tpad[0:n, 0:128]
            for i in range(NB):
                ebd[pl.ds(128 * first + 32 * t + i, n, stride=128), :] = grab(tile, NB * i, t, lane)

    def pair_step(k, parts=2):
        bm = b2[...]
        for l in range(0, NB, 2):
            xx = jnp.concatenate([v_ref[k, 16 * l:16 * l + 16, :], v_ref[k, 16 * l + 16:16 * l + 32, :]], 1)
            h, lo = split(xx)
            o = jnp.dot(bm, jnp.concatenate([h, lo], 0), preferred_element_type=F)
            h, lo = split(o)
            mixed[0, l] = h[:, :128]
            mixed[0, l + 1] = h[:, 128:]
            if parts == 2:
                mixed[1, l] = lo[:, :128]
                mixed[1, l + 1] = lo[:, 128:]

    def right_step(first=0, last=NW):
        for w in range(first, last):
            h = mixed[0, :, 16 * w:16 * w + 16, :].reshape(384, 128)
            lo = mixed[1, :, 16 * w:16 * w + 16, :].reshape(384, 128)
            o = jnp.dot(jnp.concatenate([h, lo], 1), c2[w], preferred_element_type=F)
            moved[w] = jnp.swapaxes(o.reshape(NB, NP, 128), 0, 1)

    def right_step_rounded():
        for w in range(0, NW, 2):
            n = min(2, NW - w)
            h = jnp.concatenate([mixed[0, :, 16 * (w + i):16 * (w + i) + 16, :].reshape(384, 128) for i in range(n)], 1)
            o = jnp.dot(h, c1[w // 2, 0:128 * n, 0:128 * n], preferred_element_type=F)
            for i in range(n):
                moved[w + i] = jnp.swapaxes(o[:, 128 * i:128 * i + 128].reshape(NB, NP, 128), 0, 1)

    def left_step(k, a2, parts=2):
        for q in range(0, NP, 2):
            r = jnp.concatenate([jnp.concatenate([moved[w, q + j] for w in range(NW)], 0) for j in range(2)], 1)
            if parts == 2:
                h = r.astype(H).astype(F)
                r = jnp.concatenate([h, r - h], 0)
            o = jnp.dot(a2[:, :312 * parts], r.astype(H), preferred_element_type=F)
            for j in range(2):
                oj = o[:, 128 * j:128 * j + 128]
                y = jnp.where(tl == 0, oj[0:24], jnp.where(tl == 1, oj[24:48], jnp.where(tl == 2, oj[48:72], oj[72:96])))
                v_ref[k + 1, pl.ds(q + j, NB, stride=NP), :] = y

    pair_step(0)
    everyone(recvs[2], ssem.at[2], rsem.at[2]).wait()
    spread(2, 0, NW)
    pp = jnp.concatenate([ph, plo], 0)
    pq = jnp.concatenate([ph, plo, ph], 0)
    for w in range(NW):
        e = ebd[w * 128:(w + 1) * 128, :].astype(H)
        s = jnp.dot(jnp.concatenate([e, e], 1), pp, preferred_element_type=F)
        sh, sl = split(s.T)
        at = jnp.dot(jnp.concatenate([sh, sh, sl], 1), pq, preferred_element_type=F)
        acat[24 * w:24 * w + 24, :] = at[0:24] + at[32:56] + at[64:88] + at[96:120]
    acat[312:384, :] = jnp.zeros((72, 128), F)
    al = acat[...].T
    al = jnp.concatenate([al[32 * t:32 * t + 24] for t in range(NT)], 0)[:, :312].astype(H).astype(F)
    a2 = jnp.concatenate([al, al], 1).astype(H)
    for part, first, last in ((0, 0, 10), (1, 10, NW)):
        everyone(recvs[part], ssem.at[part], rsem.at[part]).wait()
        spread(part, first, last - first)
        for w in range(first, last):
            ct = ebd[w * 128:(w + 1) * 128, :].T.astype(H)
            c2[w, 0:128, :] = ct
            c2[w, 128:256, :] = ct
            i = 128 * (w % 2)
            c1[w // 2, i:i + 128, i:i + 128] = ct
        right_step(first, last)

    alphas = []
    betas = []
    for k in range(3):
        if k == 1:
            pair_step(k)
            right_step()
        if k == 2:
            pair_step(k, 1)
            right_step_rounded()
        left_step(k, a2, 2 if k < 2 else 1)
        y = v_ref[k + 1]
        a = full(v_ref[k] * y)
        r = y - a * v_ref[k]
        if k > 0:
            r = r - betas[-1] * v_ref[k - 1]
        b = jnp.sqrt(full(r * r))
        alphas.append(a)
        betas.append(b)
        v_ref[k + 1] = r * inverse(b)

    def qcopy(i, j):
        return pltpu.make_async_remote_copy(
            src_ref=st.at[i], dst_ref=(strecv0, strecv1)[i].at[j], send_sem=qssem.at[i], recv_sem=qrsem.at[i],
            device_id=(ch, peer(j)), device_id_type=MESH)

    def lanes(rows):
        g = jnp.concatenate(rows + [jnp.zeros((128 - len(rows), 128), F)], 0)
        return lax.dot_general(lhs, g, (((1,), (1,)), ((), ())), precision=lax.Precision.HIGHEST, preferred_element_type=F)

    def gathered(ref):
        return jnp.concatenate([ref[:, 0, :], jnp.zeros((128 - nsec, 128), F)], 0).T

    kp = jnp.where(tl == 0, kept_ref[0, 0], jnp.where(tl == 1, kept_ref[0, 1], jnp.where(tl == 2, kept_ref[0, 2], kept_ref[0, 3])))
    keep = lax.rem(lane, 32) < kp
    r8 = lax.broadcasted_iota(jnp.int32, (8, 128), 0)
    lhs = jnp.where(r8 == 0, 1.0, jnp.where((r8 == 1) & keep, 1.0, 0.0))
    s = lanes([jnp.sum(v_ref[i] * v_ref[j], axis=0, keepdims=True) for i in range(4) for j in range(i, 4)])
    s = s[0:1] + pltpu.roll(s[1:2], 64, 1)
    for i, val in enumerate([n0] + alphas + betas):
        s = s + jnp.where(lane == 16 + i, val, 0.0)
    st[0] = s
    for j in far:
        qcopy(0, j).start()
    strecv0[0] = s
    pair_step(3, 1)
    right_step_rounded()
    left_step(3, a2, 1)
    s = lanes([jnp.sum(v_ref[i] * v_ref[4], axis=0, keepdims=True) for i in range(4)])[0:1]
    st[1] = s
    for j in far:
        qcopy(1, j).start()
    strecv1[0] = s
    for k in range(1, 4):
        for p in range(NP):
            a = v_ref[k, pl.ds(p, NB, stride=NP), :]
            for t in range(NT):
                vout[k - 1, t, :, NB * p:NB * p + NB] = a[:, 32 * t:32 * t + NB]
    everyone(strecv0, qssem.at[0], qrsem.at[0]).wait()
    q0 = gathered(strecv0)
    cs, g, diag, off, norms, mine = recursion(lambda i: q0[i:i + 1, :], lane == 0)
    everyone(strecv1, qssem.at[1], qrsem.at[1]).wait()
    q1 = gathered(strecv1)
    z = cs[3][0] * q1[0:1, :]
    for i in range(1, 4):
        z = z + cs[3][i] * q1[i:i + 1, :]
    diag.append(total(g + z * cs[3][3]))
    e, co = ritz(diag, off)
    en_ref[...] = e
    n2 = None
    for k in range(4):
        for m in range(4):
            z = co[k] * co[m] * norms[k][m]
            n2 = z if n2 is None else n2 + z
    scale = jnp.sqrt(entries / n2)
    f = []
    for i in range(4):
        z = None
        for k in range(i, 4):
            c = co[k] * mine[k][i]
            z = c if z is None else z + c
        f.append(z * scale)
    f[0] = f[0] * inverse(n0)
    column = lax.rem(lax.broadcasted_iota(jnp.int32, (1, NP * NB), 1), NB)
    for t in range(NT):
        y = f[0] * x_ref[t]
        for k in range(1, 4):
            y = y + f[k] * vout[k - 1, t]
        out_ref[t] = jnp.where(column < kept_ref[0, t], y, 0.0)


def body(wavefunction, transfer, left_env, right_env, pair_ops, env_slot, kept_ranks):
    nsec = lax.axis_size("sector")
    nch = lax.axis_size("chain")
    cap = left_env.shape[1]
    entries = float(nsec * NT * NB * NP * NB)
    vmem = pl.BlockSpec(memory_space=pltpu.VMEM)
    hbm = pl.BlockSpec(memory_space=pltpu.HBM)
    dma = pltpu.SemaphoreType.DMA
    out, en = pl.pallas_call(
        functools.partial(whole, entries, nsec, nch),
        out_shape=(jax.ShapeDtypeStruct((NT, NB, NP * NB), F), jax.ShapeDtypeStruct((1, 1), F)),
        in_specs=[hbm] * 7,
        out_specs=(vmem, vmem),
        scratch_shapes=[
            pltpu.VMEM((NW, cap, 576), H),
            pltpu.VMEM((NW, cap, 576), H),
            pltpu.SMEM(env_slot.shape, jnp.int32),
            pltpu.VMEM(transfer.shape[1:], F),
            pltpu.VMEM(wavefunction.shape[1:], F),
            pltpu.VMEM(pair_ops.shape[1:], H),
            pltpu.SMEM(kept_ranks.shape, jnp.int32),
            dma((7,)),
            pltpu.VMEM((5, cap * NW, 128), F),
            pltpu.VMEM((cap, 64, 128), F),
            pltpu.VMEM((2, cap, 64, 128), H),
            pltpu.VMEM((2, nsec, 64, 128), H),
            pltpu.VMEM((nsec, 48, 128), H),
            pltpu.VMEM((nsec, 16, 128), H),
            pltpu.VMEM((nsec, 64, 128), H),
            pltpu.VMEM((nch, NT, 576), F),
            pltpu.VMEM((5, 384, 128), F),
            pltpu.VMEM((2, 1, 128), F),
            pltpu.VMEM((nsec, 1, 128), F),
            pltpu.VMEM((nsec, 1, 128), F),
            pltpu.VMEM((3, NT, NB, NP * NB), F),
            pltpu.VMEM((16, 640), F),
            pltpu.VMEM((1024, 128), F),
            pltpu.VMEM((1664, 128), F),
            pltpu.VMEM((208, 32), H),
            pltpu.VMEM((NW, 256, 128), H),
            pltpu.VMEM(((NW + 1) // 2, 256, 256), H),
            pltpu.VMEM((2, NB, 208, 128), H),
            pltpu.VMEM((NW, NP, NB, 128), F),
            pltpu.VMEM((384, 128), F),
            dma((3,)), dma((3,)), dma((nch,)), dma((nch,)), dma((2,)), dma((2,)),
        ],
        compiler_params=pltpu.CompilerParams(collective_id=0, has_side_effects=True, vmem_limit_bytes=48 * 2**20),
        name="lanczos",
    )(*(
        pltpu.with_memory_space_constraint(a, pltpu.HBM)
        for a in (
            jnp.swapaxes(left_env[0], 0, 1), jnp.swapaxes(right_env[0], 0, 1), env_slot, transfer[0], wavefunction[0],
            pair_ops[0], kept_ranks)
    ))
    return out[None], en.reshape(1)


def solution(mesh):
    return jax.shard_map(
        body,
        mesh=mesh,
        in_specs=(
            P("chain", "sector", None, None),
            P("chain", "sector", None),
            P("chain", "sector", None, None),
            P("chain", "sector", None, None),
            P("chain", None, None),
            P("chain", None),
            P("chain", "sector"),
        ),
        out_specs=(P("chain", "sector", None, None), P("chain")),
        check_vma=False,
    )
```

```python
import functools

import jax
import jax.numpy as jnp
from jax import lax
from jax.experimental import pallas as pl
from jax.experimental.pallas import tpu as pltpu
from jax.sharding import PartitionSpec as P

F = jnp.float32
H = jnp.bfloat16
NT = 4
NB = 24
NP = 16
NW = 13
NY = 4
MESH = pl.DeviceIdType.MESH


def split(x):
    h = x.astype(H)
    return h, (x - h.astype(F)).astype(H)


def grab(tile, off, t, lane):
    c0, o = off // 128, off % 128
    sh = (32 * t - o) % 128
    a = tile(c0)
    a = pltpu.roll(a, sh, 1) if sh else a
    if o + NB > 128:
        b = tile(c0 + 1)
        b = pltpu.roll(b, sh, 1) if sh else b
        a = jnp.where(lane < 32 * t + 128 - o, a, b)
    return jnp.where((lane >= 32 * t) & (lane < 32 * t + NB), a, 0.0)


def full(x):
    return jnp.sum(jnp.sum(x, axis=0, keepdims=True), axis=1, keepdims=True)


def inverse(n):
    return jnp.where(n > 0, 1.0 / n, 0.0)


def loop(a, b, f):
    def step(j, c):
        f(j)
        return c

    lax.fori_loop(a, b, step, 0)


def total(x):
    return jnp.sum(x, axis=1, keepdims=True)


def weighted(m, a, b):
    acc = None
    for i in range(len(a)):
        s = None
        for j in range(len(b)):
            z = m[i][j] * b[j]
            s = z if s is None else s + z
        s = s * a[i]
        acc = s if acc is None else acc + s
    return acc


def recursion(q, sel):
    pos = {}
    for i in range(4):
        for j in range(i, 4):
            pos[i, j] = pos[j, i] = len(set(pos.values()))
    gram = [[q(pos[i, j]) for j in range(4)] for i in range(4)]
    kept = [[q(64 + pos[i, j]) for j in range(4)] for i in range(4)]
    n0 = q(16)
    al = [q(17 + i) for i in range(3)]
    be = [q(20 + i) for i in range(3)]

    def image(c):
        k = len(c) - 1
        y = [None] * min(k + 2, 4)

        def add(i, z):
            y[i] = z if y[i] is None else y[i] + z

        for j in range(min(k + 1, 3)):
            add(j, al[j] * c[j])
            add(j + 1, be[j] * c[j])
            if j > 0:
                add(j - 1, be[j - 1] * c[j])
        return y

    c = [n0 / jnp.sqrt(total(n0 * n0))]
    cp = []
    b = None
    cs = []
    diag = []
    off = []
    for k in range(4):
        cs.append(c)
        y = image(c)
        g = weighted(gram, c, y)
        if k == 3:
            break
        a = total(g)
        diag.append(a)
        r = []
        for i in range(len(y)):
            z = y[i]
            if i < len(c):
                z = z - a * c[i]
            if i < len(cp):
                z = z - b * cp[i]
            r.append(z)
        b = jnp.sqrt(total(weighted(gram, r, r)))
        off.append(b)
        cp = c
        c = [z / b for z in r]
    norms = [[total(weighted(kept, cs[k], cs[m])) for m in range(4)] for k in range(4)]
    mine = [[total(jnp.where(sel, z, 0.0)) for z in cs[k]] for k in range(4)]
    return cs, g, diag, off, norms, mine


def smallest(d, off):
    ab = [jnp.abs(z) for z in off]
    w2 = [z * z for z in off]
    least = lambda v: jnp.minimum(jnp.minimum(v[0], v[1]), jnp.minimum(v[2], v[3]))
    lo = least([d[0] - ab[0], d[1] - ab[0] - ab[1], d[2] - ab[1] - ab[2], d[3] - ab[2]])
    hi = least(d)
    idx = (lax.broadcasted_iota(jnp.int32, (8, 128), 0) * 128 + lax.broadcasted_iota(jnp.int32, (8, 128), 1) + 1).astype(F)
    for _ in range(2):
        h = (hi - lo) * (1.0 / 1024.0)
        x = lo + h * idx
        p1 = d[0] - x
        p2 = (d[1] - x) * p1 - w2[0]
        p3 = (d[2] - x) * p2 - w2[1] * p1
        p4 = (d[3] - x) * p3 - w2[2] * p2
        below = (p1 > 0) & (p2 > 0) & (p3 > 0) & (p4 > 0)
        x = jnp.where(below, x, lo)
        lo = jnp.max(jnp.max(x, axis=0, keepdims=True), axis=1, keepdims=True)
        hi = lo + h
    e = lo
    for _ in range(3):
        vp, vn, sp, sn = jnp.ones_like(e), d[0] - e, jnp.zeros_like(e), -jnp.ones_like(e)
        for p in range(1, 4):
            z = d[p] - e
            v2 = z * vn - w2[p - 1] * vp
            s2 = z * sn - vn - w2[p - 1] * sp
            vp, vn, sp, sn = vn, v2, sn, s2
        e = e - jnp.where(sn != 0, vn / sn, 0.0)
    return e


def ritz(d, off):
    e = smallest(d, off)
    co = [jnp.ones_like(e), (e - d[0]) / off[0]]
    for p in range(1, 3):
        co.append(((e - d[p]) * co[p] - off[p - 1] * co[p - 1]) / off[p])
    n = jnp.sqrt(co[0] * co[0] + co[1] * co[1] + co[2] * co[2] + co[3] * co[3])
    return e, [z / n for z in co]


def whole(
    entries, nsec, nch,
    left_in, right_in, slot_in, tr_in, x_in, b_in, kept_in,
    out_ref, en_ref,
    left, right, slot_ref, tr, x_ref, b_ref, kept_ref, lsem,
    wide, wire, cat, stage, recva, recvb, recvl, trecv, v_ref, st, strecv0, strecv1, vout,
    tpad, tbd, ebd, b2, c2, c1, mixed, moved, acat,
    ssem, rsem, tssem, trsem, qssem, qrsem,
):
    me = lax.axis_index("sector")
    ch = lax.axis_index("chain")
    cap = left_in.shape[1]
    recvs = (recva, recvb, recvl)
    my_z, my_y = me // NY, lax.rem(me, NY)
    nz = nsec // NY

    def peer(j):
        return lax.rem(my_z + j // NY, nz) * NY + lax.rem(my_y + j % NY, NY)

    def row_of(o):
        return lax.rem(my_z - o // NY + nz, nz) * NY + lax.rem(my_y - lax.rem(o, NY) + NY, NY)

    far = sorted(range(1, nsec), key=lambda j: -min(j // NY, nz - j // NY) - min(j % NY, NY - j % NY))
    order = sorted(range(1, nsec), key=lambda j: ((0, 2, 1, 3)[j % NY], -min(j // NY, nz - j // NY)))
    lane = lax.broadcasted_iota(jnp.int32, (1, 128), 1)
    tl = lane // 32
    loads = [
        pltpu.make_async_copy(a, b, lsem.at[i])
        for i, (a, b) in enumerate((
            (slot_in, slot_ref), (left_in, left), (tr_in, tr), (right_in, right), (b_in, b_ref), (x_in, x_ref), (kept_in, kept_ref)))
    ]
    for c in loads:
        c.start()
    bar = pltpu.get_barrier_semaphore()
    loop(1, nsec, lambda j: pl.semaphore_signal(bar, inc=1, device_id=(ch, lax.rem(me + j, nsec)), device_id_type=MESH))
    loop(1, nch, lambda j: pl.semaphore_signal(bar, inc=1, device_id=(lax.rem(ch + j, nch), me), device_id_type=MESH))
    def widen(src):
        for w in range(NW):
            row8 = src[w].astype(F)
            for c in range(4):
                wide[c, cap * w:cap * w + cap, :] = row8[:, 128 * c:128 * c + 128]
            wide[4, cap * w:cap * w + cap, 0:64] = row8[:, 512:576]

    def pack(side, row, first, n):
        half = (n + 1) // 2
        for s in range(cap):
            for c in range(4):
                wire[s, row + n * c:row + n * c + n, :] = wide[c, pl.ds(s + cap * first, n, stride=cap), :]
            lo = wide[4, pl.ds(s + cap * first, half, stride=cap), :]
            hi = pltpu.roll(wide[4, pl.ds(s + cap * (first + half), n - half, stride=cap), :], 64, 1)
            wire[s, row + 4 * n:row + 4 * n + half, :] = jnp.where(lane < 64, lo, 0.0)
            wire[s, row + 4 * n:row + 5 * n - half, :] = jnp.where(lane < 64, lo[0:n - half], hi)

    def place(side, chosen):
        cat[side] = wire[...].astype(H)
        for j in range(nsec):
            stage[side, j] = cat[side, chosen[j]]

    def tcopy(j):
        return pltpu.make_async_remote_copy(
            src_ref=tr, dst_ref=trecv.at[ch], send_sem=tssem.at[j], recv_sem=trsem.at[j],
            device_id=(lax.rem(ch + j, nch), me), device_id_type=MESH)

    def ecopy(part, j):
        src = stage.at[1, j] if part == 2 else stage.at[0, j, pl.ds(48 * part, 48 - 32 * part)]
        return pltpu.make_async_remote_copy(
            src_ref=src, dst_ref=recvs[part].at[j], send_sem=ssem.at[part], recv_sem=rsem.at[part],
            device_id=(ch, peer(j)), device_id_type=MESH)

    def everyone(ref, send_sem, recv_sem):
        rows = ref.at[pl.ds(1, nsec - 1)]
        return pltpu.make_async_remote_copy(
            src_ref=rows, dst_ref=rows, send_sem=send_sem, recv_sem=recv_sem,
            device_id=(ch, lax.rem(me + 1, nsec)), device_id_type=MESH)

    loads[0].wait()
    chosen = []
    for j in range(nsec):
        h = peer(j)
        s = jnp.int32(0)
        for k in range(NT):
            g = slot_ref[0, h * NT + k]
            s = s + jnp.where(g // cap == me, lax.rem(g, cap), 0)
        chosen.append(s)
    loads[1].wait()
    wire[...] = jnp.zeros_like(wire)
    widen(left)
    pack(1, 0, 0, NW)
    place(1, chosen)
    pl.semaphore_wait(bar, nsec + nch - 2)
    for j in order:
        ecopy(2, j).start()
    loads[2].wait()
    trecv[ch] = tr[...]
    loop(1, nch, lambda j: tcopy(j).start())
    loads[3].wait()
    widen(right)
    pack(0, 0, 0, 10)
    pack(0, 48, 10, 3)
    place(0, chosen)
    for j in order:
        ecopy(0, j).start()
    for j in order:
        ecopy(1, j).start()
    recvs[0][0] = stage[0, 0, 0:48]
    recvs[1][0] = stage[0, 0, 48:64]
    recvs[2][0] = stage[1, 0]
    loads[4].wait()
    loads[5].wait()
    loads[6].wait()

    bf = b_ref[...].astype(F)
    for q in range(NP):
        off = 16 * q
        a = bf[:, (off // 128) * 128:(off // 128) * 128 + 128]
        sh = (-(off % 128)) % 128
        a = pltpu.roll(a, sh, 1) if sh else a
        tbd[pl.ds(q, NW, stride=NP), :] = jnp.where(lane < 16, a, 0.0)
    bb = tbd[0:208, :]
    b2[...] = (bb + pltpu.roll(bb, 16, 1))[:, :32].astype(H)
    for p in range(NP):
        acc = jnp.zeros((NB, 128), F)
        for t in range(NT):
            acc = acc + grab(lambda c: x_ref[t, :, c * 128:(c + 1) * 128], NB * p, t, lane)
        v_ref[0, pl.ds(p, NB, stride=NP), :] = acc
    x = v_ref[0]
    n0 = jnp.sqrt(full(x * x))
    v_ref[0] = x * inverse(n0)
    loop(1, nch, lambda j: tcopy(j).wait())
    tbd[...] = jnp.zeros_like(tbd)
    for t in range(NT):
        tpad[0:8, 0:576] = trecv[:, t, :]
        for i in range(NB):
            tbd[pl.ds(32 * t + i, 8, stride=128), :] = grab(lambda c: tpad[0:8, c * 128:(c + 1) * 128], NB * i, t, lane)
    row = lax.broadcasted_iota(jnp.int32, (128, 128), 0)
    col = lax.broadcasted_iota(jnp.int32, (128, 128), 1)
    eye = (row == col).astype(F)
    T = [jnp.where(ch > c, tbd[c * 128:(c + 1) * 128, :], eye) for c in range(7)]

    def mm(a, b):
        return jnp.dot(a, b, precision=lax.Precision.HIGHEST, preferred_element_type=F)

    pre = mm(mm(T[6], mm(T[5], T[4])), mm(mm(T[3], T[2]), mm(T[1], T[0])))
    ph, plo = split(pre.T)

    ebd[...] = jnp.zeros_like(ebd)
    c1[...] = jnp.zeros_like(c1)

    def spread(part, first, n):
        half = (n + 1) // 2
        m = recvs[part].shape[1]
        for t in range(NT):
            o = slot_ref[0, me * NT + t] // cap
            wire[t, 0:m] = recvs[part][row_of(o)].astype(F)
            tpad[0:half, 0:128] = wire[t, 4 * n:4 * n + half, :]
            tpad[half:n, 0:128] = pltpu.roll(wire[t, 4 * n:5 * n - half, :], 64, 1)
            tile = lambda c: wire[t, n * c:n * c + n, :] if c < 4 else tpad[0:n, 0:128]
            for i in range(NB):
                ebd[pl.ds(128 * first + 32 * t + i, n, stride=128), :] = grab(tile, NB * i, t, lane)

    def pair_step(k, parts=2):
        bm = b2[...]
        for l in range(0, NB, 2):
            xx = jnp.concatenate([v_ref[k, 16 * l:16 * l + 16, :], v_ref[k, 16 * l + 16:16 * l + 32, :]], 1)
            h, lo = split(xx)
            o = jnp.dot(bm, jnp.concatenate([h, lo], 0), preferred_element_type=F)
            h, lo = split(o)
            mixed[0, l] = h[:, :128]
            mixed[0, l + 1] = h[:, 128:]
            if parts == 2:
                mixed[1, l] = lo[:, :128]
                mixed[1, l + 1] = lo[:, 128:]

    def right_step(first=0, last=NW):
        for w in range(first, last):
            h = mixed[0, :, 16 * w:16 * w + 16, :].reshape(384, 128)
            lo = mixed[1, :, 16 * w:16 * w + 16, :].reshape(384, 128)
            o = jnp.dot(jnp.concatenate([h, lo], 1), c2[w], preferred_element_type=F)
            moved[w] = jnp.swapaxes(o.reshape(NB, NP, 128), 0, 1)

    def right_step_rounded():
        for w in range(0, NW, 2):
            n = min(2, NW - w)
            h = jnp.concatenate([mixed[0, :, 16 * (w + i):16 * (w + i) + 16, :].reshape(384, 128) for i in range(n)], 1)
            o = jnp.dot(h, c1[w // 2, 0:128 * n, 0:128 * n], preferred_element_type=F)
            for i in range(n):
                moved[w + i] = jnp.swapaxes(o[:, 128 * i:128 * i + 128].reshape(NB, NP, 128), 0, 1)

    def left_step(k, a2, parts=2):
        for q in range(0, NP, 2):
            r = jnp.concatenate([jnp.concatenate([moved[w, q + j] for w in range(NW)], 0) for j in range(2)], 1)
            if parts == 2:
                h = r.astype(H).astype(F)
                r = jnp.concatenate([h, r - h], 0)
            o = jnp.dot(a2[:, :312 * parts], r.astype(H), preferred_element_type=F)
            for j in range(2):
                oj = o[:, 128 * j:128 * j + 128]
                y = jnp.where(tl == 0, oj[0:24], jnp.where(tl == 1, oj[24:48], jnp.where(tl == 2, oj[48:72], oj[72:96])))
                v_ref[k + 1, pl.ds(q + j, NB, stride=NP), :] = y

    pair_step(0)
    everyone(recvs[2], ssem.at[2], rsem.at[2]).wait()
    spread(2, 0, NW)
    pp = jnp.concatenate([ph, plo], 0)
    pq = jnp.concatenate([ph, plo, ph], 0)
    for w in range(NW):
        e = ebd[w * 128:(w + 1) * 128, :].astype(H)
        s = jnp.dot(jnp.concatenate([e, e], 1), pp, preferred_element_type=F)
        sh, sl = split(s.T)
        at = jnp.dot(jnp.concatenate([sh, sh, sl], 1), pq, preferred_element_type=F)
        acat[24 * w:24 * w + 24, :] = at[0:24] + at[32:56] + at[64:88] + at[96:120]
    acat[312:384, :] = jnp.zeros((72, 128), F)
    al = acat[...].T
    al = jnp.concatenate([al[32 * t:32 * t + 24] for t in range(NT)], 0)[:, :312].astype(H).astype(F)
    a2 = jnp.concatenate([al, al], 1).astype(H)
    for part, first, last in ((0, 0, 10), (1, 10, NW)):
        everyone(recvs[part], ssem.at[part], rsem.at[part]).wait()
        spread(part, first, last - first)
        for w in range(first, last):
            ct = ebd[w * 128:(w + 1) * 128, :].T.astype(H)
            c2[w, 0:128, :] = ct
            c2[w, 128:256, :] = ct
            i = 128 * (w % 2)
            c1[w // 2, i:i + 128, i:i + 128] = ct
        right_step(first, last)

    alphas = []
    betas = []
    for k in range(3):
        if k > 0:
            pair_step(k, 1)
            right_step_rounded()
        left_step(k, a2, 2 if k < 2 else 1)
        y = v_ref[k + 1]
        a = full(v_ref[k] * y)
        r = y - a * v_ref[k]
        if k > 0:
            r = r - betas[-1] * v_ref[k - 1]
        b = jnp.sqrt(full(r * r))
        alphas.append(a)
        betas.append(b)
        v_ref[k + 1] = r * inverse(b)

    def qcopy(i, j):
        return pltpu.make_async_remote_copy(
            src_ref=st.at[i], dst_ref=(strecv0, strecv1)[i].at[j], send_sem=qssem.at[i], recv_sem=qrsem.at[i],
            device_id=(ch, peer(j)), device_id_type=MESH)

    def lanes(rows):
        g = jnp.concatenate(rows + [jnp.zeros((128 - len(rows), 128), F)], 0)
        return lax.dot_general(lhs, g, (((1,), (1,)), ((), ())), precision=lax.Precision.HIGHEST, preferred_element_type=F)

    def gathered(ref):
        return jnp.concatenate([ref[:, 0, :], jnp.zeros((128 - nsec, 128), F)], 0).T

    kp = jnp.where(tl == 0, kept_ref[0, 0], jnp.where(tl == 1, kept_ref[0, 1], jnp.where(tl == 2, kept_ref[0, 2], kept_ref[0, 3])))
    keep = lax.rem(lane, 32) < kp
    r8 = lax.broadcasted_iota(jnp.int32, (8, 128), 0)
    lhs = jnp.where(r8 == 0, 1.0, jnp.where((r8 == 1) & keep, 1.0, 0.0))
    s = lanes([jnp.sum(v_ref[i] * v_ref[j], axis=0, keepdims=True) for i in range(4) for j in range(i, 4)])
    s = s[0:1] + pltpu.roll(s[1:2], 64, 1)
    for i, val in enumerate([n0] + alphas + betas):
        s = s + jnp.where(lane == 16 + i, val, 0.0)
    st[0] = s
    for j in far:
        qcopy(0, j).start()
    strecv0[0] = s
    pair_step(3, 1)
    right_step_rounded()
    left_step(3, a2, 1)
    s = jnp.zeros((1, 128), F)
    for i in range(4):
        s = s + jnp.where(lane == i, full(v_ref[i] * v_ref[4]), 0.0)
    st[1] = s
    for j in far:
        qcopy(1, j).start()
    strecv1[0] = s
    for k in range(1, 4):
        for p in range(NP):
            a = v_ref[k, pl.ds(p, NB, stride=NP), :]
            for t in range(NT):
                vout[k - 1, t, :, NB * p:NB * p + NB] = a[:, 32 * t:32 * t + NB]
    everyone(strecv0, qssem.at[0], qrsem.at[0]).wait()
    q0 = gathered(strecv0)
    cs, g, diag, off, norms, mine = recursion(lambda i: q0[i:i + 1, :], lane == 0)
    everyone(strecv1, qssem.at[1], qrsem.at[1]).wait()
    q1 = gathered(strecv1)
    z = cs[3][0] * q1[0:1, :]
    for i in range(1, 4):
        z = z + cs[3][i] * q1[i:i + 1, :]
    diag.append(total(g + z * cs[3][3]))
    e, co = ritz(diag, off)
    en_ref[...] = e
    n2 = None
    for k in range(4):
        for m in range(4):
            z = co[k] * co[m] * norms[k][m]
            n2 = z if n2 is None else n2 + z
    scale = jnp.sqrt(entries / n2)
    f = []
    for i in range(4):
        z = None
        for k in range(i, 4):
            c = co[k] * mine[k][i]
            z = c if z is None else z + c
        f.append(z * scale)
    f[0] = f[0] * inverse(n0)
    column = lax.rem(lax.broadcasted_iota(jnp.int32, (1, NP * NB), 1), NB)
    for t in range(NT):
        y = f[0] * x_ref[t]
        for k in range(1, 4):
            y = y + f[k] * vout[k - 1, t]
        out_ref[t] = jnp.where(column < kept_ref[0, t], y, 0.0)


def body(wavefunction, transfer, left_env, right_env, pair_ops, env_slot, kept_ranks):
    nsec = lax.axis_size("sector")
    nch = lax.axis_size("chain")
    cap = left_env.shape[1]
    entries = float(nsec * NT * NB * NP * NB)
    vmem = pl.BlockSpec(memory_space=pltpu.VMEM)
    hbm = pl.BlockSpec(memory_space=pltpu.HBM)
    dma = pltpu.SemaphoreType.DMA
    out, en = pl.pallas_call(
        functools.partial(whole, entries, nsec, nch),
        out_shape=(jax.ShapeDtypeStruct((NT, NB, NP * NB), F), jax.ShapeDtypeStruct((1, 1), F)),
        in_specs=[hbm] * 7,
        out_specs=(vmem, vmem),
        scratch_shapes=[
            pltpu.VMEM((NW, cap, 576), H),
            pltpu.VMEM((NW, cap, 576), H),
            pltpu.SMEM(env_slot.shape, jnp.int32),
            pltpu.VMEM(transfer.shape[1:], F),
            pltpu.VMEM(wavefunction.shape[1:], F),
            pltpu.VMEM(pair_ops.shape[1:], H),
            pltpu.SMEM(kept_ranks.shape, jnp.int32),
            dma((7,)),
            pltpu.VMEM((5, cap * NW, 128), F),
            pltpu.VMEM((cap, 64, 128), F),
            pltpu.VMEM((2, cap, 64, 128), H),
            pltpu.VMEM((2, nsec, 64, 128), H),
            pltpu.VMEM((nsec, 48, 128), H),
            pltpu.VMEM((nsec, 16, 128), H),
            pltpu.VMEM((nsec, 64, 128), H),
            pltpu.VMEM((nch, NT, 576), F),
            pltpu.VMEM((5, 384, 128), F),
            pltpu.VMEM((2, 1, 128), F),
            pltpu.VMEM((nsec, 1, 128), F),
            pltpu.VMEM((nsec, 1, 128), F),
            pltpu.VMEM((3, NT, NB, NP * NB), F),
            pltpu.VMEM((16, 640), F),
            pltpu.VMEM((1024, 128), F),
            pltpu.VMEM((1664, 128), F),
            pltpu.VMEM((208, 32), H),
            pltpu.VMEM((NW, 256, 128), H),
            pltpu.VMEM(((NW + 1) // 2, 256, 256), H),
            pltpu.VMEM((2, NB, 208, 128), H),
            pltpu.VMEM((NW, NP, NB, 128), F),
            pltpu.VMEM((384, 128), F),
            dma((3,)), dma((3,)), dma((nch,)), dma((nch,)), dma((2,)), dma((2,)),
        ],
        compiler_params=pltpu.CompilerParams(collective_id=0, has_side_effects=True, vmem_limit_bytes=48 * 2**20),
        name="lanczos",
    )(*(
        pltpu.with_memory_space_constraint(a, pltpu.HBM)
        for a in (
            jnp.swapaxes(left_env[0], 0, 1), jnp.swapaxes(right_env[0], 0, 1), env_slot, transfer[0], wavefunction[0],
            pair_ops[0], kept_ranks)
    ))
    return out[None], en.reshape(1)


def solution(mesh):
    return jax.shard_map(
        body,
        mesh=mesh,
        in_specs=(
            P("chain", "sector", None, None),
            P("chain", "sector", None),
            P("chain", "sector", None, None),
            P("chain", "sector", None, None),
            P("chain", None, None),
            P("chain", None),
            P("chain", "sector"),
        ),
        out_specs=(P("chain", "sector", None, None), P("chain")),
        check_vma=False,
    )
```

```python
import functools

import jax
import jax.numpy as jnp
from jax import lax
from jax.experimental import pallas as pl
from jax.experimental.pallas import tpu as pltpu
from jax.sharding import PartitionSpec as P

F = jnp.float32
H = jnp.bfloat16
NT = 4
NB = 24
NP = 16
NW = 13
NY = 4
MESH = pl.DeviceIdType.MESH


def split(x):
    h = x.astype(H)
    return h, (x - h.astype(F)).astype(H)


def grab(tile, off, t, lane):
    c0, o = off // 128, off % 128
    sh = (32 * t - o) % 128
    a = tile(c0)
    a = pltpu.roll(a, sh, 1) if sh else a
    if o + NB > 128:
        b = tile(c0 + 1)
        b = pltpu.roll(b, sh, 1) if sh else b
        a = jnp.where(lane < 32 * t + 128 - o, a, b)
    return jnp.where((lane >= 32 * t) & (lane < 32 * t + NB), a, 0.0)


def full(x):
    return jnp.sum(jnp.sum(x, axis=0, keepdims=True), axis=1, keepdims=True)


def inverse(n):
    return jnp.where(n > 0, 1.0 / n, 0.0)


def loop(a, b, f):
    def step(j, c):
        f(j)
        return c

    lax.fori_loop(a, b, step, 0)


def total(x):
    return jnp.sum(x, axis=1, keepdims=True)


def weighted(m, a, b):
    acc = None
    for i in range(len(a)):
        s = None
        for j in range(len(b)):
            z = m[i][j] * b[j]
            s = z if s is None else s + z
        s = s * a[i]
        acc = s if acc is None else acc + s
    return acc


def recursion(q, sel):
    pos = {}
    for i in range(4):
        for j in range(i, 4):
            pos[i, j] = pos[j, i] = len(set(pos.values()))
    gram = [[q(pos[i, j]) for j in range(4)] for i in range(4)]
    kept = [[q(64 + pos[i, j]) for j in range(4)] for i in range(4)]
    n0 = q(16)
    al = [q(17 + i) for i in range(3)]
    be = [q(20 + i) for i in range(3)]

    def image(c):
        k = len(c) - 1
        y = [None] * min(k + 2, 4)

        def add(i, z):
            y[i] = z if y[i] is None else y[i] + z

        for j in range(min(k + 1, 3)):
            add(j, al[j] * c[j])
            add(j + 1, be[j] * c[j])
            if j > 0:
                add(j - 1, be[j - 1] * c[j])
        return y

    c = [n0 / jnp.sqrt(total(n0 * n0))]
    cp = []
    b = None
    cs = []
    diag = []
    off = []
    for k in range(4):
        cs.append(c)
        y = image(c)
        g = weighted(gram, c, y)
        if k == 3:
            break
        a = total(g)
        diag.append(a)
        r = []
        for i in range(len(y)):
            z = y[i]
            if i < len(c):
                z = z - a * c[i]
            if i < len(cp):
                z = z - b * cp[i]
            r.append(z)
        b = jnp.sqrt(total(weighted(gram, r, r)))
        off.append(b)
        cp = c
        c = [z / b for z in r]
    norms = [[total(weighted(kept, cs[k], cs[m])) for m in range(4)] for k in range(4)]
    mine = [[total(jnp.where(sel, z, 0.0)) for z in cs[k]] for k in range(4)]
    return cs, g, diag, off, norms, mine


def smallest(d, off):
    ab = [jnp.abs(z) for z in off]
    w2 = [z * z for z in off]
    least = lambda v: jnp.minimum(jnp.minimum(v[0], v[1]), jnp.minimum(v[2], v[3]))
    lo = least([d[0] - ab[0], d[1] - ab[0] - ab[1], d[2] - ab[1] - ab[2], d[3] - ab[2]])
    hi = least(d)
    idx = (lax.broadcasted_iota(jnp.int32, (8, 128), 0) * 128 + lax.broadcasted_iota(jnp.int32, (8, 128), 1) + 1).astype(F)
    for _ in range(2):
        h = (hi - lo) * (1.0 / 1024.0)
        x = lo + h * idx
        p1 = d[0] - x
        p2 = (d[1] - x) * p1 - w2[0]
        p3 = (d[2] - x) * p2 - w2[1] * p1
        p4 = (d[3] - x) * p3 - w2[2] * p2
        below = (p1 > 0) & (p2 > 0) & (p3 > 0) & (p4 > 0)
        x = jnp.where(below, x, lo)
        lo = jnp.max(jnp.max(x, axis=0, keepdims=True), axis=1, keepdims=True)
        hi = lo + h
    e = lo
    for _ in range(3):
        vp, vn, sp, sn = jnp.ones_like(e), d[0] - e, jnp.zeros_like(e), -jnp.ones_like(e)
        for p in range(1, 4):
            z = d[p] - e
            v2 = z * vn - w2[p - 1] * vp
            s2 = z * sn - vn - w2[p - 1] * sp
            vp, vn, sp, sn = vn, v2, sn, s2
        e = e - jnp.where(sn != 0, vn / sn, 0.0)
    return e


def ritz(d, off):
    e = smallest(d, off)
    co = [jnp.ones_like(e), (e - d[0]) / off[0]]
    for p in range(1, 3):
        co.append(((e - d[p]) * co[p] - off[p - 1] * co[p - 1]) / off[p])
    n = jnp.sqrt(co[0] * co[0] + co[1] * co[1] + co[2] * co[2] + co[3] * co[3])
    return e, [z / n for z in co]


def whole(
    entries, nsec, nch,
    left_in, right_in, slot_in, tr_in, x_in, b_in, kept_in,
    out_ref, en_ref,
    left, right, slot_ref, tr, x_ref, b_ref, kept_ref, lsem,
    wide, wire, cat, stage, recva, recvb, recvl, recvk, trecv, v_ref, st, strecv0, strecv1, vout,
    tpad, tbd, ebd, b2, c2, c1, mixed, moved, early, acat,
    ssem, rsem, tssem, trsem, qssem, qrsem,
):
    me = lax.axis_index("sector")
    ch = lax.axis_index("chain")
    cap = left_in.shape[1]
    recvs = (recva, recvb, recvl, recvk)
    parts = ((0, 0, 48, 0, 10), (0, 48, 16, 10, 3), (1, 0, 48, 0, 10), (1, 48, 16, 10, 3))
    my_z, my_y = me // NY, lax.rem(me, NY)
    nz = nsec // NY

    def peer(j):
        return lax.rem(my_z + j // NY, nz) * NY + lax.rem(my_y + j % NY, NY)

    def row_of(o):
        return lax.rem(my_z - o // NY + nz, nz) * NY + lax.rem(my_y - lax.rem(o, NY) + NY, NY)

    far = sorted(range(1, nsec), key=lambda j: -min(j // NY, nz - j // NY) - min(j % NY, NY - j % NY))
    order = sorted(range(1, nsec), key=lambda j: ((0, 2, 1, 3)[j % NY], -min(j // NY, nz - j // NY)))
    lane = lax.broadcasted_iota(jnp.int32, (1, 128), 1)
    tl = lane // 32
    loads = [
        pltpu.make_async_copy(a, b, lsem.at[i])
        for i, (a, b) in enumerate((
            (slot_in, slot_ref), (left_in, left), (tr_in, tr), (right_in, right), (b_in, b_ref), (x_in, x_ref), (kept_in, kept_ref)))
    ]
    for c in loads:
        c.start()
    bar = pltpu.get_barrier_semaphore()
    loop(1, nsec, lambda j: pl.semaphore_signal(bar, inc=1, device_id=(ch, lax.rem(me + j, nsec)), device_id_type=MESH))
    loop(1, nch, lambda j: pl.semaphore_signal(bar, inc=1, device_id=(lax.rem(ch + j, nch), me), device_id_type=MESH))
    def widen(src, first, n):
        for w in range(first, first + n):
            row8 = src[w].astype(F)
            for c in range(4):
                wide[c, cap * w:cap * w + cap, :] = row8[:, 128 * c:128 * c + 128]
            wide[4, cap * w:cap * w + cap, 0:64] = row8[:, 512:576]

    def pack(side, row, first, n):
        half = (n + 1) // 2
        for s in range(cap):
            for c in range(4):
                wire[s, row + n * c:row + n * c + n, :] = wide[c, pl.ds(s + cap * first, n, stride=cap), :]
            lo = wide[4, pl.ds(s + cap * first, half, stride=cap), :]
            hi = pltpu.roll(wide[4, pl.ds(s + cap * (first + half), n - half, stride=cap), :], 64, 1)
            wire[s, row + 4 * n:row + 4 * n + half, :] = jnp.where(lane < 64, lo, 0.0)
            wire[s, row + 4 * n:row + 5 * n - half, :] = jnp.where(lane < 64, lo[0:n - half], hi)

    def place(part, chosen):
        side, row, n = parts[part][:3]
        cat[side, :, row:row + n] = wire[:, row:row + n, :].astype(H)
        for j in range(nsec):
            stage[side, j, row:row + n] = cat[side, chosen[j], row:row + n]

    def tcopy(j):
        return pltpu.make_async_remote_copy(
            src_ref=tr, dst_ref=trecv.at[ch], send_sem=tssem.at[j], recv_sem=trsem.at[j],
            device_id=(lax.rem(ch + j, nch), me), device_id_type=MESH)

    def ecopy(part, j):
        side, row, n = parts[part][:3]
        src = stage.at[side, j, pl.ds(row, n)]
        return pltpu.make_async_remote_copy(
            src_ref=src, dst_ref=recvs[part].at[j], send_sem=ssem.at[part], recv_sem=rsem.at[part],
            device_id=(ch, peer(j)), device_id_type=MESH)

    def everyone(ref, send_sem, recv_sem):
        rows = ref.at[pl.ds(1, nsec - 1)]
        return pltpu.make_async_remote_copy(
            src_ref=rows, dst_ref=rows, send_sem=send_sem, recv_sem=recv_sem,
            device_id=(ch, lax.rem(me + 1, nsec)), device_id_type=MESH)

    loads[0].wait()
    chosen = []
    for j in range(nsec):
        h = peer(j)
        s = jnp.int32(0)
        for k in range(NT):
            g = slot_ref[0, h * NT + k]
            s = s + jnp.where(g // cap == me, lax.rem(g, cap), 0)
        chosen.append(s)
    loads[1].wait()
    wire[...] = jnp.zeros_like(wire)
    widen(left, 10, 3)
    pack(1, 48, 10, 3)
    place(3, chosen)
    pl.semaphore_wait(bar, nsec + nch - 2)
    for j in order:
        ecopy(3, j).start()
    widen(left, 0, 10)
    pack(1, 0, 0, 10)
    place(2, chosen)
    for j in order:
        ecopy(2, j).start()
    loads[2].wait()
    trecv[ch] = tr[...]
    loop(1, nch, lambda j: tcopy(j).start())
    loads[3].wait()
    widen(right, 0, NW)
    pack(0, 0, 0, 10)
    place(0, chosen)
    for j in order:
        ecopy(0, j).start()
    pack(0, 48, 10, 3)
    place(1, chosen)
    for j in order:
        ecopy(1, j).start()
    for part in range(4):
        side, row, n = parts[part][:3]
        recvs[part][0] = stage[side, 0, row:row + n]
    loads[4].wait()
    loads[5].wait()
    loads[6].wait()

    bf = b_ref[...].astype(F)
    for q in range(NP):
        off = 16 * q
        a = bf[:, (off // 128) * 128:(off // 128) * 128 + 128]
        sh = (-(off % 128)) % 128
        a = pltpu.roll(a, sh, 1) if sh else a
        tbd[pl.ds(q, NW, stride=NP), :] = jnp.where(lane < 16, a, 0.0)
    bb = tbd[0:208, :]
    b2[...] = (bb + pltpu.roll(bb, 16, 1))[:, :32].astype(H)
    for p in range(NP):
        acc = jnp.zeros((NB, 128), F)
        for t in range(NT):
            acc = acc + grab(lambda c: x_ref[t, :, c * 128:(c + 1) * 128], NB * p, t, lane)
        v_ref[0, pl.ds(p, NB, stride=NP), :] = acc
    x = v_ref[0]
    n0 = jnp.sqrt(full(x * x))
    v_ref[0] = x * inverse(n0)
    loop(1, nch, lambda j: tcopy(j).wait())
    tbd[...] = jnp.zeros_like(tbd)
    for t in range(NT):
        tpad[0:8, 0:576] = trecv[:, t, :]
        for i in range(NB):
            tbd[pl.ds(32 * t + i, 8, stride=128), :] = grab(lambda c: tpad[0:8, c * 128:(c + 1) * 128], NB * i, t, lane)
    row = lax.broadcasted_iota(jnp.int32, (128, 128), 0)
    col = lax.broadcasted_iota(jnp.int32, (128, 128), 1)
    eye = (row == col).astype(F)
    T = [jnp.where(ch > c, tbd[c * 128:(c + 1) * 128, :], eye) for c in range(7)]

    def mm(a, b):
        return jnp.dot(a, b, precision=lax.Precision.HIGHEST, preferred_element_type=F)

    pre = mm(mm(T[6], mm(T[5], T[4])), mm(mm(T[3], T[2]), mm(T[1], T[0])))
    ph, plo = split(pre.T)

    ebd[...] = jnp.zeros_like(ebd)
    c1[...] = jnp.zeros_like(c1)

    def spread(part, first, n):
        half = (n + 1) // 2
        m = recvs[part].shape[1]
        for t in range(NT):
            o = slot_ref[0, me * NT + t] // cap
            wire[t, 0:m] = recvs[part][row_of(o)].astype(F)
            tpad[0:half, 0:128] = wire[t, 4 * n:4 * n + half, :]
            tpad[half:n, 0:128] = pltpu.roll(wire[t, 4 * n:5 * n - half, :], 64, 1)
            tile = lambda c: wire[t, n * c:n * c + n, :] if c < 4 else tpad[0:n, 0:128]
            for i in range(NB):
                ebd[pl.ds(128 * first + 32 * t + i, n, stride=128), :] = grab(tile, NB * i, t, lane)

    def pair_step(k, parts=2):
        bm = b2[...]
        for l in range(0, NB, 2):
            xx = jnp.concatenate([v_ref[k, 16 * l:16 * l + 16, :], v_ref[k, 16 * l + 16:16 * l + 32, :]], 1)
            h, lo = split(xx)
            o = jnp.dot(bm, jnp.concatenate([h, lo], 0), preferred_element_type=F)
            h, lo = split(o)
            mixed[0, l] = h[:, :128]
            mixed[0, l + 1] = h[:, 128:]
            if parts == 2:
                mixed[1, l] = lo[:, :128]
                mixed[1, l + 1] = lo[:, 128:]

    def right_step(first=0, last=NW):
        for w in range(first, last):
            h = mixed[0, :, 16 * w:16 * w + 16, :].reshape(384, 128)
            lo = mixed[1, :, 16 * w:16 * w + 16, :].reshape(384, 128)
            o = jnp.dot(jnp.concatenate([h, lo], 1), c2[w], preferred_element_type=F)
            moved[w] = jnp.swapaxes(o.reshape(NB, NP, 128), 0, 1)

    def right_step_rounded():
        for w in range(0, NW, 2):
            n = min(2, NW - w)
            h = jnp.concatenate([mixed[0, :, 16 * (w + i):16 * (w + i) + 16, :].reshape(384, 128) for i in range(n)], 1)
            o = jnp.dot(h, c1[w // 2, 0:128 * n, 0:128 * n], preferred_element_type=F)
            for i in range(n):
                moved[w + i] = jnp.swapaxes(o[:, 128 * i:128 * i + 128].reshape(NB, NP, 128), 0, 1)

    def columns(q, first, last):
        return jnp.concatenate([jnp.concatenate([moved[w, q + j] for w in range(first, last)], 0) for j in range(2)], 1)

    def emit(k, q, o):
        for j in range(2):
            oj = o[:, 128 * j:128 * j + 128]
            y = jnp.where(tl == 0, oj[0:24], jnp.where(tl == 1, oj[24:48], jnp.where(tl == 2, oj[48:72], oj[72:96])))
            v_ref[k + 1, pl.ds(q + j, NB, stride=NP), :] = y

    def twice(a):
        return jnp.concatenate([a, a], 1).astype(H)

    def left_dot(a, r, both):
        if both:
            h = r.astype(H).astype(F)
            r = jnp.concatenate([h, r - h], 0)
        return jnp.dot(a, r.astype(H), preferred_element_type=F)

    def left_step(k, a2, both):
        a = a2 if both else a2[:, :24 * NW]
        for q in range(0, NP, 2):
            emit(k, q, left_dot(a, columns(q, 0, NW), both))

    pair_step(0)
    for part in (3, 2):
        everyone(recvs[part], ssem.at[part], rsem.at[part]).wait()
        spread(part, *parts[part][3:])
    pp = jnp.concatenate([ph, plo], 0)
    pq = jnp.concatenate([ph, plo, ph], 0)
    for w in range(NW):
        e = ebd[w * 128:(w + 1) * 128, :].astype(H)
        s = jnp.dot(jnp.concatenate([e, e], 1), pp, preferred_element_type=F)
        sh, sl = split(s.T)
        at = jnp.dot(jnp.concatenate([sh, sh, sl], 1), pq, preferred_element_type=F)
        acat[24 * w:24 * w + 24, :] = at[0:24] + at[32:56] + at[64:88] + at[96:120]
    acat[312:384, :] = jnp.zeros((72, 128), F)
    al = acat[...].T
    al = jnp.concatenate([al[32 * t:32 * t + 24] for t in range(NT)], 0)[:, :312].astype(H).astype(F)
    a2 = twice(al)
    for part, first, last in ((0, 0, 10), (1, 10, NW)):
        everyone(recvs[part], ssem.at[part], rsem.at[part]).wait()
        spread(part, first, last - first)
        for w in range(first, last):
            ct = ebd[w * 128:(w + 1) * 128, :].T.astype(H)
            c2[w, 0:128, :] = ct
            c2[w, 128:256, :] = ct
            i = 128 * (w % 2)
            c1[w // 2, i:i + 128, i:i + 128] = ct
        right_step(first, last)
        a = twice(al[:, 24 * first:24 * last])
        for q in range(0, NP, 2):
            o = left_dot(a, columns(q, first, last), True)
            if part == 0:
                early[q // 2] = o
            else:
                emit(0, q, early[q // 2] + o)

    alphas = []
    betas = []
    for k in range(3):
        if k > 0:
            pair_step(k, 1)
            right_step_rounded()
            left_step(k, a2, k == 1)
        y = v_ref[k + 1]
        a = full(v_ref[k] * y)
        r = y - a * v_ref[k]
        if k > 0:
            r = r - betas[-1] * v_ref[k - 1]
        b = jnp.sqrt(full(r * r))
        alphas.append(a)
        betas.append(b)
        v_ref[k + 1] = r * inverse(b)

    def qcopy(i, j):
        return pltpu.make_async_remote_copy(
            src_ref=st.at[i], dst_ref=(strecv0, strecv1)[i].at[j], send_sem=qssem.at[i], recv_sem=qrsem.at[i],
            device_id=(ch, peer(j)), device_id_type=MESH)

    def lanes(rows):
        g = jnp.concatenate(rows + [jnp.zeros((128 - len(rows), 128), F)], 0)
        return lax.dot_general(lhs, g, (((1,), (1,)), ((), ())), precision=lax.Precision.HIGHEST, preferred_element_type=F)

    def gathered(ref):
        return jnp.concatenate([ref[:, 0, :], jnp.zeros((128 - nsec, 128), F)], 0).T

    kp = jnp.where(tl == 0, kept_ref[0, 0], jnp.where(tl == 1, kept_ref[0, 1], jnp.where(tl == 2, kept_ref[0, 2], kept_ref[0, 3])))
    keep = lax.rem(lane, 32) < kp
    r8 = lax.broadcasted_iota(jnp.int32, (8, 128), 0)
    lhs = jnp.where(r8 == 0, 1.0, jnp.where((r8 == 1) & keep, 1.0, 0.0))
    s = lanes([jnp.sum(v_ref[i] * v_ref[j], axis=0, keepdims=True) for i in range(4) for j in range(i, 4)])
    s = s[0:1] + pltpu.roll(s[1:2], 64, 1)
    for i, val in enumerate([n0] + alphas + betas):
        s = s + jnp.where(lane == 16 + i, val, 0.0)
    st[0] = s
    for j in far:
        qcopy(0, j).start()
    strecv0[0] = s
    pair_step(3, 1)
    right_step_rounded()
    left_step(3, a2, False)
    s = jnp.zeros((1, 128), F)
    for i in range(4):
        s = s + jnp.where(lane == i, full(v_ref[i] * v_ref[4]), 0.0)
    st[1] = s
    for j in far:
        qcopy(1, j).start()
    strecv1[0] = s
    for k in range(1, 4):
        for p in range(NP):
            a = v_ref[k, pl.ds(p, NB, stride=NP), :]
            for t in range(NT):
                vout[k - 1, t, :, NB * p:NB * p + NB] = a[:, 32 * t:32 * t + NB]
    everyone(strecv0, qssem.at[0], qrsem.at[0]).wait()
    q0 = gathered(strecv0)
    cs, g, diag, off, norms, mine = recursion(lambda i: q0[i:i + 1, :], lane == 0)
    everyone(strecv1, qssem.at[1], qrsem.at[1]).wait()
    q1 = gathered(strecv1)
    z = cs[3][0] * q1[0:1, :]
    for i in range(1, 4):
        z = z + cs[3][i] * q1[i:i + 1, :]
    diag.append(total(g + z * cs[3][3]))
    e, co = ritz(diag, off)
    en_ref[...] = e
    n2 = None
    for k in range(4):
        for m in range(4):
            z = co[k] * co[m] * norms[k][m]
            n2 = z if n2 is None else n2 + z
    scale = jnp.sqrt(entries / n2)
    f = []
    for i in range(4):
        z = None
        for k in range(i, 4):
            c = co[k] * mine[k][i]
            z = c if z is None else z + c
        f.append(z * scale)
    f[0] = f[0] * inverse(n0)
    column = lax.rem(lax.broadcasted_iota(jnp.int32, (1, NP * NB), 1), NB)
    for t in range(NT):
        y = f[0] * x_ref[t]
        for k in range(1, 4):
            y = y + f[k] * vout[k - 1, t]
        out_ref[t] = jnp.where(column < kept_ref[0, t], y, 0.0)


def body(wavefunction, transfer, left_env, right_env, pair_ops, env_slot, kept_ranks):
    nsec = lax.axis_size("sector")
    nch = lax.axis_size("chain")
    cap = left_env.shape[1]
    entries = float(nsec * NT * NB * NP * NB)
    vmem = pl.BlockSpec(memory_space=pltpu.VMEM)
    hbm = pl.BlockSpec(memory_space=pltpu.HBM)
    dma = pltpu.SemaphoreType.DMA
    out, en = pl.pallas_call(
        functools.partial(whole, entries, nsec, nch),
        out_shape=(jax.ShapeDtypeStruct((NT, NB, NP * NB), F), jax.ShapeDtypeStruct((1, 1), F)),
        in_specs=[hbm] * 7,
        out_specs=(vmem, vmem),
        scratch_shapes=[
            pltpu.VMEM((NW, cap, 576), H),
            pltpu.VMEM((NW, cap, 576), H),
            pltpu.SMEM(env_slot.shape, jnp.int32),
            pltpu.VMEM(transfer.shape[1:], F),
            pltpu.VMEM(wavefunction.shape[1:], F),
            pltpu.VMEM(pair_ops.shape[1:], H),
            pltpu.SMEM(kept_ranks.shape, jnp.int32),
            dma((7,)),
            pltpu.VMEM((5, cap * NW, 128), F),
            pltpu.VMEM((cap, 64, 128), F),
            pltpu.VMEM((2, cap, 64, 128), H),
            pltpu.VMEM((2, nsec, 64, 128), H),
            pltpu.VMEM((nsec, 48, 128), H),
            pltpu.VMEM((nsec, 16, 128), H),
            pltpu.VMEM((nsec, 48, 128), H),
            pltpu.VMEM((nsec, 16, 128), H),
            pltpu.VMEM((nch, NT, 576), F),
            pltpu.VMEM((5, 384, 128), F),
            pltpu.VMEM((2, 1, 128), F),
            pltpu.VMEM((nsec, 1, 128), F),
            pltpu.VMEM((nsec, 1, 128), F),
            pltpu.VMEM((3, NT, NB, NP * NB), F),
            pltpu.VMEM((16, 640), F),
            pltpu.VMEM((1024, 128), F),
            pltpu.VMEM((1664, 128), F),
            pltpu.VMEM((208, 32), H),
            pltpu.VMEM((NW, 256, 128), H),
            pltpu.VMEM(((NW + 1) // 2, 256, 256), H),
            pltpu.VMEM((2, NB, 208, 128), H),
            pltpu.VMEM((NW, NP, NB, 128), F),
            pltpu.VMEM((NP // 2, NT * NB, 256), F),
            pltpu.VMEM((384, 128), F),
            dma((4,)), dma((4,)), dma((nch,)), dma((nch,)), dma((2,)), dma((2,)),
        ],
        compiler_params=pltpu.CompilerParams(collective_id=0, has_side_effects=True, vmem_limit_bytes=48 * 2**20),
        name="lanczos",
    )(*(
        pltpu.with_memory_space_constraint(a, pltpu.HBM)
        for a in (
            jnp.swapaxes(left_env[0], 0, 1), jnp.swapaxes(right_env[0], 0, 1), env_slot, transfer[0], wavefunction[0],
            pair_ops[0], kept_ranks)
    ))
    return out[None], en.reshape(1)


def solution(mesh):
    return jax.shard_map(
        body,
        mesh=mesh,
        in_specs=(
            P("chain", "sector", None, None),
            P("chain", "sector", None),
            P("chain", "sector", None, None),
            P("chain", "sector", None, None),
            P("chain", None, None),
            P("chain", None),
            P("chain", "sector"),
        ),
        out_specs=(P("chain", "sector", None, None), P("chain")),
        check_vma=False,
    )
```

```python
import functools

import jax
import jax.numpy as jnp
from jax import lax
from jax.experimental import pallas as pl
from jax.experimental.pallas import tpu as pltpu
from jax.sharding import PartitionSpec as P

F = jnp.float32
H = jnp.bfloat16
NT = 4
NB = 24
NP = 16
NW = 13
NY = 4
MESH = pl.DeviceIdType.MESH


def split(x):
    h = x.astype(H)
    return h, (x - h.astype(F)).astype(H)


def grab(tile, off, t, lane):
    c0, o = off // 128, off % 128
    sh = (32 * t - o) % 128
    a = tile(c0)
    a = pltpu.roll(a, sh, 1) if sh else a
    if o + NB > 128:
        b = tile(c0 + 1)
        b = pltpu.roll(b, sh, 1) if sh else b
        a = jnp.where(lane < 32 * t + 128 - o, a, b)
    return jnp.where((lane >= 32 * t) & (lane < 32 * t + NB), a, 0.0)


def full(x):
    return jnp.sum(jnp.sum(x, axis=0, keepdims=True), axis=1, keepdims=True)


def inverse(n):
    return jnp.where(n > 0, 1.0 / n, 0.0)


def loop(a, b, f):
    def step(j, c):
        f(j)
        return c

    lax.fori_loop(a, b, step, 0)


def total(x):
    return jnp.sum(x, axis=1, keepdims=True)


def weighted(m, a, b):
    acc = None
    for i in range(len(a)):
        s = None
        for j in range(len(b)):
            z = m[i][j] * b[j]
            s = z if s is None else s + z
        s = s * a[i]
        acc = s if acc is None else acc + s
    return acc


def recursion(q, sel):
    pos = {}
    for i in range(4):
        for j in range(i, 4):
            pos[i, j] = pos[j, i] = len(set(pos.values()))
    gram = [[q(pos[i, j]) for j in range(4)] for i in range(4)]
    kept = [[q(64 + pos[i, j]) for j in range(4)] for i in range(4)]
    n0 = q(16)
    al = [q(17 + i) for i in range(3)]
    be = [q(20 + i) for i in range(3)]

    def image(c):
        k = len(c) - 1
        y = [None] * min(k + 2, 4)

        def add(i, z):
            y[i] = z if y[i] is None else y[i] + z

        for j in range(min(k + 1, 3)):
            add(j, al[j] * c[j])
            add(j + 1, be[j] * c[j])
            if j > 0:
                add(j - 1, be[j - 1] * c[j])
        return y

    c = [n0 / jnp.sqrt(total(n0 * n0))]
    cp = []
    b = None
    cs = []
    diag = []
    off = []
    for k in range(4):
        cs.append(c)
        y = image(c)
        g = weighted(gram, c, y)
        if k == 3:
            break
        a = total(g)
        diag.append(a)
        r = []
        for i in range(len(y)):
            z = y[i]
            if i < len(c):
                z = z - a * c[i]
            if i < len(cp):
                z = z - b * cp[i]
            r.append(z)
        b = jnp.sqrt(total(weighted(gram, r, r)))
        off.append(b)
        cp = c
        c = [z / b for z in r]
    norms = [[total(weighted(kept, cs[k], cs[m])) for m in range(4)] for k in range(4)]
    mine = [[total(jnp.where(sel, z, 0.0)) for z in cs[k]] for k in range(4)]
    return cs, g, diag, off, norms, mine


def smallest(d, off):
    ab = [jnp.abs(z) for z in off]
    w2 = [z * z for z in off]
    least = lambda v: jnp.minimum(jnp.minimum(v[0], v[1]), jnp.minimum(v[2], v[3]))
    lo = least([d[0] - ab[0], d[1] - ab[0] - ab[1], d[2] - ab[1] - ab[2], d[3] - ab[2]])
    hi = least(d)
    idx = (lax.broadcasted_iota(jnp.int32, (8, 128), 0) * 128 + lax.broadcasted_iota(jnp.int32, (8, 128), 1) + 1).astype(F)
    for _ in range(2):
        h = (hi - lo) * (1.0 / 1024.0)
        x = lo + h * idx
        p1 = d[0] - x
        p2 = (d[1] - x) * p1 - w2[0]
        p3 = (d[2] - x) * p2 - w2[1] * p1
        p4 = (d[3] - x) * p3 - w2[2] * p2
        below = (p1 > 0) & (p2 > 0) & (p3 > 0) & (p4 > 0)
        x = jnp.where(below, x, lo)
        lo = jnp.max(jnp.max(x, axis=0, keepdims=True), axis=1, keepdims=True)
        hi = lo + h
    e = lo
    for _ in range(3):
        vp, vn, sp, sn = jnp.ones_like(e), d[0] - e, jnp.zeros_like(e), -jnp.ones_like(e)
        for p in range(1, 4):
            z = d[p] - e
            v2 = z * vn - w2[p - 1] * vp
            s2 = z * sn - vn - w2[p - 1] * sp
            vp, vn, sp, sn = vn, v2, sn, s2
        e = e - jnp.where(sn != 0, vn / sn, 0.0)
    return e


def ritz(d, off):
    e = smallest(d, off)
    co = [jnp.ones_like(e), (e - d[0]) / off[0]]
    for p in range(1, 3):
        co.append(((e - d[p]) * co[p] - off[p - 1] * co[p - 1]) / off[p])
    n = jnp.sqrt(co[0] * co[0] + co[1] * co[1] + co[2] * co[2] + co[3] * co[3])
    return e, [z / n for z in co]


def whole(
    entries, nsec, nch,
    left_in, right_in, slot_in, tr_in, x_in, b_in, kept_in,
    out_ref, en_ref,
    left, right, slot_ref, tr, x_ref, b_ref, kept_ref, lsem,
    wide, wire, cat, stage, recva, recvb, recvl, trecv, v_ref, st, strecv0, strecv1, vout,
    tpad, tbd, ebd, b2, c2, c1, mixed, moved, early, acat,
    ssem, rsem, tssem, trsem, qssem, qrsem,
):
    me = lax.axis_index("sector")
    ch = lax.axis_index("chain")
    cap = left_in.shape[1]
    recvs = (recva, recvb, recvl)
    parts = ((0, 0, 48, 0, 10), (0, 48, 16, 10, 3), (1, 0, 64, 0, NW))
    my_z, my_y = me // NY, lax.rem(me, NY)
    nz = nsec // NY

    def peer(j):
        return lax.rem(my_z + j // NY, nz) * NY + lax.rem(my_y + j % NY, NY)

    def row_of(o):
        return lax.rem(my_z - o // NY + nz, nz) * NY + lax.rem(my_y - lax.rem(o, NY) + NY, NY)

    far = sorted(range(1, nsec), key=lambda j: -min(j // NY, nz - j // NY) - min(j % NY, NY - j % NY))
    order = sorted(range(1, nsec), key=lambda j: ((0, 2, 1, 3)[j % NY], -min(j // NY, nz - j // NY)))
    lane = lax.broadcasted_iota(jnp.int32, (1, 128), 1)
    tl = lane // 32
    loads = [
        pltpu.make_async_copy(a, b, lsem.at[i])
        for i, (a, b) in enumerate((
            (slot_in, slot_ref), (left_in, left), (tr_in, tr), (right_in, right), (b_in, b_ref), (x_in, x_ref), (kept_in, kept_ref)))
    ]
    for c in loads:
        c.start()
    bar = pltpu.get_barrier_semaphore()
    loop(1, nsec, lambda j: pl.semaphore_signal(bar, inc=1, device_id=(ch, lax.rem(me + j, nsec)), device_id_type=MESH))
    loop(1, nch, lambda j: pl.semaphore_signal(bar, inc=1, device_id=(lax.rem(ch + j, nch), me), device_id_type=MESH))
    def widen(src, first, n):
        for w in range(first, first + n):
            row8 = src[w].astype(F)
            for c in range(4):
                wide[c, cap * w:cap * w + cap, :] = row8[:, 128 * c:128 * c + 128]
            wide[4, cap * w:cap * w + cap, 0:64] = row8[:, 512:576]

    def pack(side, row, first, n):
        half = (n + 1) // 2
        for s in range(cap):
            for c in range(4):
                wire[s, row + n * c:row + n * c + n, :] = wide[c, pl.ds(s + cap * first, n, stride=cap), :]
            lo = wide[4, pl.ds(s + cap * first, half, stride=cap), :]
            hi = pltpu.roll(wide[4, pl.ds(s + cap * (first + half), n - half, stride=cap), :], 64, 1)
            wire[s, row + 4 * n:row + 4 * n + half, :] = jnp.where(lane < 64, lo, 0.0)
            wire[s, row + 4 * n:row + 5 * n - half, :] = jnp.where(lane < 64, lo[0:n - half], hi)

    def place(part, chosen):
        side, row, n = parts[part][:3]
        cat[side, :, row:row + n] = wire[:, row:row + n, :].astype(H)
        for j in range(nsec):
            stage[side, j, row:row + n] = cat[side, chosen[j], row:row + n]

    def tcopy(j):
        return pltpu.make_async_remote_copy(
            src_ref=tr, dst_ref=trecv.at[ch], send_sem=tssem.at[j], recv_sem=trsem.at[j],
            device_id=(lax.rem(ch + j, nch), me), device_id_type=MESH)

    def ecopy(part, j):
        side, row, n = parts[part][:3]
        src = stage.at[side, j, pl.ds(row, n)]
        return pltpu.make_async_remote_copy(
            src_ref=src, dst_ref=recvs[part].at[j], send_sem=ssem.at[part], recv_sem=rsem.at[part],
            device_id=(ch, peer(j)), device_id_type=MESH)

    def everyone(ref, send_sem, recv_sem):
        rows = ref.at[pl.ds(1, nsec - 1)]
        return pltpu.make_async_remote_copy(
            src_ref=rows, dst_ref=rows, send_sem=send_sem, recv_sem=recv_sem,
            device_id=(ch, lax.rem(me + 1, nsec)), device_id_type=MESH)

    loads[0].wait()
    chosen = []
    for j in range(nsec):
        h = peer(j)
        s = jnp.int32(0)
        for k in range(NT):
            g = slot_ref[0, h * NT + k]
            s = s + jnp.where(g // cap == me, lax.rem(g, cap), 0)
        chosen.append(s)
    loads[1].wait()
    wire[...] = jnp.zeros_like(wire)
    widen(left, 0, NW)
    pack(1, 0, 0, NW)
    place(2, chosen)
    pl.semaphore_wait(bar, nsec + nch - 2)
    for j in order:
        ecopy(2, j).start()
    loads[2].wait()
    trecv[ch] = tr[...]
    loop(1, nch, lambda j: tcopy(j).start())
    loads[3].wait()
    widen(right, 0, NW)
    pack(0, 0, 0, 10)
    place(0, chosen)
    for j in order:
        ecopy(0, j).start()
    pack(0, 48, 10, 3)
    place(1, chosen)
    for j in order:
        ecopy(1, j).start()
    for part in range(3):
        side, row, n = parts[part][:3]
        recvs[part][0] = stage[side, 0, row:row + n]
    loads[4].wait()
    loads[5].wait()
    loads[6].wait()

    bf = b_ref[...].astype(F)
    for q in range(NP):
        off = 16 * q
        a = bf[:, (off // 128) * 128:(off // 128) * 128 + 128]
        sh = (-(off % 128)) % 128
        a = pltpu.roll(a, sh, 1) if sh else a
        tbd[pl.ds(q, NW, stride=NP), :] = jnp.where(lane < 16, a, 0.0)
    bb = tbd[0:208, :]
    b2[...] = (bb + pltpu.roll(bb, 16, 1))[:, :32].astype(H)
    for p in range(NP):
        acc = jnp.zeros((NB, 128), F)
        for t in range(NT):
            acc = acc + grab(lambda c: x_ref[t, :, c * 128:(c + 1) * 128], NB * p, t, lane)
        v_ref[0, pl.ds(p, NB, stride=NP), :] = acc
    x = v_ref[0]
    n0 = jnp.sqrt(full(x * x))
    v_ref[0] = x * inverse(n0)
    loop(1, nch, lambda j: tcopy(j).wait())
    tbd[...] = jnp.zeros_like(tbd)
    for t in range(NT):
        tpad[0:8, 0:576] = trecv[:, t, :]
        for i in range(NB):
            tbd[pl.ds(32 * t + i, 8, stride=128), :] = grab(lambda c: tpad[0:8, c * 128:(c + 1) * 128], NB * i, t, lane)
    row = lax.broadcasted_iota(jnp.int32, (128, 128), 0)
    col = lax.broadcasted_iota(jnp.int32, (128, 128), 1)
    eye = (row == col).astype(F)
    T = [jnp.where(ch > c, tbd[c * 128:(c + 1) * 128, :], eye) for c in range(7)]

    def mm(a, b):
        return jnp.dot(a, b, precision=lax.Precision.HIGHEST, preferred_element_type=F)

    pre = mm(mm(T[6], mm(T[5], T[4])), mm(mm(T[3], T[2]), mm(T[1], T[0])))
    ph, plo = split(pre.T)

    ebd[...] = jnp.zeros_like(ebd)
    c1[...] = jnp.zeros_like(c1)

    def spread(part, first, n):
        half = (n + 1) // 2
        m = recvs[part].shape[1]
        for t in range(NT):
            o = slot_ref[0, me * NT + t] // cap
            wire[t, 0:m] = recvs[part][row_of(o)].astype(F)
            tpad[0:half, 0:128] = wire[t, 4 * n:4 * n + half, :]
            tpad[half:n, 0:128] = pltpu.roll(wire[t, 4 * n:5 * n - half, :], 64, 1)
            tile = lambda c: wire[t, n * c:n * c + n, :] if c < 4 else tpad[0:n, 0:128]
            for i in range(NB):
                ebd[pl.ds(128 * first + 32 * t + i, n, stride=128), :] = grab(tile, NB * i, t, lane)

    def pair_step(k, parts=2):
        bm = b2[...]
        for l in range(0, NB, 2):
            xx = jnp.concatenate([v_ref[k, 16 * l:16 * l + 16, :], v_ref[k, 16 * l + 16:16 * l + 32, :]], 1)
            h, lo = split(xx)
            o = jnp.dot(bm, jnp.concatenate([h, lo], 0), preferred_element_type=F)
            h, lo = split(o)
            mixed[0, l] = h[:, :128]
            mixed[0, l + 1] = h[:, 128:]
            if parts == 2:
                mixed[1, l] = lo[:, :128]
                mixed[1, l + 1] = lo[:, 128:]

    def right_step(first=0, last=NW):
        for w in range(first, last):
            h = mixed[0, :, 16 * w:16 * w + 16, :].reshape(384, 128)
            lo = mixed[1, :, 16 * w:16 * w + 16, :].reshape(384, 128)
            o = jnp.dot(jnp.concatenate([h, lo], 1), c2[w], preferred_element_type=F)
            moved[w] = jnp.swapaxes(o.reshape(NB, NP, 128), 0, 1)

    def right_step_rounded():
        for w in range(0, NW, 2):
            n = min(2, NW - w)
            h = jnp.concatenate([mixed[0, :, 16 * (w + i):16 * (w + i) + 16, :].reshape(384, 128) for i in range(n)], 1)
            o = jnp.dot(h, c1[w // 2, 0:128 * n, 0:128 * n], preferred_element_type=F)
            for i in range(n):
                moved[w + i] = jnp.swapaxes(o[:, 128 * i:128 * i + 128].reshape(NB, NP, 128), 0, 1)

    def columns(q, first, last):
        return jnp.concatenate([jnp.concatenate([moved[w, q + j] for w in range(first, last)], 0) for j in range(2)], 1)

    def emit(k, q, o):
        for j in range(2):
            oj = o[:, 128 * j:128 * j + 128]
            y = jnp.where(tl == 0, oj[0:24], jnp.where(tl == 1, oj[24:48], jnp.where(tl == 2, oj[48:72], oj[72:96])))
            v_ref[k + 1, pl.ds(q + j, NB, stride=NP), :] = y

    def twice(a):
        return jnp.concatenate([a, a], 1).astype(H)

    def left_dot(a, r, both):
        if both:
            h = r.astype(H).astype(F)
            r = jnp.concatenate([h, r - h], 0)
        return jnp.dot(a, r.astype(H), preferred_element_type=F)

    def left_step(k, a2, both):
        a = a2 if both else a2[:, :24 * NW]
        for q in range(0, NP, 2):
            emit(k, q, left_dot(a, columns(q, 0, NW), both))

    pair_step(0)
    everyone(recvs[2], ssem.at[2], rsem.at[2]).wait()
    spread(2, 0, NW)
    pp = jnp.concatenate([ph, plo], 0)
    pq = jnp.concatenate([ph, plo, ph], 0)
    for w in range(NW):
        e = ebd[w * 128:(w + 1) * 128, :].astype(H)
        s = jnp.dot(jnp.concatenate([e, e], 1), pp, preferred_element_type=F)
        sh, sl = split(s.T)
        at = jnp.dot(jnp.concatenate([sh, sh, sl], 1), pq, preferred_element_type=F)
        acat[24 * w:24 * w + 24, :] = at[0:24] + at[32:56] + at[64:88] + at[96:120]
    acat[312:384, :] = jnp.zeros((72, 128), F)
    al = acat[...].T
    al = jnp.concatenate([al[32 * t:32 * t + 24] for t in range(NT)], 0)[:, :312].astype(H).astype(F)
    a2 = twice(al)
    for part, first, last in ((0, 0, 10), (1, 10, NW)):
        everyone(recvs[part], ssem.at[part], rsem.at[part]).wait()
        spread(part, first, last - first)
        for w in range(first, last):
            ct = ebd[w * 128:(w + 1) * 128, :].T.astype(H)
            c2[w, 0:128, :] = ct
            c2[w, 128:256, :] = ct
            i = 128 * (w % 2)
            c1[w // 2, i:i + 128, i:i + 128] = ct
        right_step(first, last)
        a = twice(al[:, 24 * first:24 * last])
        for q in range(0, NP, 2):
            o = left_dot(a, columns(q, first, last), True)
            if part == 0:
                early[q // 2] = o
            else:
                emit(0, q, early[q // 2] + o)

    alphas = []
    betas = []
    for k in range(3):
        if k > 0:
            pair_step(k, 1)
            right_step_rounded()
            left_step(k, a2, k == 1)
        y = v_ref[k + 1]
        a = full(v_ref[k] * y)
        r = y - a * v_ref[k]
        if k > 0:
            r = r - betas[-1] * v_ref[k - 1]
        rr = full(r * r)
        b = jnp.sqrt(rr)
        alphas.append(a)
        betas.append(b)
        v_ref[k + 1] = r * jnp.where(rr > 0, lax.rsqrt(rr), 0.0)

    def qcopy(i, j):
        return pltpu.make_async_remote_copy(
            src_ref=st.at[i], dst_ref=(strecv0, strecv1)[i].at[j], send_sem=qssem.at[i], recv_sem=qrsem.at[i],
            device_id=(ch, peer(j)), device_id_type=MESH)

    def lanes(rows):
        g = jnp.concatenate(rows + [jnp.zeros((128 - len(rows), 128), F)], 0)
        return lax.dot_general(lhs, g, (((1,), (1,)), ((), ())), precision=lax.Precision.HIGHEST, preferred_element_type=F)

    def gathered(ref):
        return jnp.concatenate([ref[:, 0, :], jnp.zeros((128 - nsec, 128), F)], 0).T

    kp = jnp.where(tl == 0, kept_ref[0, 0], jnp.where(tl == 1, kept_ref[0, 1], jnp.where(tl == 2, kept_ref[0, 2], kept_ref[0, 3])))
    keep = lax.rem(lane, 32) < kp
    r8 = lax.broadcasted_iota(jnp.int32, (8, 128), 0)
    lhs = jnp.where(r8 == 0, 1.0, jnp.where((r8 == 1) & keep, 1.0, 0.0))
    s = lanes([jnp.sum(v_ref[i] * v_ref[j], axis=0, keepdims=True) for i in range(4) for j in range(i, 4)])
    s = s[0:1] + pltpu.roll(s[1:2], 64, 1)
    for i, val in enumerate([n0] + alphas + betas):
        s = s + jnp.where(lane == 16 + i, val, 0.0)
    st[0] = s
    for j in far:
        qcopy(0, j).start()
    strecv0[0] = s
    pair_step(3, 1)
    right_step_rounded()
    left_step(3, a2, False)
    s = jnp.zeros((1, 128), F)
    for i in range(4):
        s = s + jnp.where(lane == i, full(v_ref[i] * v_ref[4]), 0.0)
    st[1] = s
    for j in far:
        qcopy(1, j).start()
    strecv1[0] = s
    for k in range(1, 4):
        for p in range(NP):
            a = v_ref[k, pl.ds(p, NB, stride=NP), :]
            for t in range(NT):
                vout[k - 1, t, :, NB * p:NB * p + NB] = a[:, 32 * t:32 * t + NB]
    everyone(strecv0, qssem.at[0], qrsem.at[0]).wait()
    q0 = gathered(strecv0)
    cs, g, diag, off, norms, mine = recursion(lambda i: q0[i:i + 1, :], lane == 0)
    everyone(strecv1, qssem.at[1], qrsem.at[1]).wait()
    q1 = gathered(strecv1)
    z = cs[3][0] * q1[0:1, :]
    for i in range(1, 4):
        z = z + cs[3][i] * q1[i:i + 1, :]
    diag.append(total(g + z * cs[3][3]))
    e, co = ritz(diag, off)
    en_ref[...] = e
    n2 = None
    for k in range(4):
        for m in range(4):
            z = co[k] * co[m] * norms[k][m]
            n2 = z if n2 is None else n2 + z
    scale = jnp.sqrt(entries / n2)
    f = []
    for i in range(4):
        z = None
        for k in range(i, 4):
            c = co[k] * mine[k][i]
            z = c if z is None else z + c
        f.append(z * scale)
    f[0] = f[0] * inverse(n0)
    column = lax.rem(lax.broadcasted_iota(jnp.int32, (1, NP * NB), 1), NB)
    for t in range(NT):
        y = f[0] * x_ref[t]
        for k in range(1, 4):
            y = y + f[k] * vout[k - 1, t]
        out_ref[t] = jnp.where(column < kept_ref[0, t], y, 0.0)


def body(wavefunction, transfer, left_env, right_env, pair_ops, env_slot, kept_ranks):
    nsec = lax.axis_size("sector")
    nch = lax.axis_size("chain")
    cap = left_env.shape[1]
    entries = float(nsec * NT * NB * NP * NB)
    vmem = pl.BlockSpec(memory_space=pltpu.VMEM)
    hbm = pl.BlockSpec(memory_space=pltpu.HBM)
    dma = pltpu.SemaphoreType.DMA
    out, en = pl.pallas_call(
        functools.partial(whole, entries, nsec, nch),
        out_shape=(jax.ShapeDtypeStruct((NT, NB, NP * NB), F), jax.ShapeDtypeStruct((1, 1), F)),
        in_specs=[hbm] * 7,
        out_specs=(vmem, vmem),
        scratch_shapes=[
            pltpu.VMEM((NW, cap, 576), H),
            pltpu.VMEM((NW, cap, 576), H),
            pltpu.SMEM(env_slot.shape, jnp.int32),
            pltpu.VMEM(transfer.shape[1:], F),
            pltpu.VMEM(wavefunction.shape[1:], F),
            pltpu.VMEM(pair_ops.shape[1:], H),
            pltpu.SMEM(kept_ranks.shape, jnp.int32),
            dma((7,)),
            pltpu.VMEM((5, cap * NW, 128), F),
            pltpu.VMEM((cap, 64, 128), F),
            pltpu.VMEM((2, cap, 64, 128), H),
            pltpu.VMEM((2, nsec, 64, 128), H),
            pltpu.VMEM((nsec, 48, 128), H),
            pltpu.VMEM((nsec, 16, 128), H),
            pltpu.VMEM((nsec, 64, 128), H),
            pltpu.VMEM((nch, NT, 576), F),
            pltpu.VMEM((5, 384, 128), F),
            pltpu.VMEM((2, 1, 128), F),
            pltpu.VMEM((nsec, 1, 128), F),
            pltpu.VMEM((nsec, 1, 128), F),
            pltpu.VMEM((3, NT, NB, NP * NB), F),
            pltpu.VMEM((16, 640), F),
            pltpu.VMEM((1024, 128), F),
            pltpu.VMEM((1664, 128), F),
            pltpu.VMEM((208, 32), H),
            pltpu.VMEM((NW, 256, 128), H),
            pltpu.VMEM(((NW + 1) // 2, 256, 256), H),
            pltpu.VMEM((2, NB, 208, 128), H),
            pltpu.VMEM((NW, NP, NB, 128), F),
            pltpu.VMEM((NP // 2, NT * NB, 256), F),
            pltpu.VMEM((384, 128), F),
            dma((3,)), dma((3,)), dma((nch,)), dma((nch,)), dma((2,)), dma((2,)),
        ],
        compiler_params=pltpu.CompilerParams(collective_id=0, has_side_effects=True, vmem_limit_bytes=48 * 2**20),
        name="lanczos",
    )(*(
        pltpu.with_memory_space_constraint(a, pltpu.HBM)
        for a in (
            jnp.swapaxes(left_env[0], 0, 1), jnp.swapaxes(right_env[0], 0, 1), env_slot, transfer[0], wavefunction[0],
            pair_ops[0], kept_ranks)
    ))
    return out[None], en.reshape(1)


def solution(mesh):
    return jax.shard_map(
        body,
        mesh=mesh,
        in_specs=(
            P("chain", "sector", None, None),
            P("chain", "sector", None),
            P("chain", "sector", None, None),
            P("chain", "sector", None, None),
            P("chain", None, None),
            P("chain", None),
            P("chain", "sector"),
        ),
        out_specs=(P("chain", "sector", None, None), P("chain")),
        check_vma=False,
    )
```

```python
import functools

import jax
import jax.numpy as jnp
from jax import lax
from jax.experimental import pallas as pl
from jax.experimental.pallas import tpu as pltpu
from jax.sharding import PartitionSpec as P

F = jnp.float32
H = jnp.bfloat16
NT = 4
NB = 24
NP = 16
NW = 13
NY = 4
MESH = pl.DeviceIdType.MESH


def split(x):
    h = x.astype(H)
    return h, (x - h.astype(F)).astype(H)


def grab(tile, off, t, lane):
    c0, o = off // 128, off % 128
    sh = (32 * t - o) % 128
    a = tile(c0)
    a = pltpu.roll(a, sh, 1) if sh else a
    if o + NB > 128:
        b = tile(c0 + 1)
        b = pltpu.roll(b, sh, 1) if sh else b
        a = jnp.where(lane < 32 * t + 128 - o, a, b)
    return jnp.where((lane >= 32 * t) & (lane < 32 * t + NB), a, 0.0)


def full(x):
    return jnp.sum(jnp.sum(x, axis=0, keepdims=True), axis=1, keepdims=True)


def inverse(n):
    return jnp.where(n > 0, 1.0 / n, 0.0)


def loop(a, b, f):
    def step(j, c):
        f(j)
        return c

    lax.fori_loop(a, b, step, 0)


def total(x):
    return jnp.sum(x, axis=1, keepdims=True)


def weighted(m, a, b):
    acc = None
    for i in range(len(a)):
        s = None
        for j in range(len(b)):
            z = m[i][j] * b[j]
            s = z if s is None else s + z
        s = s * a[i]
        acc = s if acc is None else acc + s
    return acc


def recursion(q, sel):
    pos = {}
    for i in range(4):
        for j in range(i, 4):
            pos[i, j] = pos[j, i] = len(set(pos.values()))
    gram = [[q(pos[i, j]) for j in range(4)] for i in range(4)]
    kept = [[q(64 + pos[i, j]) for j in range(4)] for i in range(4)]
    n0 = q(16)
    al = [q(17 + i) for i in range(3)]
    be = [q(20 + i) for i in range(3)]

    def image(c):
        k = len(c) - 1
        y = [None] * min(k + 2, 4)

        def add(i, z):
            y[i] = z if y[i] is None else y[i] + z

        for j in range(min(k + 1, 3)):
            add(j, al[j] * c[j])
            add(j + 1, be[j] * c[j])
            if j > 0:
                add(j - 1, be[j - 1] * c[j])
        return y

    c = [n0 / jnp.sqrt(total(n0 * n0))]
    cp = []
    b = None
    cs = []
    diag = []
    off = []
    for k in range(4):
        cs.append(c)
        y = image(c)
        g = weighted(gram, c, y)
        if k == 3:
            break
        a = total(g)
        diag.append(a)
        r = []
        for i in range(len(y)):
            z = y[i]
            if i < len(c):
                z = z - a * c[i]
            if i < len(cp):
                z = z - b * cp[i]
            r.append(z)
        b = jnp.sqrt(total(weighted(gram, r, r)))
        off.append(b)
        cp = c
        c = [z / b for z in r]
    norms = [[total(weighted(kept, cs[k], cs[m])) for m in range(4)] for k in range(4)]
    mine = [[total(jnp.where(sel, z, 0.0)) for z in cs[k]] for k in range(4)]
    return cs, g, diag, off, norms, mine


def smallest(d, off):
    ab = [jnp.abs(z) for z in off]
    w2 = [z * z for z in off]
    least = lambda v: jnp.minimum(jnp.minimum(v[0], v[1]), jnp.minimum(v[2], v[3]))
    lo = least([d[0] - ab[0], d[1] - ab[0] - ab[1], d[2] - ab[1] - ab[2], d[3] - ab[2]])
    hi = least(d)
    idx = (lax.broadcasted_iota(jnp.int32, (8, 128), 0) * 128 + lax.broadcasted_iota(jnp.int32, (8, 128), 1) + 1).astype(F)
    for _ in range(2):
        h = (hi - lo) * (1.0 / 1024.0)
        x = lo + h * idx
        p1 = d[0] - x
        p2 = (d[1] - x) * p1 - w2[0]
        p3 = (d[2] - x) * p2 - w2[1] * p1
        p4 = (d[3] - x) * p3 - w2[2] * p2
        below = (p1 > 0) & (p2 > 0) & (p3 > 0) & (p4 > 0)
        x = jnp.where(below, x, lo)
        lo = jnp.max(jnp.max(x, axis=0, keepdims=True), axis=1, keepdims=True)
        hi = lo + h
    e = lo
    for _ in range(2):
        vp, vn, sp, sn = jnp.ones_like(e), d[0] - e, jnp.zeros_like(e), -jnp.ones_like(e)
        for p in range(1, 4):
            z = d[p] - e
            v2 = z * vn - w2[p - 1] * vp
            s2 = z * sn - vn - w2[p - 1] * sp
            vp, vn, sp, sn = vn, v2, sn, s2
        e = e - jnp.where(sn != 0, vn / sn, 0.0)
    return e


def ritz(d, off):
    e = smallest(d, off)
    co = [jnp.ones_like(e), (e - d[0]) / off[0]]
    for p in range(1, 3):
        co.append(((e - d[p]) * co[p] - off[p - 1] * co[p - 1]) / off[p])
    n = jnp.sqrt(co[0] * co[0] + co[1] * co[1] + co[2] * co[2] + co[3] * co[3])
    return e, [z / n for z in co]


def whole(
    entries, nsec, nch,
    left_in, right_in, slot_in, tr_in, x_in, b_in, kept_in,
    out_ref, en_ref,
    left, right, slot_ref, tr, x_ref, b_ref, kept_ref, lsem,
    wide, wire, cat, stage, recva, recvb, recvl, trecv, v_ref, st, strecv0, strecv1, vout,
    tpad, tbd, ebd, b2, c2, c1, mixed, moved, early, acat,
    ssem, rsem, tssem, trsem, qssem, qrsem,
):
    me = lax.axis_index("sector")
    ch = lax.axis_index("chain")
    cap = left_in.shape[1]
    recvs = (recva, recvb, recvl)
    parts = ((0, 0, 48, 0, 10), (0, 48, 16, 10, 3), (1, 0, 64, 0, NW))
    my_z, my_y = me // NY, lax.rem(me, NY)
    nz = nsec // NY

    def peer(j):
        return lax.rem(my_z + j // NY, nz) * NY + lax.rem(my_y + j % NY, NY)

    def row_of(o):
        return lax.rem(my_z - o // NY + nz, nz) * NY + lax.rem(my_y - lax.rem(o, NY) + NY, NY)

    far = sorted(range(1, nsec), key=lambda j: -min(j // NY, nz - j // NY) - min(j % NY, NY - j % NY))
    order = sorted(range(1, nsec), key=lambda j: ((0, 2, 1, 3)[j % NY], -min(j // NY, nz - j // NY)))
    lane = lax.broadcasted_iota(jnp.int32, (1, 128), 1)
    tl = lane // 32
    loads = [
        pltpu.make_async_copy(a, b, lsem.at[i])
        for i, (a, b) in enumerate((
            (slot_in, slot_ref), (left_in, left), (tr_in, tr), (right_in, right), (b_in, b_ref), (x_in, x_ref), (kept_in, kept_ref)))
    ]
    for c in loads:
        c.start()
    bar = pltpu.get_barrier_semaphore()
    for j in far:
        pl.semaphore_signal(bar, inc=1, device_id=(ch, peer(j)), device_id_type=MESH)
    for j in range(1, nch):
        pl.semaphore_signal(bar, inc=1, device_id=(lax.rem(ch + j, nch), me), device_id_type=MESH)

    def widen(src, first, n):
        for w in range(first, first + n):
            row8 = src[w].astype(F)
            for c in range(4):
                wide[c, cap * w:cap * w + cap, :] = row8[:, 128 * c:128 * c + 128]
            wide[4, cap * w:cap * w + cap, 0:64] = row8[:, 512:576]

    def pack(side, row, first, n):
        half = (n + 1) // 2
        for s in range(cap):
            for c in range(4):
                wire[s, row + n * c:row + n * c + n, :] = wide[c, pl.ds(s + cap * first, n, stride=cap), :]
            lo = wide[4, pl.ds(s + cap * first, half, stride=cap), :]
            hi = pltpu.roll(wide[4, pl.ds(s + cap * (first + half), n - half, stride=cap), :], 64, 1)
            wire[s, row + 4 * n:row + 4 * n + half, :] = jnp.where(lane < 64, lo, 0.0)
            wire[s, row + 4 * n:row + 5 * n - half, :] = jnp.where(lane < 64, lo[0:n - half], hi)

    def place(part, chosen):
        side, row, n = parts[part][:3]
        cat[side, :, row:row + n] = wire[:, row:row + n, :].astype(H)
        for j in range(nsec):
            stage[side, j, row:row + n] = cat[side, chosen[j], row:row + n]

    def tcopy(j):
        return pltpu.make_async_remote_copy(
            src_ref=tr, dst_ref=trecv.at[ch], send_sem=tssem.at[j], recv_sem=trsem.at[j],
            device_id=(lax.rem(ch + j, nch), me), device_id_type=MESH)

    def ecopy(part, j):
        side, row, n = parts[part][:3]
        src = stage.at[side, j, pl.ds(row, n)]
        return pltpu.make_async_remote_copy(
            src_ref=src, dst_ref=recvs[part].at[j], send_sem=ssem.at[part], recv_sem=rsem.at[part],
            device_id=(ch, peer(j)), device_id_type=MESH)

    def everyone(ref, send_sem, recv_sem):
        rows = ref.at[pl.ds(1, nsec - 1)]
        return pltpu.make_async_remote_copy(
            src_ref=rows, dst_ref=rows, send_sem=send_sem, recv_sem=recv_sem,
            device_id=(ch, lax.rem(me + 1, nsec)), device_id_type=MESH)

    loads[0].wait()
    chosen = []
    for j in range(nsec):
        h = peer(j)
        s = jnp.int32(0)
        for k in range(NT):
            g = slot_ref[0, h * NT + k]
            s = s + jnp.where(g // cap == me, lax.rem(g, cap), 0)
        chosen.append(s)
    loads[1].wait()
    wire[...] = jnp.zeros_like(wire)
    widen(left, 0, NW)
    pack(1, 0, 0, NW)
    place(2, chosen)
    pl.semaphore_wait(bar, nsec + nch - 2)
    for j in order:
        ecopy(2, j).start()
    loads[2].wait()
    trecv[ch] = tr[...]
    for j in range(1, nch):
        tcopy(j).start()
    loads[3].wait()
    widen(right, 0, NW)
    pack(0, 0, 0, 10)
    place(0, chosen)
    for j in order:
        ecopy(0, j).start()
    pack(0, 48, 10, 3)
    place(1, chosen)
    for j in order:
        ecopy(1, j).start()
    for part in range(3):
        side, row, n = parts[part][:3]
        recvs[part][0] = stage[side, 0, row:row + n]
    loads[4].wait()
    loads[5].wait()
    loads[6].wait()

    bf = b_ref[...].astype(F)
    for q in range(NP):
        off = 16 * q
        a = bf[:, (off // 128) * 128:(off // 128) * 128 + 128]
        sh = (-(off % 128)) % 128
        a = pltpu.roll(a, sh, 1) if sh else a
        tbd[pl.ds(q, NW, stride=NP), :] = jnp.where(lane < 16, a, 0.0)
    bb = tbd[0:208, :]
    b2[...] = (bb + pltpu.roll(bb, 16, 1))[:, :32].astype(H)
    for p in range(NP):
        acc = jnp.zeros((NB, 128), F)
        for t in range(NT):
            acc = acc + grab(lambda c: x_ref[t, :, c * 128:(c + 1) * 128], NB * p, t, lane)
        v_ref[0, pl.ds(p, NB, stride=NP), :] = acc
    x = v_ref[0]
    n0 = jnp.sqrt(full(x * x))
    v_ref[0] = x * inverse(n0)
    loop(1, nch, lambda j: tcopy(j).wait())
    tbd[...] = jnp.zeros_like(tbd)
    for t in range(NT):
        tpad[0:8, 0:576] = trecv[:, t, :]
        for i in range(NB):
            tbd[pl.ds(32 * t + i, 8, stride=128), :] = grab(lambda c: tpad[0:8, c * 128:(c + 1) * 128], NB * i, t, lane)
    row = lax.broadcasted_iota(jnp.int32, (128, 128), 0)
    col = lax.broadcasted_iota(jnp.int32, (128, 128), 1)
    eye = (row == col).astype(F)
    T = [jnp.where(ch > c, tbd[c * 128:(c + 1) * 128, :], eye) for c in range(7)]

    def mm(a, b):
        return jnp.dot(a, b, precision=lax.Precision.HIGHEST, preferred_element_type=F)

    pre = mm(mm(T[6], mm(T[5], T[4])), mm(mm(T[3], T[2]), mm(T[1], T[0])))
    ph, plo = split(pre.T)

    ebd[...] = jnp.zeros_like(ebd)
    c1[...] = jnp.zeros_like(c1)

    def spread(part, first, n):
        half = (n + 1) // 2
        m = recvs[part].shape[1]
        for t in range(NT):
            o = slot_ref[0, me * NT + t] // cap
            wire[t, 0:m] = recvs[part][row_of(o)].astype(F)
            tpad[0:half, 0:128] = wire[t, 4 * n:4 * n + half, :]
            tpad[half:n, 0:128] = pltpu.roll(wire[t, 4 * n:5 * n - half, :], 64, 1)
            tile = lambda c: wire[t, n * c:n * c + n, :] if c < 4 else tpad[0:n, 0:128]
            for i in range(NB):
                ebd[pl.ds(128 * first + 32 * t + i, n, stride=128), :] = grab(tile, NB * i, t, lane)

    def pair_step(k, parts=2):
        bm = b2[...]
        for l in range(0, NB, 2):
            xx = jnp.concatenate([v_ref[k, 16 * l:16 * l + 16, :], v_ref[k, 16 * l + 16:16 * l + 32, :]], 1)
            h, lo = split(xx)
            o = jnp.dot(bm, jnp.concatenate([h, lo], 0), preferred_element_type=F)
            h, lo = split(o)
            mixed[0, l] = h[:, :128]
            mixed[0, l + 1] = h[:, 128:]
            if parts == 2:
                mixed[1, l] = lo[:, :128]
                mixed[1, l + 1] = lo[:, 128:]

    def right_step(first=0, last=NW):
        for w in range(first, last):
            h = mixed[0, :, 16 * w:16 * w + 16, :].reshape(384, 128)
            lo = mixed[1, :, 16 * w:16 * w + 16, :].reshape(384, 128)
            o = jnp.dot(jnp.concatenate([h, lo], 1), c2[w], preferred_element_type=F)
            moved[w] = jnp.swapaxes(o.reshape(NB, NP, 128), 0, 1)

    def right_step_rounded():
        for w in range(0, NW, 2):
            n = min(2, NW - w)
            h = jnp.concatenate([mixed[0, :, 16 * (w + i):16 * (w + i) + 16, :].reshape(384, 128) for i in range(n)], 1)
            o = jnp.dot(h, c1[w // 2, 0:128 * n, 0:128 * n], preferred_element_type=F)
            for i in range(n):
                moved[w + i] = jnp.swapaxes(o[:, 128 * i:128 * i + 128].reshape(NB, NP, 128), 0, 1)

    def columns(q, first, last):
        return jnp.concatenate([jnp.concatenate([moved[w, q + j] for w in range(first, last)], 0) for j in range(2)], 1)

    def emit(k, q, o):
        for j in range(2):
            oj = o[:, 128 * j:128 * j + 128]
            y = jnp.where(tl == 0, oj[0:24], jnp.where(tl == 1, oj[24:48], jnp.where(tl == 2, oj[48:72], oj[72:96])))
            v_ref[k + 1, pl.ds(q + j, NB, stride=NP), :] = y

    def twice(a):
        return jnp.concatenate([a, a], 1).astype(H)

    def left_dot(a, r, both):
        if both:
            h = r.astype(H).astype(F)
            r = jnp.concatenate([h, r - h], 0)
        return jnp.dot(a, r.astype(H), preferred_element_type=F)

    def left_step(k, a2, both):
        a = a2 if both else a2[:, :24 * NW]
        for q in range(0, NP, 2):
            emit(k, q, left_dot(a, columns(q, 0, NW), both))

    pair_step(0)
    everyone(recvs[2], ssem.at[2], rsem.at[2]).wait()
    spread(2, 0, NW)
    pp = jnp.concatenate([ph, plo], 0)
    pq = jnp.concatenate([ph, plo, ph], 0)
    for w in range(NW):
        e = ebd[w * 128:(w + 1) * 128, :].astype(H)
        s = jnp.dot(jnp.concatenate([e, e], 1), pp, preferred_element_type=F)
        sh, sl = split(s.T)
        at = jnp.dot(jnp.concatenate([sh, sh, sl], 1), pq, preferred_element_type=F)
        acat[24 * w:24 * w + 24, :] = at[0:24] + at[32:56] + at[64:88] + at[96:120]
    acat[312:384, :] = jnp.zeros((72, 128), F)
    al = acat[...].T
    al = jnp.concatenate([al[32 * t:32 * t + 24] for t in range(NT)], 0)[:, :312].astype(H).astype(F)
    a2 = twice(al)
    for part, first, last in ((0, 0, 10), (1, 10, NW)):
        everyone(recvs[part], ssem.at[part], rsem.at[part]).wait()
        spread(part, first, last - first)
        for w in range(first, last):
            ct = ebd[w * 128:(w + 1) * 128, :].T.astype(H)
            c2[w, 0:128, :] = ct
            c2[w, 128:256, :] = ct
            i = 128 * (w % 2)
            c1[w // 2, i:i + 128, i:i + 128] = ct
        right_step(first, last)
        a = twice(al[:, 24 * first:24 * last])
        for q in range(0, NP, 2):
            o = left_dot(a, columns(q, first, last), True)
            if part == 0:
                early[q // 2] = o
            else:
                emit(0, q, early[q // 2] + o)

    alphas = []
    betas = []
    for k in range(3):
        if k > 0:
            pair_step(k, 1)
            right_step_rounded()
            left_step(k, a2, k == 1)
        y = v_ref[k + 1]
        a = full(v_ref[k] * y)
        r = y - a * v_ref[k]
        if k > 0:
            r = r - betas[-1] * v_ref[k - 1]
        rr = full(r * r)
        b = jnp.sqrt(rr)
        alphas.append(a)
        betas.append(b)
        v_ref[k + 1] = r * jnp.where(rr > 0, lax.rsqrt(rr), 0.0)

    def qcopy(i, j):
        return pltpu.make_async_remote_copy(
            src_ref=st.at[i], dst_ref=(strecv0, strecv1)[i].at[j], send_sem=qssem.at[i], recv_sem=qrsem.at[i],
            device_id=(ch, peer(j)), device_id_type=MESH)

    def lanes(rows):
        g = jnp.concatenate(rows + [jnp.zeros((128 - len(rows), 128), F)], 0)
        return lax.dot_general(lhs, g, (((1,), (1,)), ((), ())), precision=lax.Precision.HIGHEST, preferred_element_type=F)

    def gathered(ref):
        return jnp.concatenate([ref[:, 0, :], jnp.zeros((128 - nsec, 128), F)], 0).T

    kp = jnp.where(tl == 0, kept_ref[0, 0], jnp.where(tl == 1, kept_ref[0, 1], jnp.where(tl == 2, kept_ref[0, 2], kept_ref[0, 3])))
    keep = lax.rem(lane, 32) < kp
    r8 = lax.broadcasted_iota(jnp.int32, (8, 128), 0)
    lhs = jnp.where(r8 == 0, 1.0, jnp.where((r8 == 1) & keep, 1.0, 0.0))
    s = lanes([jnp.sum(v_ref[i] * v_ref[j], axis=0, keepdims=True) for i in range(4) for j in range(i, 4)])
    s = s[0:1] + pltpu.roll(s[1:2], 64, 1)
    for i, val in enumerate([n0] + alphas + betas):
        s = s + jnp.where(lane == 16 + i, val, 0.0)
    st[0] = s
    for j in far:
        qcopy(0, j).start()
    strecv0[0] = s
    pair_step(3, 1)
    right_step_rounded()
    left_step(3, a2, False)
    s = jnp.zeros((1, 128), F)
    for i in range(4):
        s = s + jnp.where(lane == i, full(v_ref[i] * v_ref[4]), 0.0)
    st[1] = s
    for j in far:
        qcopy(1, j).start()
    strecv1[0] = s
    for k in range(1, 4):
        for p in range(NP):
            a = v_ref[k, pl.ds(p, NB, stride=NP), :]
            for t in range(NT):
                vout[k - 1, t, :, NB * p:NB * p + NB] = a[:, 32 * t:32 * t + NB]
    everyone(strecv0, qssem.at[0], qrsem.at[0]).wait()
    q0 = gathered(strecv0)
    cs, g, diag, off, norms, mine = recursion(lambda i: q0[i:i + 1, :], lane == 0)
    everyone(strecv1, qssem.at[1], qrsem.at[1]).wait()
    q1 = gathered(strecv1)
    z = cs[3][0] * q1[0:1, :]
    for i in range(1, 4):
        z = z + cs[3][i] * q1[i:i + 1, :]
    diag.append(total(g + z * cs[3][3]))
    e, co = ritz(diag, off)
    en_ref[...] = e
    n2 = None
    for k in range(4):
        for m in range(4):
            z = co[k] * co[m] * norms[k][m]
            n2 = z if n2 is None else n2 + z
    scale = jnp.sqrt(entries / n2)
    f = []
    for i in range(4):
        z = None
        for k in range(i, 4):
            c = co[k] * mine[k][i]
            z = c if z is None else z + c
        f.append(z * scale)
    f[0] = f[0] * inverse(n0)
    column = lax.rem(lax.broadcasted_iota(jnp.int32, (1, NP * NB), 1), NB)
    for t in range(NT):
        y = f[0] * x_ref[t]
        for k in range(1, 4):
            y = y + f[k] * vout[k - 1, t]
        out_ref[t] = jnp.where(column < kept_ref[0, t], y, 0.0)


def body(wavefunction, transfer, left_env, right_env, pair_ops, env_slot, kept_ranks):
    nsec = lax.axis_size("sector")
    nch = lax.axis_size("chain")
    cap = left_env.shape[1]
    entries = float(nsec * NT * NB * NP * NB)
    vmem = pl.BlockSpec(memory_space=pltpu.VMEM)
    hbm = pl.BlockSpec(memory_space=pltpu.HBM)
    dma = pltpu.SemaphoreType.DMA
    out, en = pl.pallas_call(
        functools.partial(whole, entries, nsec, nch),
        out_shape=(jax.ShapeDtypeStruct((NT, NB, NP * NB), F), jax.ShapeDtypeStruct((1, 1), F)),
        in_specs=[hbm] * 7,
        out_specs=(vmem, vmem),
        scratch_shapes=[
            pltpu.VMEM((NW, cap, 576), H),
            pltpu.VMEM((NW, cap, 576), H),
            pltpu.SMEM(env_slot.shape, jnp.int32),
            pltpu.VMEM(transfer.shape[1:], F),
            pltpu.VMEM(wavefunction.shape[1:], F),
            pltpu.VMEM(pair_ops.shape[1:], H),
            pltpu.SMEM(kept_ranks.shape, jnp.int32),
            dma((7,)),
            pltpu.VMEM((5, cap * NW, 128), F),
            pltpu.VMEM((cap, 64, 128), F),
            pltpu.VMEM((2, cap, 64, 128), H),
            pltpu.VMEM((2, nsec, 64, 128), H),
            pltpu.VMEM((nsec, 48, 128), H),
            pltpu.VMEM((nsec, 16, 128), H),
            pltpu.VMEM((nsec, 64, 128), H),
            pltpu.VMEM((nch, NT, 576), F),
            pltpu.VMEM((5, 384, 128), F),
            pltpu.VMEM((2, 1, 128), F),
            pltpu.VMEM((nsec, 1, 128), F),
            pltpu.VMEM((nsec, 1, 128), F),
            pltpu.VMEM((3, NT, NB, NP * NB), F),
            pltpu.VMEM((16, 640), F),
            pltpu.VMEM((1024, 128), F),
            pltpu.VMEM((1664, 128), F),
            pltpu.VMEM((208, 32), H),
            pltpu.VMEM((NW, 256, 128), H),
            pltpu.VMEM(((NW + 1) // 2, 256, 256), H),
            pltpu.VMEM((2, NB, 208, 128), H),
            pltpu.VMEM((NW, NP, NB, 128), F),
            pltpu.VMEM((NP // 2, NT * NB, 256), F),
            pltpu.VMEM((384, 128), F),
            dma((3,)), dma((3,)), dma((nch,)), dma((nch,)), dma((2,)), dma((2,)),
        ],
        compiler_params=pltpu.CompilerParams(collective_id=0, has_side_effects=True, vmem_limit_bytes=48 * 2**20),
        name="lanczos",
    )(*(
        pltpu.with_memory_space_constraint(a, pltpu.HBM)
        for a in (
            jnp.swapaxes(left_env[0], 0, 1), jnp.swapaxes(right_env[0], 0, 1), env_slot, transfer[0], wavefunction[0],
            pair_ops[0], kept_ranks)
    ))
    return out[None], en.reshape(1)


def solution(mesh):
    return jax.shard_map(
        body,
        mesh=mesh,
        in_specs=(
            P("chain", "sector", None, None),
            P("chain", "sector", None),
            P("chain", "sector", None, None),
            P("chain", "sector", None, None),
            P("chain", None, None),
            P("chain", None),
            P("chain", "sector"),
        ),
        out_specs=(P("chain", "sector", None, None), P("chain")),
        check_vma=False,
    )
```

```python
import functools

import jax
import jax.numpy as jnp
from jax import lax
from jax.experimental import pallas as pl
from jax.experimental.pallas import tpu as pltpu
from jax.sharding import PartitionSpec as P

F = jnp.float32
H = jnp.bfloat16
NT = 4
NB = 24
NP = 16
NW = 13
NY = 4
MESH = pl.DeviceIdType.MESH


def split(x):
    h = x.astype(H)
    return h, (x - h.astype(F)).astype(H)


def grab(tile, off, t, lane):
    c0, o = off // 128, off % 128
    sh = (32 * t - o) % 128
    a = tile(c0)
    a = pltpu.roll(a, sh, 1) if sh else a
    if o + NB > 128:
        b = tile(c0 + 1)
        b = pltpu.roll(b, sh, 1) if sh else b
        a = jnp.where(lane < 32 * t + 128 - o, a, b)
    return jnp.where((lane >= 32 * t) & (lane < 32 * t + NB), a, 0.0)


def full(x):
    return jnp.sum(jnp.sum(x, axis=0, keepdims=True), axis=1, keepdims=True)


def inverse(n):
    return jnp.where(n > 0, 1.0 / n, 0.0)


def loop(a, b, f):
    def step(j, c):
        f(j)
        return c

    lax.fori_loop(a, b, step, 0)


def total(x):
    return jnp.sum(x, axis=1, keepdims=True)


def weighted(m, a, b):
    acc = None
    for i in range(len(a)):
        s = None
        for j in range(len(b)):
            z = m[i][j] * b[j]
            s = z if s is None else s + z
        s = s * a[i]
        acc = s if acc is None else acc + s
    return acc


def recursion(q, sel):
    pos = {}
    for i in range(4):
        for j in range(i, 4):
            pos[i, j] = pos[j, i] = len(set(pos.values()))
    gram = [[q(pos[i, j]) for j in range(4)] for i in range(4)]
    kept = [[q(64 + pos[i, j]) for j in range(4)] for i in range(4)]
    n0 = q(16)
    al = [q(17 + i) for i in range(3)]
    be = [q(20 + i) for i in range(3)]

    def image(c):
        k = len(c) - 1
        y = [None] * min(k + 2, 4)

        def add(i, z):
            y[i] = z if y[i] is None else y[i] + z

        for j in range(min(k + 1, 3)):
            add(j, al[j] * c[j])
            add(j + 1, be[j] * c[j])
            if j > 0:
                add(j - 1, be[j - 1] * c[j])
        return y

    c = [n0 / jnp.sqrt(total(n0 * n0))]
    cp = []
    b = None
    cs = []
    diag = []
    off = []
    for k in range(4):
        cs.append(c)
        y = image(c)
        g = weighted(gram, c, y)
        if k == 3:
            break
        a = total(g)
        diag.append(a)
        r = []
        for i in range(len(y)):
            z = y[i]
            if i < len(c):
                z = z - a * c[i]
            if i < len(cp):
                z = z - b * cp[i]
            r.append(z)
        b = jnp.sqrt(total(weighted(gram, r, r)))
        off.append(b)
        cp = c
        c = [z / b for z in r]
    norms = [[total(weighted(kept, cs[k], cs[m])) for m in range(4)] for k in range(4)]
    mine = [[total(jnp.where(sel, z, 0.0)) for z in cs[k]] for k in range(4)]
    return cs, g, diag, off, norms, mine


def smallest(d, off):
    ab = [jnp.abs(z) for z in off]
    w2 = [z * z for z in off]
    least = lambda v: jnp.minimum(jnp.minimum(v[0], v[1]), jnp.minimum(v[2], v[3]))
    lo = least([d[0] - ab[0], d[1] - ab[0] - ab[1], d[2] - ab[1] - ab[2], d[3] - ab[2]])
    hi = least(d)
    idx = (lax.broadcasted_iota(jnp.int32, (8, 128), 0) * 128 + lax.broadcasted_iota(jnp.int32, (8, 128), 1) + 1).astype(F)
    for _ in range(2):
        h = (hi - lo) * (1.0 / 1024.0)
        x = lo + h * idx
        p1 = d[0] - x
        p2 = (d[1] - x) * p1 - w2[0]
        p3 = (d[2] - x) * p2 - w2[1] * p1
        p4 = (d[3] - x) * p3 - w2[2] * p2
        below = (p1 > 0) & (p2 > 0) & (p3 > 0) & (p4 > 0)
        x = jnp.where(below, x, lo)
        lo = jnp.max(jnp.max(x, axis=0, keepdims=True), axis=1, keepdims=True)
        hi = lo + h
    e = lo
    for _ in range(2):
        vp, vn, sp, sn = jnp.ones_like(e), d[0] - e, jnp.zeros_like(e), -jnp.ones_like(e)
        for p in range(1, 4):
            z = d[p] - e
            v2 = z * vn - w2[p - 1] * vp
            s2 = z * sn - vn - w2[p - 1] * sp
            vp, vn, sp, sn = vn, v2, sn, s2
        e = e - jnp.where(sn != 0, vn / sn, 0.0)
    return e


def ritz(d, off):
    e = smallest(d, off)
    co = [jnp.ones_like(e), (e - d[0]) / off[0]]
    for p in range(1, 3):
        co.append(((e - d[p]) * co[p] - off[p - 1] * co[p - 1]) / off[p])
    n = jnp.sqrt(co[0] * co[0] + co[1] * co[1] + co[2] * co[2] + co[3] * co[3])
    return e, [z / n for z in co]


def whole(
    entries, nsec, nch,
    left_in, right_in, slot_in, tr_in, x_in, b_in, kept_in,
    out_ref, en_ref,
    left, right, slot_ref, tr, x_ref, b_ref, kept_ref, lsem,
    wide, wire, cat, stage, recva, recvb, recvl, trecv, v_ref, st, strecv0, strecv1, vout,
    tpad, tbd, ebd, b2, c2, c1, mixed, moved, early, acat,
    ssem, rsem, tssem, trsem, qssem, qrsem,
):
    me = lax.axis_index("sector")
    ch = lax.axis_index("chain")
    cap = left_in.shape[1]
    recvs = (recva, recvb, recvl)
    parts = ((0, 0, 48, 0, 10), (0, 48, 16, 10, 3), (1, 0, 64, 0, NW))
    my_z, my_y = me // NY, lax.rem(me, NY)
    nz = nsec // NY

    def peer(j):
        return lax.rem(my_z + j // NY, nz) * NY + lax.rem(my_y + j % NY, NY)

    def row_of(o):
        return lax.rem(my_z - o // NY + nz, nz) * NY + lax.rem(my_y - lax.rem(o, NY) + NY, NY)

    far = sorted(range(1, nsec), key=lambda j: -min(j // NY, nz - j // NY) - min(j % NY, NY - j % NY))
    order = sorted(range(1, nsec), key=lambda j: ((0, 2, 1, 3)[j % NY], -min(j // NY, nz - j // NY)))
    lane = lax.broadcasted_iota(jnp.int32, (1, 128), 1)
    tl = lane // 32
    loads = [
        pltpu.make_async_copy(a, b, lsem.at[i])
        for i, (a, b) in enumerate((
            (slot_in, slot_ref), (left_in, left), (tr_in, tr), (right_in, right), (b_in, b_ref), (x_in, x_ref), (kept_in, kept_ref)))
    ]
    for c in loads:
        c.start()
    bar = pltpu.get_barrier_semaphore()
    for j in far:
        pl.semaphore_signal(bar, inc=1, device_id=(ch, peer(j)), device_id_type=MESH)
    for j in range(1, nch):
        pl.semaphore_signal(bar, inc=1, device_id=(lax.rem(ch + j, nch), me), device_id_type=MESH)

    def widen(src, first, n):
        for w in range(first, first + n):
            row8 = src[w].astype(F)
            for c in range(4):
                wide[c, cap * w:cap * w + cap, :] = row8[:, 128 * c:128 * c + 128]
            wide[4, cap * w:cap * w + cap, 0:64] = row8[:, 512:576]

    def pack(side, row, first, n):
        half = (n + 1) // 2
        for s in range(cap):
            for c in range(4):
                wire[s, row + n * c:row + n * c + n, :] = wide[c, pl.ds(s + cap * first, n, stride=cap), :]
            lo = wide[4, pl.ds(s + cap * first, half, stride=cap), :]
            hi = pltpu.roll(wide[4, pl.ds(s + cap * (first + half), n - half, stride=cap), :], 64, 1)
            wire[s, row + 4 * n:row + 4 * n + half, :] = jnp.where(lane < 64, lo, 0.0)
            wire[s, row + 4 * n:row + 5 * n - half, :] = jnp.where(lane < 64, lo[0:n - half], hi)

    def place(part, chosen):
        side, row, n = parts[part][:3]
        cat[side, :, row:row + n] = wire[0:cap, row:row + n, :].astype(H)
        for j in range(nsec):
            stage[side, j, row:row + n] = cat[side, chosen[j], row:row + n]

    def tcopy(j):
        return pltpu.make_async_remote_copy(
            src_ref=tr, dst_ref=trecv.at[ch], send_sem=tssem.at[j], recv_sem=trsem.at[j],
            device_id=(lax.rem(ch + j, nch), me), device_id_type=MESH)

    def ecopy(part, j):
        side, row, n = parts[part][:3]
        src = stage.at[side, j, pl.ds(row, n)]
        return pltpu.make_async_remote_copy(
            src_ref=src, dst_ref=recvs[part].at[j], send_sem=ssem.at[part], recv_sem=rsem.at[part],
            device_id=(ch, peer(j)), device_id_type=MESH)

    def everyone(ref, send_sem, recv_sem):
        rows = ref.at[pl.ds(1, nsec - 1)]
        return pltpu.make_async_remote_copy(
            src_ref=rows, dst_ref=rows, send_sem=send_sem, recv_sem=recv_sem,
            device_id=(ch, lax.rem(me + 1, nsec)), device_id_type=MESH)

    loads[0].wait()
    chosen = []
    for j in range(nsec):
        h = peer(j)
        s = jnp.int32(0)
        for k in range(NT):
            g = slot_ref[0, h * NT + k]
            s = s + jnp.where(g // cap == me, lax.rem(g, cap), 0)
        chosen.append(s)
    loads[1].wait()
    wire[...] = jnp.zeros_like(wire)
    widen(left, 0, NW)
    pack(1, 0, 0, NW)
    place(2, chosen)
    pl.semaphore_wait(bar, nsec + nch - 2)
    for j in order:
        ecopy(2, j).start()
    loads[2].wait()
    trecv[ch] = tr[...]
    for j in range(1, nch):
        tcopy(j).start()
    loads[3].wait()
    widen(right, 0, NW)
    pack(0, 0, 0, 10)
    place(0, chosen)
    for j in order:
        ecopy(0, j).start()
    pack(0, 48, 10, 3)
    place(1, chosen)
    for j in order:
        ecopy(1, j).start()
    for part in range(3):
        side, row, n = parts[part][:3]
        recvs[part][0] = stage[side, 0, row:row + n]
    loads[4].wait()
    loads[5].wait()
    loads[6].wait()

    bf = b_ref[...].astype(F)
    for q in range(NP):
        off = 16 * q
        a = bf[:, (off // 128) * 128:(off // 128) * 128 + 128]
        sh = (-(off % 128)) % 128
        a = pltpu.roll(a, sh, 1) if sh else a
        tbd[pl.ds(q, NW, stride=NP), :] = jnp.where(lane < 16, a, 0.0)
    bb = tbd[0:208, :]
    b2[...] = (bb + pltpu.roll(bb, 16, 1))[:, :32].astype(H)
    for p in range(NP):
        acc = jnp.zeros((NB, 128), F)
        for t in range(NT):
            acc = acc + grab(lambda c: x_ref[t, :, c * 128:(c + 1) * 128], NB * p, t, lane)
        v_ref[0, pl.ds(p, NB, stride=NP), :] = acc
    x = v_ref[0]
    n0 = jnp.sqrt(full(x * x))
    v_ref[0] = x * inverse(n0)
    loop(1, nch, lambda j: tcopy(j).wait())
    tbd[...] = jnp.zeros_like(tbd)
    for t in range(NT):
        tpad[0:8, 0:576] = trecv[:, t, :]
        for i in range(NB):
            tbd[pl.ds(32 * t + i, 8, stride=128), :] = grab(lambda c: tpad[0:8, c * 128:(c + 1) * 128], NB * i, t, lane)
    row = lax.broadcasted_iota(jnp.int32, (128, 128), 0)
    col = lax.broadcasted_iota(jnp.int32, (128, 128), 1)
    eye = (row == col).astype(F)
    T = [jnp.where(ch > c, tbd[c * 128:(c + 1) * 128, :], eye) for c in range(7)]

    def mm(a, b):
        return jnp.dot(a, b, precision=lax.Precision.HIGHEST, preferred_element_type=F)

    pre = mm(mm(T[6], mm(T[5], T[4])), mm(mm(T[3], T[2]), mm(T[1], T[0])))
    ph, plo = split(pre.T)

    ebd[...] = jnp.zeros_like(ebd)
    c1[...] = jnp.zeros_like(c1)

    def spread(part, first, n):
        half = (n + 1) // 2
        m = recvs[part].shape[1]
        for t in range(NT):
            o = slot_ref[0, me * NT + t] // cap
            wire[t, 0:m] = recvs[part][row_of(o)].astype(F)
            tpad[0:half, 0:128] = wire[t, 4 * n:4 * n + half, :]
            tpad[half:n, 0:128] = pltpu.roll(wire[t, 4 * n:5 * n - half, :], 64, 1)
            tile = lambda c: wire[t, n * c:n * c + n, :] if c < 4 else tpad[0:n, 0:128]
            for i in range(NB):
                ebd[pl.ds(128 * first + 32 * t + i, n, stride=128), :] = grab(tile, NB * i, t, lane)

    def pair_step(k, parts=2):
        bm = b2[...]
        for l in range(0, NB, 2):
            xx = jnp.concatenate([v_ref[k, 16 * l:16 * l + 16, :], v_ref[k, 16 * l + 16:16 * l + 32, :]], 1)
            h, lo = split(xx)
            o = jnp.dot(bm, jnp.concatenate([h, lo], 0), preferred_element_type=F)
            h, lo = split(o)
            mixed[0, l] = h[:, :128]
            mixed[0, l + 1] = h[:, 128:]
            if parts == 2:
                mixed[1, l] = lo[:, :128]
                mixed[1, l + 1] = lo[:, 128:]

    def right_step(first=0, last=NW):
        for w in range(first, last):
            h = mixed[0, :, 16 * w:16 * w + 16, :].reshape(384, 128)
            lo = mixed[1, :, 16 * w:16 * w + 16, :].reshape(384, 128)
            o = jnp.dot(jnp.concatenate([h, lo], 1), c2[w], preferred_element_type=F)
            moved[w] = jnp.swapaxes(o.reshape(NB, NP, 128), 0, 1)

    def right_step_rounded():
        for w in range(0, NW, 2):
            n = min(2, NW - w)
            h = jnp.concatenate([mixed[0, :, 16 * (w + i):16 * (w + i) + 16, :].reshape(384, 128) for i in range(n)], 1)
            o = jnp.dot(h, c1[w // 2, 0:128 * n, 0:128 * n], preferred_element_type=F)
            for i in range(n):
                moved[w + i] = jnp.swapaxes(o[:, 128 * i:128 * i + 128].reshape(NB, NP, 128), 0, 1)

    def columns(q, first, last):
        return jnp.concatenate([jnp.concatenate([moved[w, q + j] for w in range(first, last)], 0) for j in range(2)], 1)

    def emit(k, q, o):
        for j in range(2):
            oj = o[:, 128 * j:128 * j + 128]
            y = jnp.where(tl == 0, oj[0:24], jnp.where(tl == 1, oj[24:48], jnp.where(tl == 2, oj[48:72], oj[72:96])))
            v_ref[k + 1, pl.ds(q + j, NB, stride=NP), :] = y

    def twice(a):
        return jnp.concatenate([a, a], 1).astype(H)

    def left_dot(a, r, both):
        if both:
            h = r.astype(H).astype(F)
            r = jnp.concatenate([h, r - h], 0)
        return jnp.dot(a, r.astype(H), preferred_element_type=F)

    def left_step(k, a2, both):
        a = a2 if both else a2[:, :24 * NW]
        for q in range(0, NP, 2):
            emit(k, q, left_dot(a, columns(q, 0, NW), both))

    pair_step(0)
    everyone(recvs[2], ssem.at[2], rsem.at[2]).wait()
    spread(2, 0, NW)
    pp = jnp.concatenate([ph, plo], 0)
    pq = jnp.concatenate([ph, plo, ph], 0)
    for w in range(NW):
        e = ebd[w * 128:(w + 1) * 128, :].astype(H)
        s = jnp.dot(jnp.concatenate([e, e], 1), pp, preferred_element_type=F)
        sh, sl = split(s.T)
        at = jnp.dot(jnp.concatenate([sh, sh, sl], 1), pq, preferred_element_type=F)
        acat[24 * w:24 * w + 24, :] = at[0:24] + at[32:56] + at[64:88] + at[96:120]
    acat[312:384, :] = jnp.zeros((72, 128), F)
    al = acat[...].T
    al = jnp.concatenate([al[32 * t:32 * t + 24] for t in range(NT)], 0)[:, :312].astype(H).astype(F)
    a2 = twice(al)
    for part, first, last in ((0, 0, 10), (1, 10, NW)):
        everyone(recvs[part], ssem.at[part], rsem.at[part]).wait()
        spread(part, first, last - first)
        for w in range(first, last):
            ct = ebd[w * 128:(w + 1) * 128, :].T.astype(H)
            c2[w, 0:128, :] = ct
            c2[w, 128:256, :] = ct
            i = 128 * (w % 2)
            c1[w // 2, i:i + 128, i:i + 128] = ct
        right_step(first, last)
        a = twice(al[:, 24 * first:24 * last])
        for q in range(0, NP, 2):
            o = left_dot(a, columns(q, first, last), True)
            if part == 0:
                early[q // 2] = o
            else:
                emit(0, q, early[q // 2] + o)

    alphas = []
    betas = []
    for k in range(3):
        if k > 0:
            pair_step(k, 1)
            right_step_rounded()
            left_step(k, a2, k == 1)
        y = v_ref[k + 1]
        a = full(v_ref[k] * y)
        r = y - a * v_ref[k]
        if k > 0:
            r = r - betas[-1] * v_ref[k - 1]
        rr = full(r * r)
        b = jnp.sqrt(rr)
        alphas.append(a)
        betas.append(b)
        v_ref[k + 1] = r * jnp.where(rr > 0, lax.rsqrt(rr), 0.0)

    def qcopy(i, j):
        return pltpu.make_async_remote_copy(
            src_ref=st.at[i], dst_ref=(strecv0, strecv1)[i].at[j], send_sem=qssem.at[i], recv_sem=qrsem.at[i],
            device_id=(ch, peer(j)), device_id_type=MESH)

    def lanes(rows):
        g = jnp.concatenate(rows + [jnp.zeros((128 - len(rows), 128), F)], 0)
        return lax.dot_general(lhs, g, (((1,), (1,)), ((), ())), precision=lax.Precision.HIGHEST, preferred_element_type=F)

    def gathered(ref):
        return jnp.concatenate([ref[:, 0, :], jnp.zeros((128 - nsec, 128), F)], 0).T

    kp = jnp.where(tl == 0, kept_ref[0, 0], jnp.where(tl == 1, kept_ref[0, 1], jnp.where(tl == 2, kept_ref[0, 2], kept_ref[0, 3])))
    keep = lax.rem(lane, 32) < kp
    r8 = lax.broadcasted_iota(jnp.int32, (8, 128), 0)
    lhs = jnp.where(r8 == 0, 1.0, jnp.where((r8 == 1) & keep, 1.0, 0.0))
    s = lanes([jnp.sum(v_ref[i] * v_ref[j], axis=0, keepdims=True) for i in range(4) for j in range(i, 4)])
    s = s[0:1] + pltpu.roll(s[1:2], 64, 1)
    for i, val in enumerate([n0] + alphas + betas):
        s = s + jnp.where(lane == 16 + i, val, 0.0)
    st[0] = s
    for j in far:
        qcopy(0, j).start()
    strecv0[0] = s
    pair_step(3, 1)
    right_step_rounded()
    left_step(3, a2, False)
    s = jnp.zeros((1, 128), F)
    for i in range(4):
        s = s + jnp.where(lane == i, full(v_ref[i] * v_ref[4]), 0.0)
    st[1] = s
    for j in far:
        qcopy(1, j).start()
    strecv1[0] = s
    for k in range(1, 4):
        for p in range(NP):
            a = v_ref[k, pl.ds(p, NB, stride=NP), :]
            for t in range(NT):
                vout[k - 1, t, :, NB * p:NB * p + NB] = a[:, 32 * t:32 * t + NB]
    everyone(strecv0, qssem.at[0], qrsem.at[0]).wait()
    q0 = gathered(strecv0)
    cs, g, diag, off, norms, mine = recursion(lambda i: q0[i:i + 1, :], lane == 0)
    everyone(strecv1, qssem.at[1], qrsem.at[1]).wait()
    q1 = gathered(strecv1)
    z = cs[3][0] * q1[0:1, :]
    for i in range(1, 4):
        z = z + cs[3][i] * q1[i:i + 1, :]
    diag.append(total(g + z * cs[3][3]))
    e, co = ritz(diag, off)
    en_ref[...] = e
    n2 = None
    for k in range(4):
        for m in range(4):
            z = co[k] * co[m] * norms[k][m]
            n2 = z if n2 is None else n2 + z
    scale = jnp.sqrt(entries / n2)
    f = []
    for i in range(4):
        z = None
        for k in range(i, 4):
            c = co[k] * mine[k][i]
            z = c if z is None else z + c
        f.append(z * scale)
    f[0] = f[0] * inverse(n0)
    column = lax.rem(lax.broadcasted_iota(jnp.int32, (1, NP * NB), 1), NB)
    for t in range(NT):
        y = f[0] * x_ref[t]
        for k in range(1, 4):
            y = y + f[k] * vout[k - 1, t]
        out_ref[t] = jnp.where(column < kept_ref[0, t], y, 0.0)


def body(wavefunction, transfer, left_env, right_env, pair_ops, env_slot, kept_ranks):
    nsec = lax.axis_size("sector")
    nch = lax.axis_size("chain")
    cap = left_env.shape[1]
    entries = float(nsec * NT * NB * NP * NB)
    vmem = pl.BlockSpec(memory_space=pltpu.VMEM)
    hbm = pl.BlockSpec(memory_space=pltpu.HBM)
    dma = pltpu.SemaphoreType.DMA
    out, en = pl.pallas_call(
        functools.partial(whole, entries, nsec, nch),
        out_shape=(jax.ShapeDtypeStruct((NT, NB, NP * NB), F), jax.ShapeDtypeStruct((1, 1), F)),
        in_specs=[hbm] * 7,
        out_specs=(vmem, vmem),
        scratch_shapes=[
            pltpu.VMEM((NW, cap, 576), H),
            pltpu.VMEM((NW, cap, 576), H),
            pltpu.SMEM(env_slot.shape, jnp.int32),
            pltpu.VMEM(transfer.shape[1:], F),
            pltpu.VMEM(wavefunction.shape[1:], F),
            pltpu.VMEM(pair_ops.shape[1:], H),
            pltpu.SMEM(kept_ranks.shape, jnp.int32),
            dma((7,)),
            pltpu.VMEM((5, cap * 20, 128), F),
            pltpu.VMEM((cap + 1, 64, 128), F),
            pltpu.VMEM((2, cap, 64, 128), H),
            pltpu.VMEM((2, nsec, 64, 128), H),
            pltpu.VMEM((nsec, 48, 128), H),
            pltpu.VMEM((nsec, 16, 128), H),
            pltpu.VMEM((nsec, 64, 128), H),
            pltpu.VMEM((nch, NT, 576), F),
            pltpu.VMEM((5, 384, 128), F),
            pltpu.VMEM((2, 1, 128), F),
            pltpu.VMEM((nsec, 1, 128), F),
            pltpu.VMEM((nsec, 1, 128), F),
            pltpu.VMEM((3, NT, NB, NP * NB), F),
            pltpu.VMEM((16, 640), F),
            pltpu.VMEM((1024, 128), F),
            pltpu.VMEM((2304, 128), F),
            pltpu.VMEM((208, 32), H),
            pltpu.VMEM((NW, 256, 128), H),
            pltpu.VMEM(((NW + 1) // 2, 256, 256), H),
            pltpu.VMEM((2, NB, 208, 128), H),
            pltpu.VMEM((NW, NP, NB, 128), F),
            pltpu.VMEM((NP // 2, NT * NB, 256), F),
            pltpu.VMEM((384, 128), F),
            dma((3,)), dma((3,)), dma((nch,)), dma((nch,)), dma((2,)), dma((2,)),
        ],
        compiler_params=pltpu.CompilerParams(collective_id=0, has_side_effects=True, vmem_limit_bytes=48 * 2**20),
        name="lanczos",
    )(*(
        pltpu.with_memory_space_constraint(a, pltpu.HBM)
        for a in (
            jnp.swapaxes(left_env[0], 0, 1), jnp.swapaxes(right_env[0], 0, 1), env_slot, transfer[0], wavefunction[0],
            pair_ops[0], kept_ranks)
    ))
    return out[None], en.reshape(1)


def solution(mesh):
    return jax.shard_map(
        body,
        mesh=mesh,
        in_specs=(
            P("chain", "sector", None, None),
            P("chain", "sector", None),
            P("chain", "sector", None, None),
            P("chain", "sector", None, None),
            P("chain", None, None),
            P("chain", None),
            P("chain", "sector"),
        ),
        out_specs=(P("chain", "sector", None, None), P("chain")),
        check_vma=False,
    )
```
